32 devices in a mesh: groups: 2 (over y), dp: 8 (over z, x), tensor: 2 (over core).
Axes of the slice: x: 2, y: 2, z: 4, core: 2. Of those that a mesh axis runs over, the one named last changes fastest.
Arguments:
- inputs: bfloat16 [2048, 14336], P(('groups', 'dp'), 'tensor'), parts along dimension 0, may hold values from -6 to 6
- out_grads: bfloat16 [2048, 4096], P(('groups', 'dp'), 'tensor'), parts along dimension 0, may hold values from -6 to 6
- proj_in: bfloat16 [14336, 64], replicated, may hold values from -0.046875 to 0.046875
- proj_out: bfloat16 [4096, 64], replicated, may hold values from -0.09375 to 0.09375
- doc_ids: int32 [16, 128], P(('groups', 'dp')), parts along dimension 0, may hold values from 0 to 7, never falling along the last dimension, each value on 1 to 64 neighbouring positions
- queries: float32 [16, 4096], replicated, may hold values from -6 to 6
Outputs:
- gram: float32 [128, 64], P(('groups', 'dp'), 'tensor'), parts along dimension 0
- scores: float32 [128, 16], P(('groups', 'dp')), parts along dimension 0
The draws below stay inside these ranges and needn't reach their ends.
There are 2 independent parts, one for each index of `groups`. The reference program is written for one: setup_inputs(seed, part) draws one part's arguments, and reference() takes and returns one part's arrays. A program takes and returns all parts, laid end to end along the dimension named above; an argument that names none is the same for every part. Nothing has to cross between parts.
Inputs may be any that keep to these rules, and one draw needn't show every extreme that they name: `doc_ids`: within each block of 128 tokens ids never fall, every id 0 to 7 occurs, and one document has exactly 64 tokens.
All inputs are finite; a program needn't handle non-finite values.
Results may differ from the reference program's by a relative error of at most 0.0003.
Values may be sent and summed in bfloat16 or wider, within the bound.
No kernel may reach another device: no remote copies, remote signals or barrier semaphores. Data moves between devices by JAX's collectives and lax.ppermute only.
A program may use at most 64 MiB of HBM per device.

```python
import math
import jax
import jax.numpy as jnp
import numpy as np
from jax import lax

D = 4096
FF = 14336
RANK = 64
QUERIES = 16
TOK_DEV = 128
DOCS_DEV = 8
SHARDS = 8
TOKENS = 1024
DOCS = 64


def steps_of(key, shape, shards, low, high):
    def one(axis_at, parts):
        draws = jax.random.uniform(jax.random.fold_in(jax.random.fold_in(key, 6), axis_at), (parts,), jnp.float32, low / len(shards), high / len(shards))
        return jnp.repeat(jnp.exp(draws), shape[axis_at] // parts).reshape((-1,) + (1,) * (len(shape) - axis_at - 1))

    loudness = one(*shards[0])
    for cut in shards[1:]:
        loudness = loudness * one(*cut)
    return loudness


def profile(number_of, total, limit, skew):
    portions = [(1 << 20) // math.isqrt(grade ** skew) + 1 for grade in range(2, number_of + 1)]
    surplus, holding = total - limit - (number_of - 1), [1] * (number_of - 1)
    while surplus > 0:
        candidates = [i for i in range(number_of - 1) if holding[i] < limit]
        whole, remaining = sum([portions[i] for i in candidates]), surplus
        for i in candidates:
            extra = min(limit - holding[i], max(1, remaining * portions[i] // whole), surplus)
            holding[i] = holding[i] + extra
            surplus = surplus - extra
    return np.array([limit] + holding)


def uneven(rng, number_of, total, most, slope):
    if number_of == 2:
        one = jax.random.randint(rng, (), max(1, total - most), min(most, total - 1) + 1)
        return jnp.stack([one, total - one])
    tallies = jnp.asarray(profile(number_of, total, most, slope), jnp.int32)
    twos = (number_of - 1) // 2
    donor, taker = tallies[1:1 + 2 * twos:2], tallies[2:2 + 2 * twos:2]
    margin = jnp.minimum(donor - 1, most - taker)
    passed = jax.random.randint(jax.random.fold_in(rng, 1), (twos,), 0, 1 << 20) % (margin + 1)
    tallies = tallies.at[1:1 + 2 * twos:2].set(donor - passed).at[2:2 + 2 * twos:2].set(taker + passed)
    return tallies[jax.random.permutation(jax.random.fold_in(rng, 2), number_of)]


def bell_draw(key, shape, deviation, most, split=(), kind=jnp.bfloat16):
    values = deviation * jax.random.normal(key, shape, jnp.float32)
    if split:
        values = values * steps_of(key, shape, split, -0.22, 0.18)
    return jnp.clip(values, -most, most).astype(kind)


def setup_inputs(seed: int = 0, part: int = 0) -> dict:
    seeds = jax.random.split(jax.random.key(seed), 7)
    part_splits = jax.random.split(jax.random.fold_in(seeds[6], part), 7)
    return {
        "inputs": bell_draw(part_splits[0], (TOKENS, FF), 1.0, 6.0, ((0, 8), (1, 2))),
        "out_grads": bell_draw(part_splits[1], (TOKENS, D), 1.0, 6.0, ((0, 8), (1, 2))),
        "proj_in": bell_draw(seeds[2], (FF, RANK), FF ** -0.5, 0.046875),
        "proj_out": bell_draw(seeds[3], (D, RANK), D ** -0.5, 0.09375),
        "doc_ids": jax.vmap(lambda own: jnp.searchsorted(jnp.cumsum(uneven(own, DOCS_DEV, TOK_DEV, TOK_DEV // 2, 1)), jnp.arange(TOK_DEV), side="right"))(jax.random.split(part_splits[4], SHARDS)).reshape((SHARDS, TOK_DEV)).astype(jnp.int32),
        "queries": bell_draw(seeds[5], (QUERIES, RANK * RANK), 1.0, 6.0, (), jnp.float32),
    }


def reference(inputs, out_grads, proj_in, proj_out, doc_ids, queries):
    in_code = jnp.dot(inputs, proj_in, preferred_element_type=jnp.float32).reshape(SHARDS, TOK_DEV, RANK)
    grad_code = jnp.dot(out_grads, proj_out, preferred_element_type=jnp.float32).reshape(SHARDS, TOK_DEV, RANK)
    onehot = (doc_ids[:, :, None] == jnp.arange(DOCS_DEV, dtype=jnp.int32)[None, None, :]).astype(jnp.float32)
    raw = jnp.einsum('std,sti,stj->sdij', onehot, grad_code, in_code, precision=lax.Precision.HIGHEST)
    count = lax.optimization_barrier(jnp.sum(onehot, axis=1))
    features = (raw / jnp.sqrt(count)[:, :, None, None]).reshape(DOCS, RANK * RANK)
    gram = jnp.dot(features, features.T, precision=lax.Precision.HIGHEST) / (RANK * RANK)
    scores = jnp.dot(features, queries.T, precision=lax.Precision.HIGHEST) / RANK
    return (gram, scores)
```

```python
import functools

import jax
import jax.numpy as jnp
from jax import lax
from jax.experimental import pallas as pl
from jax.experimental.pallas import tpu as pltpu
from jax.sharding import PartitionSpec as P

DOCS_DEV = 8
HIGHEST = lax.Precision.HIGHEST
NT = (((1,), (1,)), ((), ()))
TN = (((0,), (0,)), ((), ()))


def chunks_of(depth):
    for size in (1024, 512, 256, 128):
        if depth % size == 0:
            return [(at, size) for at in range(0, depth, size)]
    return [(0, depth)]


def codes_kernel(x_hbm, y_hbm, wx_hbm, wy_hbm, out_ref, x, y, wx, wy, sems):
    at_core = lax.axis_index("tensor")
    rank = wx.shape[0]
    jobs = []
    for src, w_src, dst, w_dst, row in ((y_hbm, wy_hbm, y, wy, 0), (x_hbm, wx_hbm, x, wx, rank)):
        depth = dst.shape[1]
        for at, size in chunks_of(depth):
            jobs.append((src, w_src, dst, w_dst, row, depth, at, size))
    copies = []
    for n, (src, w_src, dst, w_dst, row, depth, at, size) in enumerate(jobs):
        w_at = pl.multiple_of(at_core * depth + at, 128)
        pair = (
            pltpu.make_async_copy(w_src.at[:, pl.ds(w_at, size)], w_dst.at[:, pl.ds(at, size)], sems.at[2 * n]),
            pltpu.make_async_copy(src.at[:, pl.ds(at, size)], dst.at[:, pl.ds(at, size)], sems.at[2 * n + 1]),
        )
        for copy in pair:
            copy.start()
        copies.append(pair)
    totals = {}
    for (src, w_src, dst, w_dst, row, depth, at, size), pair in zip(jobs, copies):
        for copy in pair:
            copy.wait()
        part = lax.dot_general(
            w_dst[:, at : at + size], dst[:, at : at + size], NT, preferred_element_type=jnp.float32
        )
        totals[row] = part if row not in totals else totals[row] + part
    for row, total in totals.items():
        out_ref[row : row + rank, :] = total


def partial_codes(inputs, out_grads, proj_in_t, proj_out_t):
    tokens, depth_in = inputs.shape
    depth_out = out_grads.shape[1]
    rank = proj_in_t.shape[0]
    jobs = len(chunks_of(depth_in)) + len(chunks_of(depth_out))
    return pl.pallas_call(
        codes_kernel,
        out_shape=jax.ShapeDtypeStruct((2 * rank, tokens), jnp.float32),
        in_specs=[pl.BlockSpec(memory_space=pl.ANY)] * 4,
        out_specs=pl.BlockSpec(memory_space=pltpu.VMEM),
        scratch_shapes=[
            pltpu.VMEM((tokens, depth_in), inputs.dtype),
            pltpu.VMEM((tokens, depth_out), out_grads.dtype),
            pltpu.VMEM((rank, depth_in), proj_in_t.dtype),
            pltpu.VMEM((rank, depth_out), proj_out_t.dtype),
            pltpu.SemaphoreType.DMA((2 * jobs,)),
        ],
        compiler_params=pltpu.CompilerParams(vmem_limit_bytes=24 << 20),
        name="partial_codes",
    )(inputs, out_grads, proj_in_t, proj_out_t)


def add_kernel(mine_ref, other_ref, ids_ref, out_ref):
    rows, tokens = mine_ref.shape
    out_ref[:rows, :] = mine_ref[...] + other_ref[...]
    out_ref[rows:, :] = jnp.broadcast_to(ids_ref[...].astype(jnp.float32), (8, tokens))


def add_pair(mine, other, ids):
    rows, tokens = mine.shape
    return pl.pallas_call(
        add_kernel,
        out_shape=jax.ShapeDtypeStruct((rows + 8, tokens), jnp.float32),
        name="add_pair",
    )(mine, other, ids)


def doc_weights(ids, first, docs):
    tokens = ids.shape[1]
    rows = lax.broadcasted_iota(jnp.int32, (docs, tokens), 0)
    onehot = (rows == ids.astype(jnp.int32) + first).astype(jnp.float32)
    count = jnp.sum(onehot, axis=1, keepdims=True)
    return onehot / jnp.sqrt(jnp.maximum(count, 1.0))


def scores_kernel(codes_ref, queries_ref, out_ref):
    rows, tokens = codes_ref.shape
    rank = (rows - 8) // 2
    weights = doc_weights(codes_ref[2 * rank : 2 * rank + 1, :], 0, DOCS_DEV)
    grads = codes_ref[:rank, :]
    ins = codes_ref[rank : 2 * rank, :]
    weighted = (grads[:, None, :] * weights[None, :, :]).reshape(rank * DOCS_DEV, tokens)
    twice = jnp.concatenate([ins, ins], axis=0)
    feats = lax.dot_general(weighted, twice, NT, precision=HIGHEST, preferred_element_type=jnp.float32)
    feats = feats.reshape(rank, DOCS_DEV, 2 * rank)
    low = lax.broadcasted_iota(jnp.int32, (DOCS_DEV, 2 * rank), 1) < rank
    flat = jnp.concatenate(
        [jnp.where(low, feats[i], feats[i + 1]) for i in range(0, rank, 2)], axis=1
    )
    out_ref[...] = lax.dot_general(
        flat, queries_ref[...], NT, precision=HIGHEST, preferred_element_type=jnp.float32
    ) * (1.0 / rank)


def score_docs(codes, queries):
    return pl.pallas_call(
        scores_kernel,
        out_shape=jax.ShapeDtypeStruct((DOCS_DEV, queries.shape[0]), jnp.float32),
        cost_estimate=pl.CostEstimate(flops=1 << 26, bytes_accessed=1 << 19, transcendentals=0),
        name="score_docs",
    )(codes, queries)


def gram_kernel(place_ref, own_ref, *refs):
    blocks, out_ref = refs[:-1], refs[-1]
    rank = (own_ref.shape[0] - 8) // 2
    half = len(blocks)
    own_grads, own_ins = own_ref[:rank, :], own_ref[rank : 2 * rank, :]
    weights = doc_weights(own_ref[2 * rank : 2 * rank + 1, :], 0, DOCS_DEV)
    total = jnp.zeros(out_ref.shape, jnp.float32)
    for n, block_ref in enumerate(blocks):
        block = block_ref[...]
        if n == 0:
            block = jnp.where(place_ref[half] == 1, own_ref[...], block)
        dots = functools.partial(
            lax.dot_general, precision=HIGHEST, preferred_element_type=jnp.float32
        )
        product = dots(own_grads, block[:rank, :], TN) * dots(own_ins, block[rank : 2 * rank, :], TN)
        theirs = doc_weights(
            block[2 * rank : 2 * rank + 1, :], place_ref[n] * DOCS_DEV, half * DOCS_DEV
        )
        rows = lax.dot_general(
            weights, product, (((1,), (0,)), ((), ())), precision=HIGHEST, preferred_element_type=jnp.float32
        )
        total = total + dots(rows, theirs, NT)
    out_ref[...] = total * (1.0 / (rank * rank))


def gram_of(place, own, blocks):
    half = len(blocks)
    return pl.pallas_call(
        gram_kernel,
        out_shape=jax.ShapeDtypeStruct((DOCS_DEV, half * DOCS_DEV), jnp.float32),
        in_specs=[pl.BlockSpec(memory_space=pltpu.SMEM)]
        + [pl.BlockSpec(memory_space=pltpu.VMEM)] * (1 + half),
        compiler_params=pltpu.CompilerParams(vmem_limit_bytes=24 << 20),
        name="gram_rows",
    )(place, own, *blocks)


def local(inputs, out_grads, proj_in, proj_out, doc_ids, queries):
    shards = lax.axis_size("dp")
    half = shards // 2
    shard, core = lax.axis_index("dp"), lax.axis_index("tensor")
    mine = partial_codes(inputs, out_grads, proj_in.T, proj_out.T)
    other = lax.ppermute(mine, "tensor", [(0, 1), (1, 0)])
    own = add_pair(mine, other, doc_ids)
    blocks, places = [], []
    for step in range(half):
        moves = []
        for s in range(shards):
            side = s // half
            if step:
                moves.append((s * 2 + side, (s + step) % shards * 2 + side))
            moves.append((s * 2 + 1 - side, (s + step + half) % shards * 2 + side))
        blocks.append(lax.ppermute(own, ("dp", "tensor"), moves))
        near = lax.rem(shard - step + shards, shards)
        places.append(lax.rem(near, half))
    is_own = (shard // half == core).astype(jnp.int32)
    place = jnp.stack(places + [is_own]).astype(jnp.int32)
    scores = score_docs(own, queries)
    return gram_of(place, own, blocks), scores


def solution(mesh):
    return jax.shard_map(
        local,
        mesh=mesh,
        in_specs=(
            P(("groups", "dp"), "tensor"),
            P(("groups", "dp"), "tensor"),
            P(),
            P(),
            P(("groups", "dp"), None),
            P(),
        ),
        out_specs=(P(("groups", "dp"), "tensor"), P(("groups", "dp"), None)),
        check_vma=False,
    )
```

```python
import functools

import jax
import jax.numpy as jnp
from jax import lax
from jax.experimental import pallas as pl
from jax.experimental.pallas import tpu as pltpu
from jax.sharding import PartitionSpec as P

DOCS_DEV = 8
EXTRA = 8
STEPS = 8.0
TOP = 32767.0
NT = (((1,), (1,)), ((), ()))
NN = (((1,), (0,)), ((), ()))
VMEM = pl.BlockSpec(memory_space=pltpu.VMEM)
HBM = pl.BlockSpec(memory_space=pltpu.HBM)

dot = functools.partial(lax.dot_general, preferred_element_type=jnp.float32)


def chunks_of(depth):
    for size in (1024, 512, 256, 128):
        if depth % size == 0:
            return [(at, size) for at in range(0, depth, size)]
    return [(0, depth)]


def halves(values):
    high = values.astype(jnp.bfloat16)
    return high, (values - high.astype(jnp.float32)).astype(jnp.bfloat16)


def members(ids, docs):
    rows = lax.broadcasted_iota(jnp.int32, (docs, ids.shape[1]), 0)
    return (rows == ids).astype(jnp.float32)


def codes_kernel(x_hbm, y_hbm, wx_hbm, wy_hbm, out_ref, x, y, wx, wy, sems):
    at_core = lax.axis_index("tensor")
    rank = wx.shape[0]
    copies = []
    for src, w_src, dst, w_dst, row in ((y_hbm, wy_hbm, y, wy, 0), (x_hbm, wx_hbm, x, wx, rank)):
        depth = dst.shape[1]
        for at, size in chunks_of(depth):
            w_at = pl.multiple_of(at_core * depth + at, 128)
            here = pl.ds(at, size)
            sem = 2 * len(copies)
            pair = (
                pltpu.make_async_copy(w_src.at[:, pl.ds(w_at, size)], w_dst.at[:, here], sems.at[sem]),
                pltpu.make_async_copy(src.at[:, here], dst.at[:, here], sems.at[sem + 1]),
            )
            for copy in pair:
                copy.start()
            copies.append((pair, dst, w_dst, row, at, size))
    totals = {}
    for pair, dst, w_dst, row, at, size in copies:
        for copy in pair:
            copy.wait()
        part = dot(w_dst[:, at : at + size], dst[:, at : at + size], NT)
        totals[row] = totals[row] + part if row in totals else part
    out_ref[:rank, :] = totals[0]
    out_ref[rank:, :] = totals[rank]


def partial_codes(inputs, out_grads, proj_in_t, proj_out_t):
    tokens, depth_in = inputs.shape
    depth_out = out_grads.shape[1]
    rank = proj_in_t.shape[0]
    jobs = len(chunks_of(depth_in)) + len(chunks_of(depth_out))
    return pl.pallas_call(
        codes_kernel,
        out_shape=jax.ShapeDtypeStruct((2 * rank, tokens), jnp.float32),
        in_specs=[HBM] * 4,
        out_specs=VMEM,
        scratch_shapes=[
            pltpu.VMEM((tokens, depth_in), inputs.dtype),
            pltpu.VMEM((tokens, depth_out), out_grads.dtype),
            pltpu.VMEM((rank, depth_in), proj_in_t.dtype),
            pltpu.VMEM((rank, depth_out), proj_out_t.dtype),
            pltpu.SemaphoreType.DMA((2 * jobs,)),
        ],
        compiler_params=pltpu.CompilerParams(vmem_limit_bytes=56_000_000),
        name="partial_codes",
    )(inputs, out_grads, proj_in_t, proj_out_t)


def fixed_point(values):
    largest = jnp.max(jnp.abs(values), axis=0, keepdims=True)
    grade = jnp.ceil(jnp.log(jnp.maximum(largest, 1e-30)) * (STEPS / 0.6931471805599453) + 0.01)
    units = values * (TOP * jnp.exp2(grade * (-1.0 / STEPS)))
    units = jnp.clip(jnp.floor(units + 0.5), -TOP, TOP)
    return units.astype(jnp.int32), grade.astype(jnp.int32)


def pack_kernel(mine_ref, other_ref, ids_ref, own_ref, message_ref):
    rows, tokens = mine_ref.shape
    rank = rows // 2
    ids = ids_ref[...]
    onehot = members(ids, DOCS_DEV)
    count = jnp.maximum(jnp.sum(onehot, axis=1, keepdims=True), 1.0)
    weight = jnp.sum(onehot / jnp.sqrt(count), axis=0, keepdims=True)
    grads = mine_ref[:rank, :] + other_ref[:rank, :]
    ins = (mine_ref[rank:, :] + other_ref[rank:, :]) * weight
    own_ref[:rank, :] = grads
    own_ref[rank:, :] = ins
    grad_units, grad_grade = fixed_point(grads)
    in_units, in_grade = fixed_point(ins)
    message_ref[:rank, :] = lax.shift_left(grad_units, 16) | (in_units & 0xFFFF)
    line = lax.broadcasted_iota(jnp.int32, (EXTRA, tokens), 0)
    message_ref[rank:, :] = jnp.where(
        line == 0, ids, jnp.where(line == 1, grad_grade, in_grade)
    )


def pack(mine, other, doc_ids):
    rows, tokens = mine.shape
    rank = rows // 2
    return pl.pallas_call(
        pack_kernel,
        out_shape=(
            jax.ShapeDtypeStruct((rows, tokens), jnp.float32),
            jax.ShapeDtypeStruct((rank + EXTRA, tokens), jnp.int32),
        ),
        in_specs=[VMEM] * 3,
        out_specs=(VMEM, VMEM),
        name="pack_codes",
    )(mine, other, doc_ids)


def scores_kernel(own_ref, message_ref, queries, scores_ref, grads_ref, ins_ref):
    rows, tokens = own_ref.shape
    rank = rows // 2
    grads = own_ref[:rank, :]
    ins = own_ref[rank:, :]
    onehot = members(message_ref[rank : rank + 1, :], DOCS_DEV)
    for values, ref in ((grads, grads_ref), (ins, ins_ref)):
        high, low = halves(values)
        stacked = jnp.concatenate([high, high, low, low], axis=0)
        ref[...] = stacked.T
    weighted = (grads[:, None, :] * onehot[None, :, :]).reshape(rank * DOCS_DEV, tokens)
    w_high, w_low = halves(weighted)
    i_high, i_low = halves(jnp.concatenate([ins, ins], axis=0))
    feats = dot(
        jnp.concatenate([w_high, w_high, w_low], axis=1),
        jnp.concatenate([i_high, i_low, i_high], axis=1),
        NT,
    )
    left = lax.broadcasted_iota(jnp.int32, (DOCS_DEV, 2 * rank), 1) < rank
    pairs = [
        jnp.where(
            left,
            feats[i * DOCS_DEV : (i + 1) * DOCS_DEV],
            feats[(i + 1) * DOCS_DEV : (i + 2) * DOCS_DEV],
        )
        for i in range(0, rank, 2)
    ]
    count = queries.shape[0]
    sums = [None] * count
    for n, pair in enumerate(pairs):
        block = queries[:, n * 2 * rank : (n + 1) * 2 * rank]
        for q in range(count):
            term = pair * block[q : q + 1, :]
            sums[q] = term if n == 0 else sums[q] + term
    columns = [jnp.sum(total, axis=1, keepdims=True) for total in sums]
    scores_ref[...] = jnp.concatenate(columns, axis=1) * (1.0 / rank)


def score_docs(own, message, queries):
    rows, tokens = own.shape
    rank = rows // 2
    operand = jax.ShapeDtypeStruct((tokens, 4 * rank), jnp.bfloat16)
    return pl.pallas_call(
        scores_kernel,
        out_shape=(
            jax.ShapeDtypeStruct((DOCS_DEV, queries.shape[0]), jnp.float32),
            operand,
            operand,
        ),
        in_specs=[VMEM] * 3,
        out_specs=(VMEM, VMEM, VMEM),
        compiler_params=pltpu.CompilerParams(vmem_limit_bytes=24 << 20),
        cost_estimate=pl.CostEstimate(flops=1 << 26, bytes_accessed=1 << 19, transcendentals=0),
        name="score_docs",
    )(own, message, queries)


def gram_kernel(message_ref, grads_ref, ins_ref, *refs):
    blocks, out_ref = refs[:-1], refs[-1]
    half = len(blocks)
    shards = 2 * half
    rank = message_ref.shape[0] - EXTRA
    shard, core = lax.axis_index("dp"), lax.axis_index("tensor")
    onehot = members(message_ref[rank : rank + 1, :], DOCS_DEV).astype(jnp.bfloat16)
    doubled = jnp.concatenate([onehot, onehot], axis=1)
    total = None
    width = min(4, half)
    for first in range(0, half, width):
        codes, ids, scales = [], [], []
        for n in range(first, min(first + width, half)):
            block = blocks[n][...]
            if n == 0:
                block = jnp.where(lax.div(shard, half) == core, message_ref[...], block)
            place = lax.rem(lax.rem(shard - n + shards, shards), half)
            codes.append(block[:rank, :])
            ids.append(block[rank : rank + 1, :] + place * DOCS_DEV)
            scales.append((block[rank + 1 : rank + 2, :] + block[rank + 2 : rank + 3, :]).astype(jnp.float32))
        codes, ids, scales = (jnp.concatenate(part, axis=1) for part in (codes, ids, scales))
        product = None
        for units, left in (
            (lax.shift_right_arithmetic(codes, 16), grads_ref),
            (lax.shift_right_arithmetic(lax.shift_left(codes, 16), 16), ins_ref),
        ):
            high, low = halves(units.astype(jnp.float32))
            part = dot(left[...], jnp.concatenate([high, low, high, low], axis=0), NN)
            product = part if product is None else product * part
        high, low = halves(product)
        by_doc = dot(doubled, jnp.concatenate([high, low], axis=0), NN)
        by_doc = by_doc * (jnp.exp2(scales * (1.0 / STEPS)) * (1.0 / (TOP * TOP)))
        high, low = halves(by_doc)
        theirs = members(ids, half * DOCS_DEV).astype(jnp.bfloat16)
        part = dot(jnp.concatenate([high, low], axis=0), theirs, NT)
        total = part if total is None else total + part
    out_ref[...] = (total[:DOCS_DEV, :] + total[DOCS_DEV:, :]) * (1.0 / (rank * rank))


def gram_of(message, grads, ins, blocks):
    half = len(blocks)
    return pl.pallas_call(
        gram_kernel,
        out_shape=jax.ShapeDtypeStruct((DOCS_DEV, half * DOCS_DEV), jnp.float32),
        in_specs=[VMEM] * (3 + half),
        out_specs=VMEM,
        compiler_params=pltpu.CompilerParams(vmem_limit_bytes=24 << 20),
        name="gram_rows",
    )(message, grads, ins, *blocks)


def local(inputs, out_grads, proj_in, proj_out, doc_ids, queries):
    shards = lax.axis_size("dp")
    half = shards // 2
    mine = partial_codes(inputs, out_grads, proj_in.T, proj_out.T)
    other = lax.ppermute(mine, "tensor", [(0, 1), (1, 0)])
    own, message = pack(mine, other, doc_ids)
    blocks = []
    for step in range(half):
        moves = []
        for s in range(shards):
            side = s // half
            if step:
                moves.append((s * 2 + side, (s + step) % shards * 2 + side))
            moves.append((s * 2 + 1 - side, (s + step + half) % shards * 2 + side))
        blocks.append(lax.ppermute(message, ("dp", "tensor"), moves))
    scores, grads, ins = score_docs(own, message, queries)
    return gram_of(message, grads, ins, blocks), scores


def solution(mesh):
    return jax.shard_map(
        local,
        mesh=mesh,
        in_specs=(
            P(("groups", "dp"), "tensor"),
            P(("groups", "dp"), "tensor"),
            P(),
            P(),
            P(("groups", "dp"), None),
            P(),
        ),
        out_specs=(P(("groups", "dp"), "tensor"), P(("groups", "dp"), None)),
        check_vma=False,
    )
```

```python
import functools

import jax
import jax.numpy as jnp
from jax import lax
from jax.experimental import pallas as pl
from jax.experimental.pallas import tpu as pltpu
from jax.sharding import PartitionSpec as P

DOCS_DEV = 8
EXTRA = 8
STEPS = 8.0
TOP = 32767.0
NT = (((1,), (1,)), ((), ()))
NN = (((1,), (0,)), ((), ()))
VMEM = pl.BlockSpec(memory_space=pltpu.VMEM)
HBM = pl.BlockSpec(memory_space=pltpu.HBM)
SMALL = pltpu.CompilerParams(vmem_limit_bytes=16 << 20)

dot = functools.partial(lax.dot_general, preferred_element_type=jnp.float32)


def chunks_of(depth):
    for size in (1024, 512, 256, 128):
        if depth % size == 0:
            return [(at, size) for at in range(0, depth, size)]
    return [(0, depth)]


def halves(values):
    high = values.astype(jnp.bfloat16)
    return high, (values - high.astype(jnp.float32)).astype(jnp.bfloat16)


def members(ids, docs):
    rows = lax.broadcasted_iota(jnp.int32, (docs, ids.shape[1]), 0)
    return (rows == ids).astype(jnp.float32)


def codes_kernel(x_hbm, y_hbm, wx_hbm, wy_hbm, out_ref, x, y, wx, wy, sems):
    at_core = lax.axis_index("tensor")
    rank = wx.shape[0]
    copies = []
    for src, w_src, dst, w_dst, row in ((y_hbm, wy_hbm, y, wy, 0), (x_hbm, wx_hbm, x, wx, rank)):
        depth = dst.shape[1]
        for at, size in chunks_of(depth):
            w_at = pl.multiple_of(at_core * depth + at, 128)
            here = pl.ds(at, size)
            sem = 2 * len(copies)
            pair = (
                pltpu.make_async_copy(w_src.at[:, pl.ds(w_at, size)], w_dst.at[:, here], sems.at[sem]),
                pltpu.make_async_copy(src.at[:, here], dst.at[:, here], sems.at[sem + 1]),
            )
            for copy in pair:
                copy.start()
            copies.append((pair, dst, w_dst, row, at, size))
    totals = {}
    for pair, dst, w_dst, row, at, size in copies:
        for copy in pair:
            copy.wait()
        part = dot(dst[:, at : at + size], w_dst[:, at : at + size], NT)
        totals[row] = totals[row] + part if row in totals else part
    out_ref[...] = jnp.concatenate([totals[0], totals[rank]], axis=1).T


def partial_codes(inputs, out_grads, proj_in_t, proj_out_t):
    tokens, depth_in = inputs.shape
    depth_out = out_grads.shape[1]
    rank = proj_in_t.shape[0]
    jobs = len(chunks_of(depth_in)) + len(chunks_of(depth_out))
    return pl.pallas_call(
        codes_kernel,
        out_shape=jax.ShapeDtypeStruct((2 * rank, tokens), jnp.float32),
        in_specs=[HBM] * 4,
        out_specs=VMEM,
        scratch_shapes=[
            pltpu.VMEM((tokens, depth_in), inputs.dtype),
            pltpu.VMEM((tokens, depth_out), out_grads.dtype),
            pltpu.VMEM((rank, depth_in), proj_in_t.dtype),
            pltpu.VMEM((rank, depth_out), proj_out_t.dtype),
            pltpu.SemaphoreType.DMA((2 * jobs,)),
        ],
        compiler_params=pltpu.CompilerParams(vmem_limit_bytes=56_000_000),
        name="partial_codes",
    )(inputs, out_grads, proj_in_t, proj_out_t)


def fixed_point(values):
    largest = jnp.max(jnp.abs(values), axis=0, keepdims=True)
    grade = jnp.ceil(jnp.log(jnp.maximum(largest, 1e-30)) * (STEPS / 0.6931471805599453) + 0.01)
    units = values * (TOP * jnp.exp2(grade * (-1.0 / STEPS)))
    units = jnp.clip(jnp.floor(units + 0.5), -TOP, TOP)
    return units.astype(jnp.int32), grade.astype(jnp.int32)


def swap(values):
    return pltpu.roll(values, values.shape[1] // 2, 1)


def pack_kernel(mine_ref, other_ref, ids_ref, own_ref, notes_ref, message_ref):
    rows, tokens = mine_ref.shape
    rank = rows // 2
    ids = ids_ref[...]
    onehot = members(ids, DOCS_DEV)
    count = jnp.maximum(jnp.sum(onehot, axis=1, keepdims=True), 1.0)
    weight = jnp.sum(onehot / jnp.sqrt(count), axis=0, keepdims=True)
    grads = mine_ref[:rank, :] + other_ref[:rank, :]
    ins = (mine_ref[rank:, :] + other_ref[rank:, :]) * weight
    own_ref[:rank, :] = grads
    own_ref[rank:, :] = ins
    grad_units, grad_grade = fixed_point(grads)
    in_units, in_grade = fixed_point(ins)
    units = lax.shift_left(grad_units, 16) | (in_units & 0xFFFF)
    line = lax.broadcasted_iota(jnp.int32, (EXTRA, tokens), 0)
    notes = jnp.where(line == 0, ids, jnp.where(line == 1, grad_grade, in_grade))
    notes_ref[...] = notes
    left = lax.broadcasted_iota(jnp.int32, (rank // 2, tokens), 1) < tokens // 2
    first = lax.axis_index("tensor") == 0
    top, bottom = units[: rank // 2, :], units[rank // 2 :, :]
    top_away, bottom_away = swap(top), swap(bottom)
    message = jnp.where(left, jnp.where(first, top, top_away), jnp.where(first, bottom_away, bottom))
    notes = jnp.where(first, notes, swap(notes))
    for s in range(message_ref.shape[0]):
        message_ref[s, : rank // 2, :] = message
        message_ref[s, rank // 2 :, :] = notes


def pack(mine, other, doc_ids, shards):
    rows, tokens = mine.shape
    rank = rows // 2
    return pl.pallas_call(
        pack_kernel,
        out_shape=(
            jax.ShapeDtypeStruct((rows, tokens), jnp.float32),
            jax.ShapeDtypeStruct((EXTRA, tokens), jnp.int32),
            jax.ShapeDtypeStruct((shards, rank // 2 + EXTRA, tokens), jnp.int32),
        ),
        in_specs=[VMEM] * 3,
        out_specs=(VMEM,) * 3,
        compiler_params=SMALL,
        name="pack_codes",
    )(mine, other, doc_ids)


def scores_kernel(own_ref, notes_ref, queries, scores_ref, grads_ref, ins_ref):
    rows, tokens = own_ref.shape
    rank = rows // 2
    grads = own_ref[:rank, :]
    ins = own_ref[rank:, :]
    onehot = members(notes_ref[:1, :], DOCS_DEV)
    for values, ref in ((grads, grads_ref), (ins, ins_ref)):
        high, low = halves(values)
        stacked = jnp.concatenate([high, high, low, low], axis=0)
        ref[...] = stacked.T
    weighted = (grads[:, None, :] * onehot[None, :, :]).reshape(rank * DOCS_DEV, tokens)
    w_high, w_low = halves(weighted)
    i_high, i_low = halves(jnp.concatenate([ins, ins], axis=0))
    feats = dot(
        jnp.concatenate([w_high, w_high, w_low], axis=1),
        jnp.concatenate([i_high, i_low, i_high], axis=1),
        NT,
    )
    left = lax.broadcasted_iota(jnp.int32, (DOCS_DEV, 2 * rank), 1) < rank
    pairs = [
        jnp.where(
            left,
            feats[i * DOCS_DEV : (i + 1) * DOCS_DEV],
            feats[(i + 1) * DOCS_DEV : (i + 2) * DOCS_DEV],
        )
        for i in range(0, rank, 2)
    ]
    count = queries.shape[0]
    sums = [None] * count
    for n, pair in enumerate(pairs):
        block = queries[:, n * 2 * rank : (n + 1) * 2 * rank]
        for q in range(count):
            term = pair * block[q : q + 1, :]
            sums[q] = term if n == 0 else sums[q] + term
    columns = [jnp.sum(total, axis=1, keepdims=True) for total in sums]
    scores_ref[...] = jnp.concatenate(columns, axis=1) * (1.0 / rank)


def score_docs(own, notes, queries):
    rows, tokens = own.shape
    rank = rows // 2
    operand = jax.ShapeDtypeStruct((tokens, 4 * rank), jnp.bfloat16)
    return pl.pallas_call(
        scores_kernel,
        out_shape=(
            jax.ShapeDtypeStruct((DOCS_DEV, queries.shape[0]), jnp.float32),
            operand,
            operand,
        ),
        in_specs=[VMEM] * 3,
        out_specs=(VMEM, VMEM, VMEM),
        compiler_params=SMALL,
        cost_estimate=pl.CostEstimate(flops=1 << 26, bytes_accessed=1 << 19, transcendentals=0),
        name="score_docs",
    )(own, notes, queries)


def gram_kernel(notes_ref, grads_ref, ins_ref, blocks_ref, keep_ref, give_ref):
    shards = blocks_ref.shape[0]
    half = shards // 2
    tokens = notes_ref.shape[1]
    rank = 2 * (blocks_ref.shape[1] - EXTRA)
    core = lax.axis_index("tensor")
    onehot = members(notes_ref[:1, :], DOCS_DEV).astype(jnp.bfloat16)
    doubled = jnp.concatenate([onehot, onehot], axis=1)
    left = lax.broadcasted_iota(jnp.int32, (blocks_ref.shape[1], tokens), 1) < tokens // 2
    left_line = left[:1, :]
    total = None
    width = min(8, shards)
    for start in range(0, shards, width):
        codes, ids, scales = [], [], []
        for s in range(start, start + width, 2):
            one, two = blocks_ref[s], blocks_ref[s + 1]
            top = jnp.where(left, one, swap(two))
            bottom = jnp.where(left[: rank // 2], swap(one[: rank // 2, :]), two[: rank // 2, :])
            codes.append(jnp.concatenate([top[: rank // 2, :], bottom], axis=0))
            notes = top[rank // 2 :, :]
            first, second = (lax.rem(at + core * half, shards) * DOCS_DEV for at in (s, s + 1))
            ids.append(notes[:1, :] + jnp.where(left_line, first, second))
            scales.append((notes[1:2, :] + notes[2:3, :]).astype(jnp.float32))
        codes, ids, scales = (jnp.concatenate(part, axis=1) for part in (codes, ids, scales))
        product = None
        for units, side in (
            (lax.shift_right_arithmetic(codes, 16), grads_ref),
            (lax.shift_right_arithmetic(lax.shift_left(codes, 16), 16), ins_ref),
        ):
            high, low = halves(units.astype(jnp.float32))
            part = dot(side[...], jnp.concatenate([high, low, high, low], axis=0), NN)
            product = part if product is None else product * part
        high, low = halves(product)
        by_doc = dot(doubled, jnp.concatenate([high, low], axis=0), NN)
        by_doc = by_doc * (jnp.exp2(scales * (1.0 / STEPS)) * (1.0 / (TOP * TOP)))
        high, low = halves(by_doc)
        theirs = members(ids, shards * DOCS_DEV).astype(jnp.bfloat16)
        part = dot(jnp.concatenate([high, low], axis=0), theirs, NT)
        total = part if total is None else total + part
    total = (total[:DOCS_DEV, :] + total[DOCS_DEV:, :]) * (1.0 / (rank * rank))
    keep_ref[...] = total[:, : half * DOCS_DEV]
    give_ref[...] = total[:, half * DOCS_DEV :]


def gram_parts(notes, grads, ins, blocks):
    part = jax.ShapeDtypeStruct((DOCS_DEV, blocks.shape[0] // 2 * DOCS_DEV), jnp.float32)
    return pl.pallas_call(
        gram_kernel,
        out_shape=(part, part),
        in_specs=[VMEM] * 4,
        out_specs=(VMEM,) * 2,
        compiler_params=SMALL,
        name="gram_parts",
    )(notes, grads, ins, blocks)


def local(inputs, out_grads, proj_in, proj_out, doc_ids, queries):
    pairs = [(0, 1), (1, 0)]
    mine = partial_codes(inputs, out_grads, proj_in.T, proj_out.T)
    other = lax.ppermute(mine, "tensor", pairs)
    own, notes, messages = pack(mine, other, doc_ids, lax.axis_size("dp"))
    blocks = lax.all_to_all(messages, "dp", 0, 0, tiled=True)
    scores, grads, ins = score_docs(own, notes, queries)
    keep, give = gram_parts(notes, grads, ins, blocks)
    return keep + lax.ppermute(give, "tensor", pairs), scores


def solution(mesh):
    return jax.shard_map(
        local,
        mesh=mesh,
        in_specs=(
            P(("groups", "dp"), "tensor"),
            P(("groups", "dp"), "tensor"),
            P(),
            P(),
            P(("groups", "dp"), None),
            P(),
        ),
        out_specs=(P(("groups", "dp"), "tensor"), P(("groups", "dp"), None)),
        check_vma=False,
    )
```

```python
import functools

import jax
import jax.numpy as jnp
from jax import lax
from jax.experimental import pallas as pl
from jax.experimental.pallas import tpu as pltpu
from jax.sharding import PartitionSpec as P

DOCS_DEV = 8
EXTRA = 8
STEPS = 8.0
TOP = 32767.0
NT = (((1,), (1,)), ((), ()))
NN = (((1,), (0,)), ((), ()))
VMEM = pl.BlockSpec(memory_space=pltpu.VMEM)
HBM = pl.BlockSpec(memory_space=pltpu.HBM)
SMALL = pltpu.CompilerParams(vmem_limit_bytes=16 << 20)

dot = functools.partial(lax.dot_general, preferred_element_type=jnp.float32)


def chunks_of(depth):
    size = next(size for size in (2048, 1792, 1024, 512, 256, 128, depth) if depth % size == 0)
    return [(at, size) for at in range(0, depth, size)]


def halves(values):
    high = values.astype(jnp.bfloat16)
    return high, (values - high.astype(jnp.float32)).astype(jnp.bfloat16)


def members(ids, docs):
    rows = lax.broadcasted_iota(jnp.int32, (docs, ids.shape[1]), 0)
    return (rows == ids).astype(jnp.float32)


def codes_kernel(x_hbm, y_hbm, wx_hbm, wy_hbm, out_ref, x, y, wx, wy, sems):
    at_core = lax.axis_index("tensor")
    rank = wx.shape[0]
    copies = []
    for src, w_src, dst, w_dst, row in ((y_hbm, wy_hbm, y, wy, 0), (x_hbm, wx_hbm, x, wx, rank)):
        depth = dst.shape[1]
        for at, size in chunks_of(depth):
            w_at = pl.multiple_of(at_core * depth + at, 128)
            here = pl.ds(at, size)
            sem = 2 * len(copies)
            pair = (
                pltpu.make_async_copy(w_src.at[:, pl.ds(w_at, size)], w_dst.at[:, here], sems.at[sem]),
                pltpu.make_async_copy(src.at[:, here], dst.at[:, here], sems.at[sem + 1]),
            )
            for copy in pair:
                copy.start()
            copies.append((pair, dst, w_dst, row, at, size))
    totals = {}
    for pair, dst, w_dst, row, at, size in copies:
        for copy in pair:
            copy.wait()
        part = dot(w_dst[:, at : at + size], dst[:, at : at + size], NT)
        totals[row] = totals[row] + part if row in totals else part
    out_ref[:rank, :] = totals[0]
    out_ref[rank:, :] = totals[rank]


def partial_codes(inputs, out_grads, proj_in_t, proj_out_t):
    tokens, depth_in = inputs.shape
    depth_out = out_grads.shape[1]
    rank = proj_in_t.shape[0]
    jobs = len(chunks_of(depth_in)) + len(chunks_of(depth_out))
    return pl.pallas_call(
        codes_kernel,
        out_shape=jax.ShapeDtypeStruct((2 * rank, tokens), jnp.float32),
        in_specs=[HBM] * 4,
        out_specs=VMEM,
        scratch_shapes=[
            pltpu.VMEM((tokens, depth_in), inputs.dtype),
            pltpu.VMEM((tokens, depth_out), out_grads.dtype),
            pltpu.VMEM((rank, depth_in), proj_in_t.dtype),
            pltpu.VMEM((rank, depth_out), proj_out_t.dtype),
            pltpu.SemaphoreType.DMA((2 * jobs,)),
        ],
        compiler_params=pltpu.CompilerParams(vmem_limit_bytes=56_000_000),
        name="partial_codes",
    )(inputs, out_grads, proj_in_t, proj_out_t)


def fixed_point(values):
    largest = jnp.max(jnp.abs(values), axis=0, keepdims=True)
    grade = jnp.ceil(jnp.log(jnp.maximum(largest, 1e-30)) * (STEPS / 0.6931471805599453) + 0.01)
    units = values * (TOP * jnp.exp2(grade * (-1.0 / STEPS)))
    units = jnp.clip(jnp.floor(units + 0.5), -TOP, TOP)
    return units.astype(jnp.int32), grade.astype(jnp.int32)


def pack_kernel(mine_ref, other_ref, ids_ref, own_ref, message_ref):
    rows, tokens = mine_ref.shape
    rank = rows // 2
    ids = ids_ref[...]
    onehot = members(ids, DOCS_DEV)
    count = jnp.maximum(jnp.sum(onehot, axis=1, keepdims=True), 1.0)
    weight = jnp.sum(onehot / jnp.sqrt(count), axis=0, keepdims=True)
    grads = mine_ref[:rank, :] + other_ref[:rank, :]
    ins = (mine_ref[rank:, :] + other_ref[rank:, :]) * weight
    own_ref[:rank, :] = grads
    own_ref[rank:, :] = ins
    grad_units, grad_grade = fixed_point(grads)
    in_units, in_grade = fixed_point(ins)
    message_ref[:rank, :] = lax.shift_left(grad_units, 16) | (in_units & 0xFFFF)
    line = lax.broadcasted_iota(jnp.int32, (EXTRA, tokens), 0)
    message_ref[rank:, :] = jnp.where(
        line == 0, ids, jnp.where(line == 1, grad_grade, in_grade)
    )


def pack(mine, other, doc_ids):
    rows, tokens = mine.shape
    rank = rows // 2
    return pl.pallas_call(
        pack_kernel,
        out_shape=(
            jax.ShapeDtypeStruct((rows, tokens), jnp.float32),
            jax.ShapeDtypeStruct((rank + EXTRA, tokens), jnp.int32),
        ),
        in_specs=[VMEM] * 3,
        out_specs=(VMEM, VMEM),
        compiler_params=SMALL,
        name="pack_codes",
    )(mine, other, doc_ids)


def scores_kernel(own_ref, message_ref, queries, scores_ref, grads_ref, ins_ref):
    rows, tokens = own_ref.shape
    rank = rows // 2
    grads = own_ref[:rank, :]
    ins = own_ref[rank:, :]
    onehot = members(message_ref[rank : rank + 1, :], DOCS_DEV)
    for values, ref in ((grads, grads_ref), (ins, ins_ref)):
        high, low = halves(values)
        stacked = jnp.concatenate([high, high, low, low], axis=0)
        ref[...] = stacked.T
    weighted = (grads[:, None, :] * onehot[None, :, :]).reshape(rank * DOCS_DEV, tokens)
    w_high, w_low = halves(weighted)
    i_high, i_low = halves(jnp.concatenate([ins, ins], axis=0))
    feats = dot(
        jnp.concatenate([w_high, w_high, w_low], axis=1),
        jnp.concatenate([i_high, i_low, i_high], axis=1),
        NT,
    )
    left = lax.broadcasted_iota(jnp.int32, (DOCS_DEV, 2 * rank), 1) < rank
    pairs = [
        jnp.where(
            left,
            feats[i * DOCS_DEV : (i + 1) * DOCS_DEV],
            feats[(i + 1) * DOCS_DEV : (i + 2) * DOCS_DEV],
        )
        for i in range(0, rank, 2)
    ]
    count = queries.shape[0]
    sums = [None] * count
    for n, pair in enumerate(pairs):
        block = queries[:, n * 2 * rank : (n + 1) * 2 * rank]
        for q in range(count):
            term = pair * block[q : q + 1, :]
            sums[q] = term if n == 0 else sums[q] + term
    columns = [jnp.sum(total, axis=1, keepdims=True) for total in sums]
    scores_ref[...] = jnp.concatenate(columns, axis=1) * (1.0 / rank)


def score_docs(own, message, queries):
    rows, tokens = own.shape
    rank = rows // 2
    operand = jax.ShapeDtypeStruct((tokens, 4 * rank), jnp.bfloat16)
    return pl.pallas_call(
        scores_kernel,
        out_shape=(
            jax.ShapeDtypeStruct((DOCS_DEV, queries.shape[0]), jnp.float32),
            operand,
            operand,
        ),
        in_specs=[VMEM] * 3,
        out_specs=(VMEM, VMEM, VMEM),
        compiler_params=SMALL,
        cost_estimate=pl.CostEstimate(flops=1 << 26, bytes_accessed=1 << 19, transcendentals=0),
        name="score_docs",
    )(own, message, queries)


def join_kernel(mine_ref, other_ref, out_ref):
    out_ref[0] = mine_ref[...]
    out_ref[1] = other_ref[...]


def join(mine, other):
    return pl.pallas_call(
        join_kernel,
        out_shape=jax.ShapeDtypeStruct((2,) + mine.shape, mine.dtype),
        in_specs=[VMEM] * 2,
        out_specs=VMEM,
        compiler_params=SMALL,
        name="join_plane",
    )(mine, other)


def gram_kernel(plane_ref, grads_ref, ins_ref, *refs):
    blocks, out_ref = refs[:-1], refs[-1]
    half = len(blocks)
    rank = plane_ref.shape[1] - EXTRA
    shard, core = lax.axis_index("dp"), lax.axis_index("tensor")
    plane, side = lax.div(shard, 2), lax.rem(shard, 2)
    own_half = lax.div(plane, half) == core
    onehot = members(plane_ref[0, rank : rank + 1, :], DOCS_DEV).astype(jnp.bfloat16)
    doubled = jnp.concatenate([onehot, onehot], axis=1)
    total = None
    width = min(2, half)
    for first in range(0, half, width):
        codes, ids, scales = [], [], []
        for n in range(first, first + width):
            block, near, far = blocks[n][...], n + 1, 2 * half - 1 - n
            if n == half - 1:
                block, near = jnp.where(own_half, plane_ref[...], block), 0
            source = lax.rem(lax.bitwise_xor(plane, jnp.where(own_half, near, far)), half)
            for slot, at in ((0, side), (1, 1 - side)):
                codes.append(block[slot, :rank, :])
                ids.append(block[slot, rank : rank + 1, :] + (2 * source + at) * DOCS_DEV)
                grades = block[slot, rank + 1 : rank + 2, :] + block[slot, rank + 2 : rank + 3, :]
                scales.append(grades.astype(jnp.float32))
        codes, ids, scales = (jnp.concatenate(part, axis=1) for part in (codes, ids, scales))
        product = None
        for units, left in (
            (lax.shift_right_arithmetic(codes, 16), grads_ref),
            (lax.shift_right_arithmetic(lax.shift_left(codes, 16), 16), ins_ref),
        ):
            high, low = halves(units.astype(jnp.float32))
            part = dot(left[...], jnp.concatenate([high, low, high, low], axis=0), NN)
            product = part if product is None else product * part
        high, low = halves(product)
        by_doc = dot(doubled, jnp.concatenate([high, low], axis=0), NN)
        by_doc = by_doc * (jnp.exp2(scales * (1.0 / STEPS)) * (1.0 / (TOP * TOP)))
        high, low = halves(by_doc)
        theirs = members(ids, 2 * half * DOCS_DEV).astype(jnp.bfloat16)
        part = dot(jnp.concatenate([high, low], axis=0), theirs, NT)
        total = part if total is None else total + part
    out_ref[...] = (total[:DOCS_DEV, :] + total[DOCS_DEV:, :]) * (1.0 / (rank * rank))


def gram_of(plane, grads, ins, blocks):
    return pl.pallas_call(
        gram_kernel,
        out_shape=jax.ShapeDtypeStruct((DOCS_DEV, 2 * len(blocks) * DOCS_DEV), jnp.float32),
        in_specs=[VMEM] * (3 + len(blocks)),
        out_specs=VMEM,
        compiler_params=SMALL,
        name="gram_rows",
    )(plane, grads, ins, *blocks)


def local(inputs, out_grads, proj_in, proj_out, doc_ids, queries):
    shards = lax.axis_size("dp")
    planes = shards // 2
    half = planes // 2
    mine = partial_codes(inputs, out_grads, proj_in.T, proj_out.T)
    other = lax.ppermute(mine, "tensor", [(0, 1), (1, 0)])
    own, message = pack(mine, other, doc_ids)
    plane = join(message, lax.ppermute(message, "dp", [(s, s ^ 1) for s in range(shards)]))
    blocks = []
    for n in range(half):
        moves = []
        for p in range(planes):
            for x in range(2):
                core = p // half
                if n < half - 1:
                    moves.append((4 * p + 2 * x + core, 4 * (p ^ (n + 1)) + 2 * x + core))
                far = p ^ (planes - 1 - n)
                moves.append((4 * p + 2 * x + 1 - core, 4 * far + 2 * x + 1 - far // half))
        blocks.append(lax.ppermute(plane, ("dp", "tensor"), moves))
    scores, grads, ins = score_docs(own, message, queries)
    return gram_of(plane, grads, ins, blocks), scores


def solution(mesh):
    return jax.shard_map(
        local,
        mesh=mesh,
        in_specs=(
            P(("groups", "dp"), "tensor"),
            P(("groups", "dp"), "tensor"),
            P(),
            P(),
            P(("groups", "dp"), None),
            P(),
        ),
        out_specs=(P(("groups", "dp"), "tensor"), P(("groups", "dp"), None)),
        check_vma=False,
    )
```

```python
import functools

import jax
import jax.numpy as jnp
from jax import lax
from jax.experimental import pallas as pl
from jax.experimental.pallas import tpu as pltpu
from jax.sharding import PartitionSpec as P

DOCS_DEV = 8
EXTRA = 8
STEPS = 8.0
TOP = 32767.0
NT = (((1,), (1,)), ((), ()))
NN = (((1,), (0,)), ((), ()))
VMEM = pl.BlockSpec(memory_space=pltpu.VMEM)
HBM = pl.BlockSpec(memory_space=pltpu.HBM)
SMALL = pltpu.CompilerParams(vmem_limit_bytes=16 << 20)

dot = functools.partial(lax.dot_general, preferred_element_type=jnp.float32)


def chunks_of(depth):
    size = next(size for size in (2048, 1792, 1024, 512, 256, 128, depth) if depth % size == 0)
    return [(at, size) for at in range(0, depth, size)]


def halves(values):
    high = values.astype(jnp.bfloat16)
    return high, (values - high.astype(jnp.float32)).astype(jnp.bfloat16)


def members(ids, docs):
    rows = lax.broadcasted_iota(jnp.int32, (docs, ids.shape[1]), 0)
    return (rows == ids).astype(jnp.float32)


def codes_kernel(x_hbm, y_hbm, wx_hbm, wy_hbm, out_ref, x, y, wx, wy, sems):
    at_core = lax.axis_index("tensor")
    rank = wx.shape[0]
    copies = []
    for src, w_src, dst, w_dst, row in ((y_hbm, wy_hbm, y, wy, 0), (x_hbm, wx_hbm, x, wx, rank)):
        depth = dst.shape[1]
        for at, size in chunks_of(depth):
            w_at = pl.multiple_of(at_core * depth + at, 128)
            here = pl.ds(at, size)
            sem = 2 * len(copies)
            pair = (
                pltpu.make_async_copy(w_src.at[:, pl.ds(w_at, size)], w_dst.at[:, here], sems.at[sem]),
                pltpu.make_async_copy(src.at[:, here], dst.at[:, here], sems.at[sem + 1]),
            )
            for copy in pair:
                copy.start()
            copies.append((pair, dst, w_dst, row, at, size))
    totals = {}
    for pair, dst, w_dst, row, at, size in copies:
        for copy in pair:
            copy.wait()
        part = dot(w_dst[:, at : at + size], dst[:, at : at + size], NT)
        totals[row] = totals[row] + part if row in totals else part
    out_ref[:rank, :] = totals[0]
    out_ref[rank:, :] = totals[rank]


def partial_codes(inputs, out_grads, proj_in_t, proj_out_t):
    tokens, depth_in = inputs.shape
    depth_out = out_grads.shape[1]
    rank = proj_in_t.shape[0]
    jobs = len(chunks_of(depth_in)) + len(chunks_of(depth_out))
    return pl.pallas_call(
        codes_kernel,
        out_shape=jax.ShapeDtypeStruct((2 * rank, tokens), jnp.float32),
        in_specs=[HBM] * 4,
        out_specs=VMEM,
        scratch_shapes=[
            pltpu.VMEM((tokens, depth_in), inputs.dtype),
            pltpu.VMEM((tokens, depth_out), out_grads.dtype),
            pltpu.VMEM((rank, depth_in), proj_in_t.dtype),
            pltpu.VMEM((rank, depth_out), proj_out_t.dtype),
            pltpu.SemaphoreType.DMA((2 * jobs,)),
        ],
        compiler_params=pltpu.CompilerParams(vmem_limit_bytes=56_000_000),
        name="partial_codes",
    )(inputs, out_grads, proj_in_t, proj_out_t)


def fixed_point(values):
    largest = jnp.max(jnp.abs(values), axis=0, keepdims=True)
    grade = jnp.ceil(jnp.log(jnp.maximum(largest, 1e-30)) * (STEPS / 0.6931471805599453) + 0.01)
    units = values * (TOP * jnp.exp2(grade * (-1.0 / STEPS)))
    units = jnp.clip(jnp.floor(units + 0.5), -TOP, TOP)
    return units.astype(jnp.int32), grade.astype(jnp.int32)


def pack_kernel(mine_ref, other_ref, ids_ref, own_ref, message_ref):
    rows, tokens = mine_ref.shape
    rank = rows // 2
    ids = ids_ref[...]
    onehot = members(ids, DOCS_DEV)
    count = jnp.maximum(jnp.sum(onehot, axis=1, keepdims=True), 1.0)
    weight = jnp.sum(onehot / jnp.sqrt(count), axis=0, keepdims=True)
    grads = mine_ref[:rank, :] + other_ref[:rank, :]
    ins = (mine_ref[rank:, :] + other_ref[rank:, :]) * weight
    own_ref[:rank, :] = grads
    own_ref[rank:, :] = ins
    grad_units, grad_grade = fixed_point(grads)
    in_units, in_grade = fixed_point(ins)
    message_ref[:rank, :] = lax.shift_left(grad_units, 16) | (in_units & 0xFFFF)
    line = lax.broadcasted_iota(jnp.int32, (EXTRA, tokens), 0)
    message_ref[rank:, :] = jnp.where(
        line == 0, ids, jnp.where(line == 1, grad_grade, in_grade)
    )


def pack(mine, other, doc_ids):
    rows, tokens = mine.shape
    rank = rows // 2
    return pl.pallas_call(
        pack_kernel,
        out_shape=(
            jax.ShapeDtypeStruct((rows, tokens), jnp.float32),
            jax.ShapeDtypeStruct((rank + EXTRA, tokens), jnp.int32),
        ),
        in_specs=[VMEM] * 3,
        out_specs=(VMEM, VMEM),
        compiler_params=SMALL,
        name="pack_codes",
    )(mine, other, doc_ids)


def scores_kernel(own_ref, message_ref, queries, scores_ref, grads_ref, ins_ref):
    rows, tokens = own_ref.shape
    rank = rows // 2
    grads = own_ref[:rank, :]
    ins = own_ref[rank:, :]
    onehot = members(message_ref[rank : rank + 1, :], DOCS_DEV)
    for values, ref in ((grads, grads_ref), (ins, ins_ref)):
        high, low = halves(values)
        stacked = jnp.concatenate([high, high, low, low], axis=0)
        ref[...] = stacked.T
    weighted = (grads[:, None, :] * onehot[None, :, :]).reshape(rank * DOCS_DEV, tokens)
    w_high, w_low = halves(weighted)
    i_high, i_low = halves(jnp.concatenate([ins, ins], axis=0))
    feats = dot(
        jnp.concatenate([w_high, w_high, w_low], axis=1),
        jnp.concatenate([i_high, i_low, i_high], axis=1),
        NT,
    )
    left = lax.broadcasted_iota(jnp.int32, (DOCS_DEV, 2 * rank), 1) < rank
    pairs = [
        jnp.where(
            left,
            feats[i * DOCS_DEV : (i + 1) * DOCS_DEV],
            feats[(i + 1) * DOCS_DEV : (i + 2) * DOCS_DEV],
        )
        for i in range(0, rank, 2)
    ]
    count = queries.shape[0]
    sums = [None] * count
    for n, pair in enumerate(pairs):
        block = queries[:, n * 2 * rank : (n + 1) * 2 * rank]
        for q in range(count):
            term = pair * block[q : q + 1, :]
            sums[q] = term if n == 0 else sums[q] + term
    columns = [jnp.sum(total, axis=1, keepdims=True) for total in sums]
    scores_ref[...] = jnp.concatenate(columns, axis=1) * (1.0 / rank)


def score_docs(own, message, queries):
    rows, tokens = own.shape
    rank = rows // 2
    operand = jax.ShapeDtypeStruct((tokens, 4 * rank), jnp.bfloat16)
    return pl.pallas_call(
        scores_kernel,
        out_shape=(
            jax.ShapeDtypeStruct((DOCS_DEV, queries.shape[0]), jnp.float32),
            operand,
            operand,
        ),
        in_specs=[VMEM] * 3,
        out_specs=(VMEM, VMEM, VMEM),
        compiler_params=SMALL,
        cost_estimate=pl.CostEstimate(flops=1 << 26, bytes_accessed=1 << 19, transcendentals=0),
        name="score_docs",
    )(own, message, queries)


def partners(shards):
    half = shards // 2
    order = [*range(half // 2, 0, -1), *range(half - 1, half // 2, -1), 0]
    return [half ^ n for n in order], [1] + [n ^ (n >> 1) for n in range(1, half)]


def gram_kernel(message_ref, grads_ref, ins_ref, *refs):
    blocks, out_ref = refs[:-1], refs[-1]
    half = len(blocks)
    rank = message_ref.shape[0] - EXTRA
    shard, core = lax.axis_index("dp"), lax.axis_index("tensor")
    own_half = lax.div(shard, half) == core
    onehot = members(message_ref[rank : rank + 1, :], DOCS_DEV).astype(jnp.bfloat16)
    doubled = jnp.concatenate([onehot, onehot], axis=1)
    far, near = partners(2 * half)
    total = None
    width = min(4, half)
    for first in range(0, half, width):
        codes, ids, scales = [], [], []
        for n in range(first, first + width):
            block, change = blocks[n][...], near[n]
            if n == 0:
                block, change = jnp.where(own_half, message_ref[...], block), 0
            place = lax.rem(lax.bitwise_xor(shard, jnp.where(own_half, change, far[n])), half)
            codes.append(block[:rank, :])
            ids.append(block[rank : rank + 1, :] + place * DOCS_DEV)
            scales.append((block[rank + 1 : rank + 2, :] + block[rank + 2 : rank + 3, :]).astype(jnp.float32))
        codes, ids, scales = (jnp.concatenate(part, axis=1) for part in (codes, ids, scales))
        product = None
        for units, left in (
            (lax.shift_right_arithmetic(codes, 16), grads_ref),
            (lax.shift_right_arithmetic(lax.shift_left(codes, 16), 16), ins_ref),
        ):
            high, low = halves(units.astype(jnp.float32))
            part = dot(left[...], jnp.concatenate([high, low, high, low], axis=0), NN)
            product = part if product is None else product * part
        high, low = halves(product)
        by_doc = dot(doubled, jnp.concatenate([high, low], axis=0), NN)
        by_doc = by_doc * (jnp.exp2(scales * (1.0 / STEPS)) * (1.0 / (TOP * TOP)))
        high, low = halves(by_doc)
        theirs = members(ids, half * DOCS_DEV).astype(jnp.bfloat16)
        part = dot(jnp.concatenate([high, low], axis=0), theirs, NT)
        total = part if total is None else total + part
    out_ref[...] = (total[:DOCS_DEV, :] + total[DOCS_DEV:, :]) * (1.0 / (rank * rank))


def gram_of(message, grads, ins, blocks):
    return pl.pallas_call(
        gram_kernel,
        out_shape=jax.ShapeDtypeStruct((DOCS_DEV, len(blocks) * DOCS_DEV), jnp.float32),
        in_specs=[VMEM] * (3 + len(blocks)),
        out_specs=VMEM,
        compiler_params=SMALL,
        name="gram_rows",
    )(message, grads, ins, *blocks)


def local(inputs, out_grads, proj_in, proj_out, doc_ids, queries):
    shards = lax.axis_size("dp")
    half = shards // 2
    mine = partial_codes(inputs, out_grads, proj_in.T, proj_out.T)
    other = lax.ppermute(mine, "tensor", [(0, 1), (1, 0)])
    own, message = pack(mine, other, doc_ids)
    blocks = []
    for far, near in zip(*partners(shards)):
        moves = []
        for s in range(shards):
            core = s // half
            moves.append((2 * s + core, 2 * (s ^ near) + core))
            moves.append((2 * s + 1 - core, 2 * (s ^ far) + core))
        blocks.append(lax.ppermute(message, ("dp", "tensor"), moves))
    scores, grads, ins = score_docs(own, message, queries)
    return gram_of(message, grads, ins, blocks), scores


def solution(mesh):
    return jax.shard_map(
        local,
        mesh=mesh,
        in_specs=(
            P(("groups", "dp"), "tensor"),
            P(("groups", "dp"), "tensor"),
            P(),
            P(),
            P(("groups", "dp"), None),
            P(),
        ),
        out_specs=(P(("groups", "dp"), "tensor"), P(("groups", "dp"), None)),
        check_vma=False,
    )
```

```python
import functools

import jax
import jax.numpy as jnp
from jax import lax
from jax.experimental import pallas as pl
from jax.experimental.pallas import tpu as pltpu
from jax.sharding import PartitionSpec as P

DOCS_DEV = 8
EXTRA = 8
STEPS = 8.0
TOP = 32767.0
NT = (((1,), (1,)), ((), ()))
NN = (((1,), (0,)), ((), ()))
VMEM = pl.BlockSpec(memory_space=pltpu.VMEM)
HBM = pl.BlockSpec(memory_space=pltpu.HBM)
SMALL = pltpu.CompilerParams(vmem_limit_bytes=16 << 20)

dot = functools.partial(lax.dot_general, preferred_element_type=jnp.float32)


def chunks_of(depth):
    pieces, at = [], 0
    while at < depth:
        size = min(1024 if at == 0 and depth > 2048 else 2048, depth - at)
        pieces.append((at, size))
        at += size
    return pieces


def halves(values):
    high = values.astype(jnp.bfloat16)
    return high, (values - high.astype(jnp.float32)).astype(jnp.bfloat16)


def members(ids, docs):
    rows = lax.broadcasted_iota(jnp.int32, (docs, ids.shape[1]), 0)
    return (rows == ids).astype(jnp.float32)


def codes_kernel(x_hbm, y_hbm, wx_hbm, wy_hbm, out_ref, x, y, wx, wy, sems):
    at_core = lax.axis_index("tensor")
    rank = wx.shape[0]
    copies = []
    for src, w_src, dst, w_dst, row in ((x_hbm, wx_hbm, x, wx, rank), (y_hbm, wy_hbm, y, wy, 0)):
        depth = dst.shape[1]
        for at, size in chunks_of(depth):
            w_at = pl.multiple_of(at_core * depth + at, 128)
            here = pl.ds(at, size)
            sem = 2 * len(copies)
            pair = (
                pltpu.make_async_copy(w_src.at[:, pl.ds(w_at, size)], w_dst.at[:, here], sems.at[sem]),
                pltpu.make_async_copy(src.at[:, here], dst.at[:, here], sems.at[sem + 1]),
            )
            for copy in pair:
                copy.start()
            copies.append((pair, dst, w_dst, row, at, size))
    totals = {}
    for pair, dst, w_dst, row, at, size in copies:
        for copy in pair:
            copy.wait()
        cut = size // 2 if size % 256 == 0 else size
        for first in range(at, at + size, cut):
            part = dot(dst[:, first : first + cut], w_dst[:, first : first + cut], NT)
            totals[row] = totals[row] + part if row in totals else part
    out_ref[...] = jnp.concatenate([totals[0], totals[rank]], axis=1).T


def partial_codes(inputs, out_grads, proj_in_t, proj_out_t):
    tokens, depth_in = inputs.shape
    depth_out = out_grads.shape[1]
    rank = proj_in_t.shape[0]
    jobs = len(chunks_of(depth_in)) + len(chunks_of(depth_out))
    return pl.pallas_call(
        codes_kernel,
        out_shape=jax.ShapeDtypeStruct((2 * rank, tokens), jnp.float32),
        in_specs=[HBM] * 4,
        out_specs=VMEM,
        scratch_shapes=[
            pltpu.VMEM((tokens, depth_in), inputs.dtype),
            pltpu.VMEM((tokens, depth_out), out_grads.dtype),
            pltpu.VMEM((rank, depth_in), proj_in_t.dtype),
            pltpu.VMEM((rank, depth_out), proj_out_t.dtype),
            pltpu.SemaphoreType.DMA((2 * jobs,)),
        ],
        compiler_params=pltpu.CompilerParams(vmem_limit_bytes=56_000_000),
        name="partial_codes",
    )(inputs, out_grads, proj_in_t, proj_out_t)


def fixed_point(values):
    largest = jnp.max(jnp.abs(values), axis=0, keepdims=True)
    grade = jnp.ceil(jnp.log(jnp.maximum(largest, 1e-30)) * (STEPS / 0.6931471805599453) + 0.01)
    units = values * (TOP * jnp.exp2(grade * (-1.0 / STEPS)))
    units = jnp.clip(jnp.floor(units + 0.5), -TOP, TOP)
    return units.astype(jnp.int32), grade.astype(jnp.int32)


def pack_kernel(mine_ref, other_ref, ids_ref, own_ref, message_ref):
    rows, tokens = mine_ref.shape
    rank = rows // 2
    ids = ids_ref[...]
    onehot = members(ids, DOCS_DEV)
    count = jnp.maximum(jnp.sum(onehot, axis=1, keepdims=True), 1.0)
    weight = jnp.sum(onehot / jnp.sqrt(count), axis=0, keepdims=True)
    grads = mine_ref[:rank, :] + other_ref[:rank, :]
    ins = (mine_ref[rank:, :] + other_ref[rank:, :]) * weight
    own_ref[:rank, :] = grads
    own_ref[rank:, :] = ins
    grad_units, grad_grade = fixed_point(grads)
    in_units, in_grade = fixed_point(ins)
    message_ref[:rank, :] = lax.shift_left(grad_units, 16) | (in_units & 0xFFFF)
    line = lax.broadcasted_iota(jnp.int32, (EXTRA, tokens), 0)
    message_ref[rank:, :] = jnp.where(
        line == 0, ids, jnp.where(line == 1, grad_grade, in_grade)
    )


def pack(mine, other, doc_ids):
    rows, tokens = mine.shape
    rank = rows // 2
    return pl.pallas_call(
        pack_kernel,
        out_shape=(
            jax.ShapeDtypeStruct((rows, tokens), jnp.float32),
            jax.ShapeDtypeStruct((rank + EXTRA, tokens), jnp.int32),
        ),
        in_specs=[VMEM] * 3,
        out_specs=(VMEM, VMEM),
        compiler_params=SMALL,
        name="pack_codes",
    )(mine, other, doc_ids)


def scores_kernel(own_ref, message_ref, queries, scores_ref, grads_ref, ins_ref):
    rows, tokens = own_ref.shape
    rank = rows // 2
    grads = own_ref[:rank, :]
    ins = own_ref[rank:, :]
    onehot = members(message_ref[rank : rank + 1, :], DOCS_DEV)
    for values, ref in ((grads, grads_ref), (ins, ins_ref)):
        high, low = halves(values)
        stacked = jnp.concatenate([high, high, low, low], axis=0)
        ref[...] = stacked.T
    weighted = (grads[:, None, :] * onehot[None, :, :]).reshape(rank * DOCS_DEV, tokens)
    w_high, w_low = halves(weighted)
    i_high, i_low = halves(jnp.concatenate([ins, ins], axis=0))
    feats = dot(
        jnp.concatenate([w_high, w_high, w_low], axis=1),
        jnp.concatenate([i_high, i_low, i_high], axis=1),
        NT,
    )
    left = lax.broadcasted_iota(jnp.int32, (DOCS_DEV, 2 * rank), 1) < rank
    pairs = [
        jnp.where(
            left,
            feats[i * DOCS_DEV : (i + 1) * DOCS_DEV],
            feats[(i + 1) * DOCS_DEV : (i + 2) * DOCS_DEV],
        )
        for i in range(0, rank, 2)
    ]
    count = queries.shape[0]
    sums = [None] * count
    for n, pair in enumerate(pairs):
        block = queries[:, n * 2 * rank : (n + 1) * 2 * rank]
        for q in range(count):
            term = pair * block[q : q + 1, :]
            sums[q] = term if n == 0 else sums[q] + term
    columns = [jnp.sum(total, axis=1, keepdims=True) for total in sums]
    scores_ref[...] = jnp.concatenate(columns, axis=1) * (1.0 / rank)


def score_docs(own, message, queries):
    rows, tokens = own.shape
    rank = rows // 2
    operand = jax.ShapeDtypeStruct((tokens, 4 * rank), jnp.bfloat16)
    return pl.pallas_call(
        scores_kernel,
        out_shape=(
            jax.ShapeDtypeStruct((DOCS_DEV, queries.shape[0]), jnp.float32),
            operand,
            operand,
        ),
        in_specs=[VMEM] * 3,
        out_specs=(VMEM, VMEM, VMEM),
        compiler_params=SMALL,
        cost_estimate=pl.CostEstimate(flops=1 << 26, bytes_accessed=1 << 19, transcendentals=0),
        name="score_docs",
    )(own, message, queries)


def partners(shards):
    half = shards // 2
    order = [*range(half // 2, 0, -1), *range(half - 1, half // 2, -1), 0]
    return [half ^ n for n in order], [1] + [n ^ (n >> 1) for n in range(1, half)]


def gram_kernel(round_, half, message_ref, grads_ref, ins_ref, block_ref, *refs):
    sum_ref, out_ref = refs if round_ else (None, *refs)
    rank = message_ref.shape[0] - EXTRA
    shard, core = lax.axis_index("dp"), lax.axis_index("tensor")
    own_half = lax.div(shard, half) == core
    onehot = members(message_ref[rank : rank + 1, :], DOCS_DEV).astype(jnp.bfloat16)
    far, near = (changes[round_] for changes in partners(2 * half))
    block = block_ref[...]
    if round_ == 0:
        block, near = jnp.where(own_half, message_ref[...], block), 0
    place = lax.rem(lax.bitwise_xor(shard, jnp.where(own_half, near, far)), half)
    codes = block[:rank, :]
    grades = block[rank + 1 : rank + 2, :] + block[rank + 2 : rank + 3, :]
    scales = jnp.exp2(grades.astype(jnp.float32) * (1.0 / STEPS))
    theirs = members(block[rank : rank + 1, :] + place * DOCS_DEV, half * DOCS_DEV).astype(jnp.bfloat16)
    product = None
    for units, left in (
        (lax.shift_right_arithmetic(codes, 16), grads_ref),
        (lax.shift_right_arithmetic(lax.shift_left(codes, 16), 16), ins_ref),
    ):
        high, low = halves(units.astype(jnp.float32))
        part = dot(left[...], jnp.concatenate([high, low, high, low], axis=0), NN)
        product = part if product is None else product * part
    high, low = halves(product)
    by_doc = dot(jnp.concatenate([onehot, onehot], axis=1), jnp.concatenate([high, low], axis=0), NN)
    high, low = halves(by_doc * (scales * (1.0 / (TOP * TOP * rank * rank))))
    part = dot(jnp.concatenate([high, low], axis=0), theirs, NT)
    total = part[:DOCS_DEV, :] + part[DOCS_DEV:, :]
    out_ref[...] = total if sum_ref is None else sum_ref[...] + total


def gram_of(message, grads, ins, blocks):
    half = len(blocks)
    total = ()
    for round_, block in enumerate(blocks):
        total = (
            pl.pallas_call(
                functools.partial(gram_kernel, round_, half),
                out_shape=jax.ShapeDtypeStruct((DOCS_DEV, half * DOCS_DEV), jnp.float32),
                in_specs=[VMEM] * (4 + len(total)),
                out_specs=VMEM,
                compiler_params=SMALL,
                name="gram_block",
            )(message, grads, ins, block, *total),
        )
    return total[0]


def local(inputs, out_grads, proj_in, proj_out, doc_ids, queries):
    shards = lax.axis_size("dp")
    half = shards // 2
    mine = partial_codes(inputs, out_grads, proj_in.T, proj_out.T)
    other = lax.ppermute(mine, "tensor", [(0, 1), (1, 0)])
    own, message = pack(mine, other, doc_ids)
    blocks = []
    for far, near in zip(*partners(shards)):
        moves = []
        for s in range(shards):
            core = s // half
            moves.append((2 * s + core, 2 * (s ^ near) + core))
            moves.append((2 * s + 1 - core, 2 * (s ^ far) + core))
        blocks.append(lax.ppermute(message, ("dp", "tensor"), moves))
    scores, grads, ins = score_docs(own, message, queries)
    return gram_of(message, grads, ins, blocks), scores


def solution(mesh):
    return jax.shard_map(
        local,
        mesh=mesh,
        in_specs=(
            P(("groups", "dp"), "tensor"),
            P(("groups", "dp"), "tensor"),
            P(),
            P(),
            P(("groups", "dp"), None),
            P(),
        ),
        out_specs=(P(("groups", "dp"), "tensor"), P(("groups", "dp"), None)),
        check_vma=False,
    )
```

```python
import functools

import jax
import jax.numpy as jnp
from jax import lax
from jax.experimental import pallas as pl
from jax.experimental.pallas import tpu as pltpu
from jax.sharding import PartitionSpec as P

DOCS_DEV = 8
EXTRA = 8
STEPS = 8.0
TOP = 32767.0
NT = (((1,), (1,)), ((), ()))
NN = (((1,), (0,)), ((), ()))
VMEM = pl.BlockSpec(memory_space=pltpu.VMEM)
HBM = pl.BlockSpec(memory_space=pltpu.HBM)
SMALL = pltpu.CompilerParams(vmem_limit_bytes=16 << 20)

dot = functools.partial(lax.dot_general, preferred_element_type=jnp.float32)


def chunks_of(depth):
    pieces, at = [], 0
    while at < depth:
        size = min(1024 if at == 0 and depth > 2048 else 2048, depth - at)
        pieces.append((at, size))
        at += size
    return pieces


def sum_of(parts):
    while len(parts) > 1:
        parts = [sum(parts[n : n + 2]) for n in range(0, len(parts), 2)]
    return parts[0]


def halves(values):
    high = values.astype(jnp.bfloat16)
    return high, (values - high.astype(jnp.float32)).astype(jnp.bfloat16)


def members(ids, docs):
    rows = lax.broadcasted_iota(jnp.int32, (docs, ids.shape[1]), 0)
    return (rows == ids).astype(jnp.float32)


def codes_kernel(x_hbm, y_hbm, wx_hbm, wy_hbm, out_ref, x, y, wx, wy, sems):
    at_core = lax.axis_index("tensor")
    rank = wx.shape[0]
    copies = []
    for src, w_src, dst, w_dst, row in ((x_hbm, wx_hbm, x, wx, rank), (y_hbm, wy_hbm, y, wy, 0)):
        depth = dst.shape[1]
        for at, size in chunks_of(depth):
            w_at = pl.multiple_of(at_core * depth + at, 128)
            here = pl.ds(at, size)
            sem = 2 * len(copies)
            pair = (
                pltpu.make_async_copy(w_src.at[:, pl.ds(w_at, size)], w_dst.at[:, here], sems.at[sem]),
                pltpu.make_async_copy(src.at[:, here], dst.at[:, here], sems.at[sem + 1]),
            )
            for copy in pair:
                copy.start()
            copies.append((pair, dst, w_dst, row, at, size))
    totals = {}
    for pair, dst, w_dst, row, at, size in copies:
        for copy in pair:
            copy.wait()
        for first in range(at, at + size, 256):
            here = slice(first, min(first + 256, at + size))
            totals.setdefault(row, []).append(dot(dst[:, here], w_dst[:, here], NT))
    out_ref[...] = jnp.concatenate([sum_of(totals[0]), sum_of(totals[rank])], axis=1).T


def partial_codes(inputs, out_grads, proj_in_t, proj_out_t):
    tokens, depth_in = inputs.shape
    depth_out = out_grads.shape[1]
    rank = proj_in_t.shape[0]
    jobs = len(chunks_of(depth_in)) + len(chunks_of(depth_out))
    return pl.pallas_call(
        codes_kernel,
        out_shape=jax.ShapeDtypeStruct((2 * rank, tokens), jnp.float32),
        in_specs=[HBM] * 4,
        out_specs=VMEM,
        scratch_shapes=[
            pltpu.VMEM((tokens, depth_in), inputs.dtype),
            pltpu.VMEM((tokens, depth_out), out_grads.dtype),
            pltpu.VMEM((rank, depth_in), proj_in_t.dtype),
            pltpu.VMEM((rank, depth_out), proj_out_t.dtype),
            pltpu.SemaphoreType.DMA((2 * jobs,)),
        ],
        compiler_params=pltpu.CompilerParams(vmem_limit_bytes=56_000_000),
        name="partial_codes",
    )(inputs, out_grads, proj_in_t, proj_out_t)


def fixed_point(values):
    largest = jnp.max(jnp.abs(values), axis=0, keepdims=True)
    grade = jnp.ceil(jnp.log(jnp.maximum(largest, 1e-30)) * (STEPS / 0.6931471805599453) + 0.01)
    units = values * (TOP * jnp.exp2(grade * (-1.0 / STEPS)))
    units = jnp.clip(jnp.floor(units + 0.5), -TOP, TOP)
    return units.astype(jnp.int32), grade.astype(jnp.int32)


def pack_kernel(mine_ref, other_ref, ids_ref, own_ref, message_ref):
    rows, tokens = mine_ref.shape
    rank = rows // 2
    ids = ids_ref[...]
    onehot = members(ids, DOCS_DEV)
    count = jnp.maximum(jnp.sum(onehot, axis=1, keepdims=True), 1.0)
    weight = jnp.sum(onehot / jnp.sqrt(count), axis=0, keepdims=True)
    grads = mine_ref[:rank, :] + other_ref[:rank, :]
    ins = (mine_ref[rank:, :] + other_ref[rank:, :]) * weight
    own_ref[:rank, :] = grads
    own_ref[rank:, :] = ins
    grad_units, grad_grade = fixed_point(grads)
    in_units, in_grade = fixed_point(ins)
    message_ref[:rank, :] = lax.shift_left(grad_units, 16) | (in_units & 0xFFFF)
    line = lax.broadcasted_iota(jnp.int32, (EXTRA, tokens), 0)
    message_ref[rank:, :] = jnp.where(
        line == 0, ids, jnp.where(line == 1, grad_grade, in_grade)
    )


def pack(mine, other, doc_ids):
    rows, tokens = mine.shape
    rank = rows // 2
    return pl.pallas_call(
        pack_kernel,
        out_shape=(
            jax.ShapeDtypeStruct((rows, tokens), jnp.float32),
            jax.ShapeDtypeStruct((rank + EXTRA, tokens), jnp.int32),
        ),
        in_specs=[VMEM] * 3,
        out_specs=(VMEM, VMEM),
        compiler_params=SMALL,
        name="pack_codes",
    )(mine, other, doc_ids)


def scores_kernel(own_ref, message_ref, queries, _, scores_ref, grads_ref, ins_ref):
    rows, tokens = own_ref.shape
    rank = rows // 2
    grads = own_ref[:rank, :]
    ins = own_ref[rank:, :]
    onehot = members(message_ref[rank : rank + 1, :], DOCS_DEV)
    for values, ref in ((grads, grads_ref), (ins, ins_ref)):
        high, low = halves(values)
        stacked = jnp.concatenate([high, high, low, low], axis=0)
        ref[...] = stacked.T
    weighted = (grads[:, None, :] * onehot[None, :, :]).reshape(rank * DOCS_DEV, tokens)
    w_high, w_low = halves(weighted)
    i_high, i_low = halves(jnp.concatenate([ins, ins], axis=0))
    feats = dot(
        jnp.concatenate([w_high, w_high, w_low], axis=1),
        jnp.concatenate([i_high, i_low, i_high], axis=1),
        NT,
    )
    left = lax.broadcasted_iota(jnp.int32, (DOCS_DEV, 2 * rank), 1) < rank
    pairs = [
        jnp.where(
            left,
            feats[i * DOCS_DEV : (i + 1) * DOCS_DEV],
            feats[(i + 1) * DOCS_DEV : (i + 2) * DOCS_DEV],
        )
        for i in range(0, rank, 2)
    ]
    count = queries.shape[0]
    sums = [None] * count
    for n, pair in enumerate(pairs):
        block = queries[:, n * 2 * rank : (n + 1) * 2 * rank]
        for q in range(count):
            term = pair * block[q : q + 1, :]
            sums[q] = term if n == 0 else sums[q] + term
    columns = [jnp.sum(total, axis=1, keepdims=True) for total in sums]
    scores_ref[...] = jnp.concatenate(columns, axis=1) * (1.0 / rank)


def score_docs(own, message, queries, after):
    rows, tokens = own.shape
    rank = rows // 2
    operand = jax.ShapeDtypeStruct((tokens, 4 * rank), jnp.bfloat16)
    return pl.pallas_call(
        scores_kernel,
        out_shape=(
            jax.ShapeDtypeStruct((DOCS_DEV, queries.shape[0]), jnp.float32),
            operand,
            operand,
        ),
        in_specs=[VMEM] * 4,
        out_specs=(VMEM, VMEM, VMEM),
        compiler_params=SMALL,
        cost_estimate=pl.CostEstimate(flops=1 << 26, bytes_accessed=1 << 19, transcendentals=0),
        name="score_docs",
    )(own, message, queries, after)


def plan(shards):
    half = shards // 2
    if half == 4:
        return [(-1, 4, 2), (-1, 7, 1), (0, 2, 2), (0, 1, 1)]
    direct = [(-1, half + n, n) for n in range(0, half, 2)]
    return direct + [(n, 1, 1) for n in range(half // 2)]


def origins(shards):
    found = []
    for what, other, own in plan(shards):
        before = found[what] if what >= 0 else (0, 0)
        found.append((before[0] ^ other, before[1] ^ own))
    return found


def gram_kernel(round_, half, message_ref, grads_ref, ins_ref, block_ref, *refs):
    sum_ref, out_ref = refs if round_ else (None, *refs)
    rank = message_ref.shape[0] - EXTRA
    shard, core = lax.axis_index("dp"), lax.axis_index("tensor")
    own_half = lax.div(shard, half) == core
    onehot = members(message_ref[rank : rank + 1, :], DOCS_DEV).astype(jnp.bfloat16)
    far, near = origins(2 * half)[round_]
    block = block_ref[...]
    place = lax.rem(lax.bitwise_xor(shard, jnp.where(own_half, near, far)), half)
    codes = block[:rank, :]
    grades = block[rank + 1 : rank + 2, :] + block[rank + 2 : rank + 3, :]
    scales = jnp.exp2(grades.astype(jnp.float32) * (1.0 / STEPS))
    theirs = members(block[rank : rank + 1, :] + place * DOCS_DEV, half * DOCS_DEV).astype(jnp.bfloat16)
    product = None
    for units, left in (
        (lax.shift_right_arithmetic(codes, 16), grads_ref),
        (lax.shift_right_arithmetic(lax.shift_left(codes, 16), 16), ins_ref),
    ):
        high, low = halves(units.astype(jnp.float32))
        part = dot(left[...], jnp.concatenate([high, low, high, low], axis=0), NN)
        product = part if product is None else product * part
    high, low = halves(product)
    by_doc = dot(jnp.concatenate([onehot, onehot], axis=1), jnp.concatenate([high, low], axis=0), NN)
    high, low = halves(by_doc * (scales * (1.0 / (TOP * TOP * rank * rank))))
    part = dot(jnp.concatenate([high, low], axis=0), theirs, NT)
    total = part[:DOCS_DEV, :] + part[DOCS_DEV:, :]
    out_ref[...] = total if sum_ref is None else sum_ref[...] + total


def gram_of(message, grads, ins, blocks):
    half = len(blocks)
    total = ()
    for round_, block in enumerate(blocks):
        total = (
            pl.pallas_call(
                functools.partial(gram_kernel, round_, half),
                out_shape=jax.ShapeDtypeStruct((DOCS_DEV, half * DOCS_DEV), jnp.float32),
                in_specs=[VMEM] * (4 + len(total)),
                out_specs=VMEM,
                compiler_params=SMALL,
                name="gram_block",
            )(message, grads, ins, block, *total),
        )
    return total[0]


def local(inputs, out_grads, proj_in, proj_out, doc_ids, queries):
    shards = lax.axis_size("dp")
    half = shards // 2
    mine = partial_codes(inputs, out_grads, proj_in.T, proj_out.T)
    other = lax.ppermute(mine, "tensor", [(0, 1), (1, 0)])
    own, message = pack(mine, other, doc_ids)
    blocks = []
    for what, far, near in plan(shards):
        moves = []
        for s in range(shards):
            for core in range(2):
                to = s ^ (near if core == s // half else far)
                moves.append((2 * s + core, 2 * to + (core if s // half == to // half else 1 - core)))
        blocks.append(lax.ppermute(blocks[what] if what >= 0 else message, ("dp", "tensor"), moves))
    scores, grads, ins = score_docs(own, message, queries, blocks[0])
    return gram_of(message, grads, ins, blocks), scores


def solution(mesh):
    return jax.shard_map(
        local,
        mesh=mesh,
        in_specs=(
            P(("groups", "dp"), "tensor"),
            P(("groups", "dp"), "tensor"),
            P(),
            P(),
            P(("groups", "dp"), None),
            P(),
        ),
        out_specs=(P(("groups", "dp"), "tensor"), P(("groups", "dp"), None)),
        check_vma=False,
    )
```

```python
import functools

import jax
import jax.numpy as jnp
from jax import lax
from jax.experimental import pallas as pl
from jax.experimental.pallas import tpu as pltpu
from jax.sharding import PartitionSpec as P

DOCS_DEV = 8
EXTRA = 8
STEPS = 8.0
TOP = 32767.0
NT = (((1,), (1,)), ((), ()))
NN = (((1,), (0,)), ((), ()))
VMEM = pl.BlockSpec(memory_space=pltpu.VMEM)
HBM = pl.BlockSpec(memory_space=pltpu.HBM)
SMALL = pltpu.CompilerParams(vmem_limit_bytes=16 << 20)

dot = functools.partial(lax.dot_general, preferred_element_type=jnp.float32)


def pieces_of(depth):
    pieces, at = [], 0
    while at < depth:
        size = min(2048 if at else 1024, depth - at)
        pieces.append((at, size))
        at += size
    return pieces


def last_pieces_of(depth):
    pieces, at = [], 0
    while at < depth:
        size = min(max((depth - at) // 1024 * 512, 512), depth - at)
        pieces.append((at, size))
        at += size
    return pieces


def sum_of(parts):
    while len(parts) > 1:
        parts = [sum(parts[n : n + 2]) for n in range(0, len(parts), 2)]
    return parts[0]


def halves(values):
    high = values.astype(jnp.bfloat16)
    return high, (values - high.astype(jnp.float32)).astype(jnp.bfloat16)


def members(ids, docs):
    rows = lax.broadcasted_iota(jnp.int32, (docs, ids.shape[1]), 0)
    return (rows == ids).astype(jnp.float32)


def codes_kernel(x_hbm, y_hbm, wx_hbm, wy_hbm, out_ref, x, y, wx, wy, sems):
    at_core = lax.axis_index("tensor")
    rank = wx.shape[0]
    sent = []

    def fetch(src, dst):
        sent.append(pltpu.make_async_copy(src, dst, sems.at[len(sent)]))
        sent[-1].start()
        return sent[-1]

    def fetch_weights(src, dst, at, size):
        there = pl.multiple_of(at_core * dst.shape[1] + at, 128)
        return fetch(src.at[:, pl.ds(there, size)], dst.at[:, pl.ds(at, size)])

    jobs = []
    for src, w_src, dst, w_dst, row, pieces in (
        (x_hbm, wx_hbm, x, wx, rank, pieces_of(x.shape[1])),
        (y_hbm, wy_hbm, y, wy, 0, last_pieces_of(y.shape[1])),
    ):
        for n, (at, size) in enumerate(pieces):
            needed = []
            if n == 0 or (n == 1 and row):
                upto = dst.shape[1] if n or not row else size
                needed.append(fetch_weights(w_src, w_dst, at, upto - at))
            needed.append(fetch(src.at[:, pl.ds(at, size)], dst.at[:, pl.ds(at, size)]))
            jobs.append((needed, dst, w_dst, row, at, size))
    totals = {}
    for needed, dst, w_dst, row, at, size in jobs:
        for copy in needed:
            copy.wait()
        for first in range(at, at + size, 512):
            here = slice(first, min(first + 512, at + size))
            totals.setdefault(row, []).append(dot(dst[:, here], w_dst[:, here], NT))
    out_ref[...] = jnp.concatenate([sum_of(totals[0]), sum_of(totals[rank])], axis=1).T


def partial_codes(inputs, out_grads, proj_in_t, proj_out_t):
    tokens, depth_in = inputs.shape
    depth_out = out_grads.shape[1]
    rank = proj_in_t.shape[0]
    copies = len(pieces_of(depth_in)) + len(last_pieces_of(depth_out)) + 3
    return pl.pallas_call(
        codes_kernel,
        out_shape=jax.ShapeDtypeStruct((2 * rank, tokens), jnp.float32),
        in_specs=[HBM] * 4,
        out_specs=VMEM,
        scratch_shapes=[
            pltpu.VMEM((tokens, depth_in), inputs.dtype),
            pltpu.VMEM((tokens, depth_out), out_grads.dtype),
            pltpu.VMEM((rank, depth_in), proj_in_t.dtype),
            pltpu.VMEM((rank, depth_out), proj_out_t.dtype),
            pltpu.SemaphoreType.DMA((copies,)),
        ],
        compiler_params=pltpu.CompilerParams(vmem_limit_bytes=56_000_000),
        name="partial_codes",
    )(inputs, out_grads, proj_in_t, proj_out_t)


def fixed_point(values):
    largest = jnp.max(jnp.abs(values), axis=0, keepdims=True)
    grade = jnp.ceil(jnp.log(jnp.maximum(largest, 1e-30)) * (STEPS / 0.6931471805599453) + 0.01)
    units = values * (TOP * jnp.exp2(grade * (-1.0 / STEPS)))
    units = jnp.clip(jnp.floor(units + 0.5), -TOP, TOP)
    return units.astype(jnp.int32), grade.astype(jnp.int32)


def pack_kernel(mine_ref, other_ref, ids_ref, own_ref, message_ref):
    rows, tokens = mine_ref.shape
    rank = rows // 2
    ids = ids_ref[...]
    onehot = members(ids, DOCS_DEV)
    count = jnp.maximum(jnp.sum(onehot, axis=1, keepdims=True), 1.0)
    weight = jnp.sum(onehot / jnp.sqrt(count), axis=0, keepdims=True)
    grads = mine_ref[:rank, :] + other_ref[:rank, :]
    ins = (mine_ref[rank:, :] + other_ref[rank:, :]) * weight
    own_ref[:rank, :] = grads
    own_ref[rank:, :] = ins
    grad_units, grad_grade = fixed_point(grads)
    in_units, in_grade = fixed_point(ins)
    message_ref[:rank, :] = lax.shift_left(grad_units, 16) | (in_units & 0xFFFF)
    line = lax.broadcasted_iota(jnp.int32, (EXTRA, tokens), 0)
    message_ref[rank:, :] = jnp.where(
        line == 0, ids, jnp.where(line == 1, grad_grade, in_grade)
    )


def pack(mine, other, doc_ids):
    rows, tokens = mine.shape
    rank = rows // 2
    return pl.pallas_call(
        pack_kernel,
        out_shape=(
            jax.ShapeDtypeStruct((rows, tokens), jnp.float32),
            jax.ShapeDtypeStruct((rank + EXTRA, tokens), jnp.int32),
        ),
        in_specs=[VMEM] * 3,
        out_specs=(VMEM, VMEM),
        compiler_params=SMALL,
        name="pack_codes",
    )(mine, other, doc_ids)


def scores_kernel(own_ref, message_ref, queries, scores_ref, grads_ref, ins_ref):
    rows, tokens = own_ref.shape
    rank = rows // 2
    grads = own_ref[:rank, :]
    ins = own_ref[rank:, :]
    onehot = members(message_ref[rank : rank + 1, :], DOCS_DEV)
    for values, ref in ((grads, grads_ref), (ins, ins_ref)):
        high, low = halves(values)
        stacked = jnp.concatenate([high, high, low, low], axis=0)
        ref[...] = stacked.T
    weighted = (grads[:, None, :] * onehot[None, :, :]).reshape(rank * DOCS_DEV, tokens)
    w_high, w_low = halves(weighted)
    i_high, i_low = halves(jnp.concatenate([ins, ins], axis=0))
    feats = dot(
        jnp.concatenate([w_high, w_high, w_low], axis=1),
        jnp.concatenate([i_high, i_low, i_high], axis=1),
        NT,
    )
    left = lax.broadcasted_iota(jnp.int32, (DOCS_DEV, 2 * rank), 1) < rank
    pairs = [
        jnp.where(
            left,
            feats[i * DOCS_DEV : (i + 1) * DOCS_DEV],
            feats[(i + 1) * DOCS_DEV : (i + 2) * DOCS_DEV],
        )
        for i in range(0, rank, 2)
    ]
    count = queries.shape[0]
    sums = [None] * count
    for n, pair in enumerate(pairs):
        block = queries[:, n * 2 * rank : (n + 1) * 2 * rank]
        for q in range(count):
            term = pair * block[q : q + 1, :]
            sums[q] = term if n == 0 else sums[q] + term
    columns = [jnp.sum(total, axis=1, keepdims=True) for total in sums]
    scores_ref[...] = jnp.concatenate(columns, axis=1) * (1.0 / rank)


def score_docs(own, message, queries):
    rows, tokens = own.shape
    rank = rows // 2
    operand = jax.ShapeDtypeStruct((tokens, 4 * rank), jnp.bfloat16)
    return pl.pallas_call(
        scores_kernel,
        out_shape=(
            jax.ShapeDtypeStruct((DOCS_DEV, queries.shape[0]), jnp.float32),
            operand,
            operand,
        ),
        in_specs=[VMEM] * 3,
        out_specs=(VMEM, VMEM, VMEM),
        compiler_params=SMALL,
        cost_estimate=pl.CostEstimate(flops=1 << 26, bytes_accessed=1 << 19, transcendentals=0),
        name="score_docs",
    )(own, message, queries)


def plan(shards):
    half = shards // 2
    if half == 4:
        return [(-1, 4, 1), (-1, 7, 2), (0, 2, 2), (0, 1, 1)]
    direct = [(-1, half + n, n) for n in range(0, half, 2)]
    return direct + [(n, 1, 1) for n in range(half // 2)]


def origins(shards):
    found = []
    for what, other, own in plan(shards):
        before = found[what] if what >= 0 else (0, 0)
        found.append((before[0] ^ other, before[1] ^ own))
    return found


def gram_kernel(message_ref, grads_ref, ins_ref, scores_ref, *refs):
    blocks, (out_ref, scores_out_ref) = refs[:-2], refs[-2:]
    scores_out_ref[...] = scores_ref[...]
    half = len(blocks)
    rank = message_ref.shape[0] - EXTRA
    shard, core = lax.axis_index("dp"), lax.axis_index("tensor")
    own_half = lax.div(shard, half) == core
    onehot = members(message_ref[rank : rank + 1, :], DOCS_DEV).astype(jnp.bfloat16)
    doubled = jnp.concatenate([onehot, onehot], axis=1)
    found = origins(2 * half)
    total = None
    width = min(4, half)
    for first in range(0, half, width):
        codes, ids, scales = [], [], []
        for n in range(first, first + width):
            block, (far, near) = blocks[n][...], found[n]
            place = lax.rem(lax.bitwise_xor(shard, jnp.where(own_half, near, far)), half)
            codes.append(block[:rank, :])
            ids.append(block[rank : rank + 1, :] + place * DOCS_DEV)
            grades = block[rank + 1 : rank + 2, :] + block[rank + 2 : rank + 3, :]
            scales.append(grades.astype(jnp.float32))
        codes, ids, scales = (jnp.concatenate(part, axis=1) for part in (codes, ids, scales))
        product = None
        for units, left in (
            (lax.shift_right_arithmetic(codes, 16), grads_ref),
            (lax.shift_right_arithmetic(lax.shift_left(codes, 16), 16), ins_ref),
        ):
            high, low = halves(units.astype(jnp.float32))
            part = dot(left[...], jnp.concatenate([high, low, high, low], axis=0), NN)
            product = part if product is None else product * part
        high, low = halves(product)
        by_doc = dot(doubled, jnp.concatenate([high, low], axis=0), NN)
        by_doc = by_doc * (jnp.exp2(scales * (1.0 / STEPS)) * (1.0 / (TOP * TOP * rank * rank)))
        high, low = halves(by_doc)
        theirs = members(ids, half * DOCS_DEV).astype(jnp.bfloat16)
        part = dot(jnp.concatenate([high, low], axis=0), theirs, NT)
        total = part if total is None else total + part
    out_ref[...] = total[:DOCS_DEV, :] + total[DOCS_DEV:, :]


def gram_of(message, grads, ins, scores, blocks):
    half = len(blocks)
    return pl.pallas_call(
        gram_kernel,
        out_shape=(
            jax.ShapeDtypeStruct((DOCS_DEV, half * DOCS_DEV), jnp.float32),
            jax.ShapeDtypeStruct(scores.shape, scores.dtype),
        ),
        in_specs=[VMEM] * (4 + half),
        out_specs=(VMEM, VMEM),
        compiler_params=SMALL,
        name="gram_rows",
    )(message, grads, ins, scores, *blocks)


def local(inputs, out_grads, proj_in, proj_out, doc_ids, queries):
    shards = lax.axis_size("dp")
    half = shards // 2
    mine = partial_codes(inputs, out_grads, proj_in.T, proj_out.T)
    other = lax.ppermute(mine, "tensor", [(0, 1), (1, 0)])
    own, message = pack(mine, other, doc_ids)
    blocks = []
    for what, far, near in plan(shards):
        moves = []
        for s in range(shards):
            for core in range(2):
                to = s ^ (near if core == s // half else far)
                moves.append((2 * s + core, 2 * to + (core if s // half == to // half else 1 - core)))
        blocks.append(lax.ppermute(blocks[what] if what >= 0 else message, ("dp", "tensor"), moves))
    scores, grads, ins = score_docs(own, message, queries)
    return gram_of(message, grads, ins, scores, blocks)


def solution(mesh):
    return jax.shard_map(
        local,
        mesh=mesh,
        in_specs=(
            P(("groups", "dp"), "tensor"),
            P(("groups", "dp"), "tensor"),
            P(),
            P(),
            P(("groups", "dp"), None),
            P(),
        ),
        out_specs=(P(("groups", "dp"), "tensor"), P(("groups", "dp"), None)),
        check_vma=False,
    )
```

```python
import functools

import jax
import jax.numpy as jnp
from jax import lax
from jax.experimental import pallas as pl
from jax.experimental.pallas import tpu as pltpu
from jax.sharding import PartitionSpec as P

DOCS_DEV = 8
EXTRA = 8
STEPS = 8.0
TOP = 32767.0
NT = (((1,), (1,)), ((), ()))
NN = (((1,), (0,)), ((), ()))
VMEM = pl.BlockSpec(memory_space=pltpu.VMEM)
HBM = pl.BlockSpec(memory_space=pltpu.HBM)
SMALL = pltpu.CompilerParams(vmem_limit_bytes=16 << 20)

dot = functools.partial(lax.dot_general, preferred_element_type=jnp.float32)


def pieces_of(depth):
    size = next(size for size in (2048, 1792, 1024, 512, 256, 128, depth) if depth % size == 0)
    return [(at, size) for at in range(0, depth, size)]


def sum_of(parts):
    while len(parts) > 1:
        parts = [sum(parts[n : n + 2]) for n in range(0, len(parts), 2)]
    return parts[0]


def halves(values):
    high = values.astype(jnp.bfloat16)
    return high, (values - high.astype(jnp.float32)).astype(jnp.bfloat16)


def members(ids, docs):
    rows = lax.broadcasted_iota(jnp.int32, (docs, ids.shape[1]), 0)
    return (rows == ids).astype(jnp.float32)


def codes_kernel(x_hbm, y_hbm, wx_hbm, wy_hbm, out_ref, x, y, wx, wy, sems):
    at_core = lax.axis_index("tensor")
    rank = wx.shape[0]
    jobs = []
    for src, w_src, dst, w_dst, row in ((y_hbm, wy_hbm, y, wy, 0), (x_hbm, wx_hbm, x, wx, rank)):
        depth = dst.shape[1]
        for at, size in pieces_of(depth):
            there = pl.multiple_of(at_core * depth + at, 128)
            here = pl.ds(at, size)
            sem = 2 * len(jobs)
            copies = (
                pltpu.make_async_copy(w_src.at[:, pl.ds(there, size)], w_dst.at[:, here], sems.at[sem]),
                pltpu.make_async_copy(src.at[:, here], dst.at[:, here], sems.at[sem + 1]),
            )
            for copy in copies:
                copy.start()
            jobs.append((copies, dst, w_dst, row, at, size))
    totals = {}
    for copies, dst, w_dst, row, at, size in jobs:
        for copy in copies:
            copy.wait()
        for first in range(at, at + size, 256):
            here = slice(first, min(first + 256, at + size))
            totals.setdefault(row, []).append(dot(w_dst[:, here], dst[:, here], NT))
    for row, parts in totals.items():
        out_ref[row : row + rank, :] = sum_of(parts)


def partial_codes(inputs, out_grads, proj_in_t, proj_out_t):
    tokens, depth_in = inputs.shape
    depth_out = out_grads.shape[1]
    rank = proj_in_t.shape[0]
    copies = 2 * (len(pieces_of(depth_in)) + len(pieces_of(depth_out)))
    return pl.pallas_call(
        codes_kernel,
        out_shape=jax.ShapeDtypeStruct((2 * rank, tokens), jnp.float32),
        in_specs=[HBM] * 4,
        out_specs=VMEM,
        scratch_shapes=[
            pltpu.VMEM((tokens, depth_in), inputs.dtype),
            pltpu.VMEM((tokens, depth_out), out_grads.dtype),
            pltpu.VMEM((rank, depth_in), proj_in_t.dtype),
            pltpu.VMEM((rank, depth_out), proj_out_t.dtype),
            pltpu.SemaphoreType.DMA((copies,)),
        ],
        compiler_params=pltpu.CompilerParams(vmem_limit_bytes=56_000_000),
        name="partial_codes",
    )(inputs, out_grads, proj_in_t, proj_out_t)


def fixed_point(values):
    largest = jnp.max(jnp.abs(values), axis=0, keepdims=True)
    grade = jnp.ceil(jnp.log(jnp.maximum(largest, 1e-30)) * (STEPS / 0.6931471805599453) + 0.01)
    units = values * (TOP * jnp.exp2(grade * (-1.0 / STEPS)))
    units = jnp.clip(jnp.floor(units + 0.5), -TOP, TOP)
    return units.astype(jnp.int32), grade.astype(jnp.int32)


def pack_kernel(mine_ref, other_ref, ids_ref, own_ref, message_ref):
    rows, tokens = mine_ref.shape
    rank = rows // 2
    ids = ids_ref[...]
    onehot = members(ids, DOCS_DEV)
    count = jnp.maximum(jnp.sum(onehot, axis=1, keepdims=True), 1.0)
    weight = jnp.sum(onehot / jnp.sqrt(count), axis=0, keepdims=True)
    grads = mine_ref[:rank, :] + other_ref[:rank, :]
    ins = (mine_ref[rank:, :] + other_ref[rank:, :]) * weight
    own_ref[:rank, :] = grads
    own_ref[rank:, :] = ins
    grad_units, grad_grade = fixed_point(grads)
    in_units, in_grade = fixed_point(ins)
    message_ref[:rank, :] = lax.shift_left(grad_units, 16) | (in_units & 0xFFFF)
    line = lax.broadcasted_iota(jnp.int32, (EXTRA, tokens), 0)
    message_ref[rank:, :] = jnp.where(
        line == 0, ids, jnp.where(line == 1, grad_grade, in_grade)
    )


def pack(mine, other, doc_ids):
    rows, tokens = mine.shape
    rank = rows // 2
    return pl.pallas_call(
        pack_kernel,
        out_shape=(
            jax.ShapeDtypeStruct((rows, tokens), jnp.float32),
            jax.ShapeDtypeStruct((rank + EXTRA, tokens), jnp.int32),
        ),
        in_specs=[VMEM] * 3,
        out_specs=(VMEM, VMEM),
        compiler_params=SMALL,
        name="pack_codes",
    )(mine, other, doc_ids)


def scores_kernel(own_ref, message_ref, queries, scores_ref, grads_ref, ins_ref):
    rows, tokens = own_ref.shape
    rank = rows // 2
    grads = own_ref[:rank, :]
    ins = own_ref[rank:, :]
    onehot = members(message_ref[rank : rank + 1, :], DOCS_DEV)
    for values, ref in ((grads, grads_ref), (ins, ins_ref)):
        high, low = halves(values)
        stacked = jnp.concatenate([high, high, low, low], axis=0)
        ref[...] = stacked.T
    weighted = (grads[:, None, :] * onehot[None, :, :]).reshape(rank * DOCS_DEV, tokens)
    w_high, w_low = halves(weighted)
    i_high, i_low = halves(jnp.concatenate([ins, ins], axis=0))
    feats = dot(
        jnp.concatenate([w_high, w_high, w_low], axis=1),
        jnp.concatenate([i_high, i_low, i_high], axis=1),
        NT,
    )
    left = lax.broadcasted_iota(jnp.int32, (DOCS_DEV, 2 * rank), 1) < rank
    pairs = [
        jnp.where(
            left,
            feats[i * DOCS_DEV : (i + 1) * DOCS_DEV],
            feats[(i + 1) * DOCS_DEV : (i + 2) * DOCS_DEV],
        )
        for i in range(0, rank, 2)
    ]
    count = queries.shape[0]
    sums = [None] * count
    for n, pair in enumerate(pairs):
        block = queries[:, n * 2 * rank : (n + 1) * 2 * rank]
        for q in range(count):
            term = pair * block[q : q + 1, :]
            sums[q] = term if n == 0 else sums[q] + term
    columns = [jnp.sum(total, axis=1, keepdims=True) for total in sums]
    scores_ref[...] = jnp.concatenate(columns, axis=1) * (1.0 / rank)


def score_docs(own, message, queries):
    rows, tokens = own.shape
    rank = rows // 2
    operand = jax.ShapeDtypeStruct((tokens, 4 * rank), jnp.bfloat16)
    return pl.pallas_call(
        scores_kernel,
        out_shape=(
            jax.ShapeDtypeStruct((DOCS_DEV, queries.shape[0]), jnp.float32),
            operand,
            operand,
        ),
        in_specs=[VMEM] * 3,
        out_specs=(VMEM, VMEM, VMEM),
        compiler_params=SMALL,
        cost_estimate=pl.CostEstimate(flops=1 << 26, bytes_accessed=1 << 19, transcendentals=0),
        name="score_docs",
    )(own, message, queries)


def plan(shards):
    half = shards // 2
    if half == 4:
        return [(-1, 4, 1), (-1, 7, 2), (0, 2, 2), (0, 1, 0)]
    direct = [(-1, half + n, n) for n in range(0, half, 2)]
    return direct + [(n, 1, 1) for n in range(half // 2)]


def origins(shards):
    found = []
    for what, other, own in plan(shards):
        before = found[what] if what >= 0 else (0, 0)
        found.append((before[0] ^ other, before[1] ^ own))
    return found


def gram_kernel(message_ref, grads_ref, ins_ref, scores_ref, *refs):
    blocks, (out_ref, scores_out_ref) = refs[:-2], refs[-2:]
    scores_out_ref[...] = scores_ref[...]
    half = len(blocks)
    rank = message_ref.shape[0] - EXTRA
    shard, core = lax.axis_index("dp"), lax.axis_index("tensor")
    own_half = lax.div(shard, half) == core
    onehot = members(message_ref[rank : rank + 1, :], DOCS_DEV).astype(jnp.bfloat16)
    doubled = jnp.concatenate([onehot, onehot], axis=1)
    found = origins(2 * half)
    total = None
    width = min(4, half)
    for first in range(0, half, width):
        codes, ids, scales = [], [], []
        for n in range(first, first + width):
            block, (far, near) = blocks[n][...], found[n]
            if near in [own for _, own in found[:n]]:
                block, near = jnp.where(own_half, message_ref[...], block), 0
            place = lax.rem(lax.bitwise_xor(shard, jnp.where(own_half, near, far)), half)
            codes.append(block[:rank, :])
            ids.append(block[rank : rank + 1, :] + place * DOCS_DEV)
            grades = block[rank + 1 : rank + 2, :] + block[rank + 2 : rank + 3, :]
            scales.append(grades.astype(jnp.float32))
        codes, ids, scales = (jnp.concatenate(part, axis=1) for part in (codes, ids, scales))
        product = None
        for units, left in (
            (lax.shift_right_arithmetic(codes, 16), grads_ref),
            (lax.shift_right_arithmetic(lax.shift_left(codes, 16), 16), ins_ref),
        ):
            high, low = halves(units.astype(jnp.float32))
            part = dot(left[...], jnp.concatenate([high, low, high, low], axis=0), NN)
            product = part if product is None else product * part
        high, low = halves(product)
        by_doc = dot(doubled, jnp.concatenate([high, low], axis=0), NN)
        by_doc = by_doc * (jnp.exp2(scales * (1.0 / STEPS)) * (1.0 / (TOP * TOP * rank * rank)))
        high, low = halves(by_doc)
        theirs = members(ids, half * DOCS_DEV).astype(jnp.bfloat16)
        part = dot(jnp.concatenate([high, low], axis=0), theirs, NT)
        total = part if total is None else total + part
    out_ref[...] = total[:DOCS_DEV, :] + total[DOCS_DEV:, :]


def gram_of(message, grads, ins, scores, blocks):
    half = len(blocks)
    return pl.pallas_call(
        gram_kernel,
        out_shape=(
            jax.ShapeDtypeStruct((DOCS_DEV, half * DOCS_DEV), jnp.float32),
            jax.ShapeDtypeStruct(scores.shape, scores.dtype),
        ),
        in_specs=[VMEM] * (4 + half),
        out_specs=(VMEM, VMEM),
        compiler_params=SMALL,
        name="gram_rows",
    )(message, grads, ins, scores, *blocks)


def local(inputs, out_grads, proj_in, proj_out, doc_ids, queries):
    shards = lax.axis_size("dp")
    half = shards // 2
    mine = partial_codes(inputs, out_grads, proj_in.T, proj_out.T)
    other = lax.ppermute(mine, "tensor", [(0, 1), (1, 0)])
    own, message = pack(mine, other, doc_ids)
    blocks = []
    for what, far, near in plan(shards):
        moves = []
        for s in range(shards):
            for core in range(2):
                to = s ^ (near if core == s // half else far)
                moves.append((2 * s + core, 2 * to + (core if s // half == to // half else 1 - core)))
        blocks.append(lax.ppermute(blocks[what] if what >= 0 else message, ("dp", "tensor"), moves))
    scores, grads, ins = score_docs(own, message, queries)
    return gram_of(message, grads, ins, scores, blocks)


def solution(mesh):
    return jax.shard_map(
        local,
        mesh=mesh,
        in_specs=(
            P(("groups", "dp"), "tensor"),
            P(("groups", "dp"), "tensor"),
            P(),
            P(),
            P(("groups", "dp"), None),
            P(),
        ),
        out_specs=(P(("groups", "dp"), "tensor"), P(("groups", "dp"), None)),
        check_vma=False,
    )
```

```python
import functools

import jax
import jax.numpy as jnp
from jax import lax
from jax.experimental import pallas as pl
from jax.experimental.pallas import tpu as pltpu
from jax.sharding import PartitionSpec as P

DOCS_DEV = 8
EXTRA = 8
STEPS = 8.0
TOP = 32767.0
NT = (((1,), (1,)), ((), ()))
NN = (((1,), (0,)), ((), ()))
VMEM = pl.BlockSpec(memory_space=pltpu.VMEM)
HBM = pl.BlockSpec(memory_space=pltpu.HBM)
SMALL = pltpu.CompilerParams(vmem_limit_bytes=16 << 20)

dot = functools.partial(lax.dot_general, preferred_element_type=jnp.float32)


def pieces_of(depth):
    size = next(size for size in (2048, 1792, 1024, 512, 256, 128, depth) if depth % size == 0)
    return [(at, size) for at in range(0, depth, size)]


def sum_of(parts):
    while len(parts) > 1:
        parts = [sum(parts[n : n + 2]) for n in range(0, len(parts), 2)]
    return parts[0]


def halves(values):
    high = values.astype(jnp.bfloat16)
    return high, (values - high.astype(jnp.float32)).astype(jnp.bfloat16)


def members(ids, docs):
    rows = lax.broadcasted_iota(jnp.int32, (docs, ids.shape[1]), 0)
    return (rows == ids).astype(jnp.float32)


def codes_kernel(x_hbm, y_hbm, wx_hbm, wy_hbm, out_ref, x, y, wx, wy, sems):
    at_core = lax.axis_index("tensor")
    rank = wx.shape[0]
    jobs = []
    for src, w_src, dst, w_dst, row in ((y_hbm, wy_hbm, y, wy, 0), (x_hbm, wx_hbm, x, wx, rank)):
        depth = dst.shape[1]
        for at, size in pieces_of(depth):
            there = pl.multiple_of(at_core * depth + at, 128)
            here = pl.ds(at, size)
            sem = 2 * len(jobs)
            copies = (
                pltpu.make_async_copy(w_src.at[:, pl.ds(there, size)], w_dst.at[:, here], sems.at[sem]),
                pltpu.make_async_copy(src.at[:, here], dst.at[:, here], sems.at[sem + 1]),
            )
            for copy in copies:
                copy.start()
            jobs.append((copies, dst, w_dst, row, at, size))
    totals = {}
    for copies, dst, w_dst, row, at, size in jobs:
        for copy in copies:
            copy.wait()
        here = slice(at, at + size)
        totals.setdefault(row, []).append(dot(dst[:, here], w_dst[:, here], NT))
    out_ref[...] = jnp.concatenate([sum_of(totals[0]), sum_of(totals[rank])], axis=1).T


def partial_codes(inputs, out_grads, proj_in_t, proj_out_t):
    tokens, depth_in = inputs.shape
    depth_out = out_grads.shape[1]
    rank = proj_in_t.shape[0]
    copies = 2 * (len(pieces_of(depth_in)) + len(pieces_of(depth_out)))
    return pl.pallas_call(
        codes_kernel,
        out_shape=jax.ShapeDtypeStruct((2 * rank, tokens), jnp.float32),
        in_specs=[HBM] * 4,
        out_specs=VMEM,
        scratch_shapes=[
            pltpu.VMEM((tokens, depth_in), inputs.dtype),
            pltpu.VMEM((tokens, depth_out), out_grads.dtype),
            pltpu.VMEM((rank, depth_in), proj_in_t.dtype),
            pltpu.VMEM((rank, depth_out), proj_out_t.dtype),
            pltpu.SemaphoreType.DMA((copies,)),
        ],
        compiler_params=pltpu.CompilerParams(vmem_limit_bytes=56_000_000),
        name="partial_codes",
    )(inputs, out_grads, proj_in_t, proj_out_t)


def fixed_point(values):
    largest = jnp.max(jnp.abs(values), axis=0, keepdims=True)
    grade = jnp.ceil(jnp.log(jnp.maximum(largest, 1e-30)) * (STEPS / 0.6931471805599453) + 0.01)
    units = values * (TOP * jnp.exp2(grade * (-1.0 / STEPS)))
    units = jnp.clip(jnp.floor(units + 0.5), -TOP, TOP)
    return units.astype(jnp.int32), grade.astype(jnp.int32)


def pack_kernel(mine_ref, other_ref, ids_ref, own_ref, message_ref):
    rows, tokens = mine_ref.shape
    rank = rows // 2
    ids = ids_ref[...]
    onehot = members(ids, DOCS_DEV)
    count = jnp.maximum(jnp.sum(onehot, axis=1, keepdims=True), 1.0)
    weight = jnp.sum(onehot / jnp.sqrt(count), axis=0, keepdims=True)
    grads = mine_ref[:rank, :] + other_ref[:rank, :]
    ins = (mine_ref[rank:, :] + other_ref[rank:, :]) * weight
    own_ref[:rank, :] = grads
    own_ref[rank:, :] = ins
    grad_units, grad_grade = fixed_point(grads)
    in_units, in_grade = fixed_point(ins)
    message_ref[:rank, :] = lax.shift_left(grad_units, 16) | (in_units & 0xFFFF)
    line = lax.broadcasted_iota(jnp.int32, (EXTRA, tokens), 0)
    message_ref[rank:, :] = jnp.where(
        line == 0, ids, jnp.where(line == 1, grad_grade, in_grade)
    )


def pack(mine, other, doc_ids):
    rows, tokens = mine.shape
    rank = rows // 2
    return pl.pallas_call(
        pack_kernel,
        out_shape=(
            jax.ShapeDtypeStruct((rows, tokens), jnp.float32),
            jax.ShapeDtypeStruct((rank + EXTRA, tokens), jnp.int32),
        ),
        in_specs=[VMEM] * 3,
        out_specs=(VMEM, VMEM),
        compiler_params=SMALL,
        name="pack_codes",
    )(mine, other, doc_ids)


def scores_kernel(own_ref, message_ref, queries, scores_ref, grads_ref, ins_ref):
    rows, tokens = own_ref.shape
    rank = rows // 2
    grads = own_ref[:rank, :]
    ins = own_ref[rank:, :]
    onehot = members(message_ref[rank : rank + 1, :], DOCS_DEV)
    for values, ref in ((grads, grads_ref), (ins, ins_ref)):
        high, low = halves(values)
        stacked = jnp.concatenate([high, high, low, low], axis=0)
        ref[...] = stacked.T
    weighted = (grads[:, None, :] * onehot[None, :, :]).reshape(rank * DOCS_DEV, tokens)
    w_high, w_low = halves(weighted)
    i_high, i_low = halves(jnp.concatenate([ins, ins], axis=0))
    feats = dot(
        jnp.concatenate([w_high, w_high, w_low], axis=1),
        jnp.concatenate([i_high, i_low, i_high], axis=1),
        NT,
    )
    left = lax.broadcasted_iota(jnp.int32, (DOCS_DEV, 2 * rank), 1) < rank
    pairs = [
        jnp.where(
            left,
            feats[i * DOCS_DEV : (i + 1) * DOCS_DEV],
            feats[(i + 1) * DOCS_DEV : (i + 2) * DOCS_DEV],
        )
        for i in range(0, rank, 2)
    ]
    count = queries.shape[0]
    sums = [None] * count
    for n, pair in enumerate(pairs):
        block = queries[:, n * 2 * rank : (n + 1) * 2 * rank]
        for q in range(count):
            term = pair * block[q : q + 1, :]
            sums[q] = term if n == 0 else sums[q] + term
    columns = [jnp.sum(total, axis=1, keepdims=True) for total in sums]
    scores_ref[...] = jnp.concatenate(columns, axis=1) * (1.0 / rank)


def score_docs(own, message, queries):
    rows, tokens = own.shape
    rank = rows // 2
    operand = jax.ShapeDtypeStruct((tokens, 4 * rank), jnp.bfloat16)
    return pl.pallas_call(
        scores_kernel,
        out_shape=(
            jax.ShapeDtypeStruct((DOCS_DEV, queries.shape[0]), jnp.float32),
            operand,
            operand,
        ),
        in_specs=[VMEM] * 3,
        out_specs=(VMEM, VMEM, VMEM),
        compiler_params=SMALL,
        cost_estimate=pl.CostEstimate(flops=1 << 26, bytes_accessed=1 << 19, transcendentals=0),
        name="score_docs",
    )(own, message, queries)


def plan(shards):
    half = shards // 2
    if half == 4:
        return [(-1, 4, 1), (-1, 7, 2), (0, 2, 2), (0, 1, 0)]
    direct = [(-1, half + n, n + 1) for n in range(0, half, 2)]
    return direct + [(n, 1, 1) for n in range(half // 2)]


def origins(shards):
    found = []
    for what, other, own in plan(shards):
        before = found[what] if what >= 0 else (0, 0)
        found.append((before[0] ^ other, before[1] ^ own if own else 0))
    return found


def gram_kernel(message_ref, grads_ref, ins_ref, scores_ref, *refs):
    blocks, (out_ref, scores_out_ref) = refs[:-2], refs[-2:]
    scores_out_ref[...] = scores_ref[...]
    half = len(blocks)
    rank = message_ref.shape[0] - EXTRA
    shard, core = lax.axis_index("dp"), lax.axis_index("tensor")
    own_half = lax.div(shard, half) == core
    onehot = members(message_ref[rank : rank + 1, :], DOCS_DEV).astype(jnp.bfloat16)
    doubled = jnp.concatenate([onehot, onehot], axis=1)
    found = origins(2 * half)
    total = None
    width = min(4, half)
    for first in range(0, half, width):
        codes, ids, scales = [], [], []
        for n in range(first, first + width):
            block, (far, near) = blocks[n][...], found[n]
            if near == 0:
                block = jnp.where(own_half, message_ref[...], block)
            place = lax.rem(lax.bitwise_xor(shard, jnp.where(own_half, near, far)), half)
            codes.append(block[:rank, :])
            ids.append(block[rank : rank + 1, :] + place * DOCS_DEV)
            grades = block[rank + 1 : rank + 2, :] + block[rank + 2 : rank + 3, :]
            scales.append(grades.astype(jnp.float32))
        codes, ids, scales = (jnp.concatenate(part, axis=1) for part in (codes, ids, scales))
        product = None
        for units, left in (
            (lax.shift_right_arithmetic(codes, 16), grads_ref),
            (lax.shift_right_arithmetic(lax.shift_left(codes, 16), 16), ins_ref),
        ):
            high, low = halves(units.astype(jnp.float32))
            part = dot(left[...], jnp.concatenate([high, low, high, low], axis=0), NN)
            product = part if product is None else product * part
        high, low = halves(product)
        by_doc = dot(doubled, jnp.concatenate([high, low], axis=0), NN)
        by_doc = by_doc * (jnp.exp2(scales * (1.0 / STEPS)) * (1.0 / (TOP * TOP * rank * rank)))
        high, low = halves(by_doc)
        theirs = members(ids, half * DOCS_DEV).astype(jnp.bfloat16)
        part = dot(jnp.concatenate([high, low], axis=0), theirs, NT)
        total = part if total is None else total + part
    out_ref[...] = total[:DOCS_DEV, :] + total[DOCS_DEV:, :]


def gram_of(message, grads, ins, scores, blocks):
    half = len(blocks)
    return pl.pallas_call(
        gram_kernel,
        out_shape=(
            jax.ShapeDtypeStruct((DOCS_DEV, half * DOCS_DEV), jnp.float32),
            jax.ShapeDtypeStruct(scores.shape, scores.dtype),
        ),
        in_specs=[VMEM] * (4 + half),
        out_specs=(VMEM, VMEM),
        compiler_params=SMALL,
        name="gram_rows",
    )(message, grads, ins, scores, *blocks)


def local(inputs, out_grads, proj_in, proj_out, doc_ids, queries):
    shards = lax.axis_size("dp")
    half = shards // 2
    mine = partial_codes(inputs, out_grads, proj_in.T, proj_out.T)
    other = lax.ppermute(mine, "tensor", [(0, 1), (1, 0)])
    own, message = pack(mine, other, doc_ids)
    blocks = []
    groups = lax.axis_size("groups")
    for what, far, near in plan(shards):
        moves = []
        for group in range(groups):
            for s in range(shards):
                for core in range(2):
                    to = s ^ (near if core == s // half else far)
                    to_group = (group + 1) % groups if to == s else group
                    to_core = core if s // half == to // half else 1 - core
                    moves.append((2 * (shards * group + s) + core, 2 * (shards * to_group + to) + to_core))
        blocks.append(lax.ppermute(blocks[what] if what >= 0 else message, ("groups", "dp", "tensor"), moves))
    scores, grads, ins = score_docs(own, message, queries)
    return gram_of(message, grads, ins, scores, blocks)


def solution(mesh):
    return jax.shard_map(
        local,
        mesh=mesh,
        in_specs=(
            P(("groups", "dp"), "tensor"),
            P(("groups", "dp"), "tensor"),
            P(),
            P(),
            P(("groups", "dp"), None),
            P(),
        ),
        out_specs=(P(("groups", "dp"), "tensor"), P(("groups", "dp"), None)),
        check_vma=False,
    )
```

```python
import functools

import jax
import jax.numpy as jnp
from jax import lax
from jax.experimental import pallas as pl
from jax.experimental.pallas import tpu as pltpu
from jax.sharding import PartitionSpec as P

DOCS_DEV = 8
EXTRA = 8
STEPS = 8.0
TOP = 32767.0
NT = (((1,), (1,)), ((), ()))
NN = (((1,), (0,)), ((), ()))
VMEM = pl.BlockSpec(memory_space=pltpu.VMEM)
HBM = pl.BlockSpec(memory_space=pltpu.HBM)
SMALL = pltpu.CompilerParams(vmem_limit_bytes=16 << 20)

dot = functools.partial(lax.dot_general, preferred_element_type=jnp.float32)


def pieces_of(depth):
    size = next(size for size in (1792, 1024, 512, 256, 128, depth) if depth % size == 0)
    return [(at, size) for at in range(0, depth, size)]


def sum_of(parts):
    while len(parts) > 1:
        parts = [sum(parts[n : n + 2]) for n in range(0, len(parts), 2)]
    return parts[0]


def halves(values):
    high = values.astype(jnp.bfloat16)
    return high, (values - high.astype(jnp.float32)).astype(jnp.bfloat16)


def members(ids, docs):
    rows = lax.broadcasted_iota(jnp.int32, (docs, ids.shape[1]), 0)
    return (rows == ids).astype(jnp.float32)


def codes_kernel(x_hbm, y_hbm, wx_hbm, wy_hbm, out_ref, x, y, wx, wy, sems):
    at_core = lax.axis_index("tensor")
    rank = wx.shape[0]
    jobs = []
    for src, w_src, dst, w_dst, row in ((y_hbm, wy_hbm, y, wy, 0), (x_hbm, wx_hbm, x, wx, rank)):
        depth = dst.shape[1]
        for at, size in pieces_of(depth):
            there = pl.multiple_of(at_core * depth + at, 128)
            here = pl.ds(at, size)
            sem = 2 * len(jobs)
            copies = (
                pltpu.make_async_copy(w_src.at[:, pl.ds(there, size)], w_dst.at[:, here], sems.at[sem]),
                pltpu.make_async_copy(src.at[:, here], dst.at[:, here], sems.at[sem + 1]),
            )
            for copy in copies:
                copy.start()
            jobs.append((copies, dst, w_dst, row, at, size))
    totals = {}
    for copies, dst, w_dst, row, at, size in jobs:
        for copy in copies:
            copy.wait()
        here = slice(at, at + size)
        totals.setdefault(row, []).append(dot(w_dst[:, here], dst[:, here], NT))
    for row, parts in totals.items():
        out_ref[row : row + rank, :] = sum_of(parts)


def partial_codes(inputs, out_grads, proj_in_t, proj_out_t):
    tokens, depth_in = inputs.shape
    depth_out = out_grads.shape[1]
    rank = proj_in_t.shape[0]
    copies = 2 * (len(pieces_of(depth_in)) + len(pieces_of(depth_out)))
    return pl.pallas_call(
        codes_kernel,
        out_shape=jax.ShapeDtypeStruct((2 * rank, tokens), jnp.float32),
        in_specs=[HBM] * 4,
        out_specs=VMEM,
        scratch_shapes=[
            pltpu.VMEM((tokens, depth_in), inputs.dtype),
            pltpu.VMEM((tokens, depth_out), out_grads.dtype),
            pltpu.VMEM((rank, depth_in), proj_in_t.dtype),
            pltpu.VMEM((rank, depth_out), proj_out_t.dtype),
            pltpu.SemaphoreType.DMA((copies,)),
        ],
        compiler_params=pltpu.CompilerParams(vmem_limit_bytes=56_000_000),
        name="partial_codes",
    )(inputs, out_grads, proj_in_t, proj_out_t)


def fixed_point(values):
    largest = jnp.max(jnp.abs(values), axis=0, keepdims=True)
    grade = jnp.ceil(jnp.log(jnp.maximum(largest, 1e-30)) * (STEPS / 0.6931471805599453) + 0.01)
    units = values * (TOP * jnp.exp2(grade * (-1.0 / STEPS)))
    units = jnp.clip(jnp.floor(units + 0.5), -TOP, TOP)
    return units.astype(jnp.int32), grade.astype(jnp.int32)


def pack_kernel(mine_ref, other_ref, ids_ref, own_ref, message_ref):
    rows, tokens = mine_ref.shape
    rank = rows // 2
    ids = ids_ref[...]
    onehot = members(ids, DOCS_DEV)
    count = jnp.maximum(jnp.sum(onehot, axis=1, keepdims=True), 1.0)
    weight = jnp.sum(onehot / jnp.sqrt(count), axis=0, keepdims=True)
    grads = mine_ref[:rank, :] + other_ref[:rank, :]
    ins = (mine_ref[rank:, :] + other_ref[rank:, :]) * weight
    own_ref[:rank, :] = grads
    own_ref[rank:, :] = ins
    grad_units, grad_grade = fixed_point(grads)
    in_units, in_grade = fixed_point(ins)
    message_ref[:rank, :] = lax.shift_left(grad_units, 16) | (in_units & 0xFFFF)
    line = lax.broadcasted_iota(jnp.int32, (EXTRA, tokens), 0)
    message_ref[rank:, :] = jnp.where(
        line == 0, ids, jnp.where(line == 1, grad_grade, in_grade)
    )


def pack(mine, other, doc_ids):
    rows, tokens = mine.shape
    rank = rows // 2
    return pl.pallas_call(
        pack_kernel,
        out_shape=(
            jax.ShapeDtypeStruct((rows, tokens), jnp.float32),
            jax.ShapeDtypeStruct((rank + EXTRA, tokens), jnp.int32),
        ),
        in_specs=[VMEM] * 3,
        out_specs=(VMEM, VMEM),
        compiler_params=SMALL,
        name="pack_codes",
    )(mine, other, doc_ids)


def scores_kernel(own_ref, message_ref, queries, scores_ref, grads_ref, ins_ref):
    rows, tokens = own_ref.shape
    rank = rows // 2
    grads = own_ref[:rank, :]
    ins = own_ref[rank:, :]
    onehot = members(message_ref[rank : rank + 1, :], DOCS_DEV)
    for values, ref in ((grads, grads_ref), (ins, ins_ref)):
        high, low = halves(values)
        stacked = jnp.concatenate([high, high, low, low], axis=0)
        ref[...] = stacked.T
    weighted = (grads[:, None, :] * onehot[None, :, :]).reshape(rank * DOCS_DEV, tokens)
    w_high, w_low = halves(weighted)
    i_high, i_low = halves(jnp.concatenate([ins, ins], axis=0))
    feats = dot(
        jnp.concatenate([w_high, w_high, w_low], axis=1),
        jnp.concatenate([i_high, i_low, i_high], axis=1),
        NT,
    )
    left = lax.broadcasted_iota(jnp.int32, (DOCS_DEV, 2 * rank), 1) < rank
    pairs = [
        jnp.where(
            left,
            feats[i * DOCS_DEV : (i + 1) * DOCS_DEV],
            feats[(i + 1) * DOCS_DEV : (i + 2) * DOCS_DEV],
        )
        for i in range(0, rank, 2)
    ]
    count = queries.shape[0]
    sums = [None] * count
    for n, pair in enumerate(pairs):
        block = queries[:, n * 2 * rank : (n + 1) * 2 * rank]
        for q in range(count):
            term = pair * block[q : q + 1, :]
            sums[q] = term if n == 0 else sums[q] + term
    columns = [jnp.sum(total, axis=1, keepdims=True) for total in sums]
    scores_ref[...] = jnp.concatenate(columns, axis=1) * (1.0 / rank)


def score_docs(own, message, queries):
    rows, tokens = own.shape
    rank = rows // 2
    operand = jax.ShapeDtypeStruct((tokens, 4 * rank), jnp.bfloat16)
    return pl.pallas_call(
        scores_kernel,
        out_shape=(
            jax.ShapeDtypeStruct((DOCS_DEV, queries.shape[0]), jnp.float32),
            operand,
            operand,
        ),
        in_specs=[VMEM] * 3,
        out_specs=(VMEM, VMEM, VMEM),
        compiler_params=SMALL,
        cost_estimate=pl.CostEstimate(flops=1 << 26, bytes_accessed=1 << 19, transcendentals=0),
        name="score_docs",
    )(own, message, queries)


def plan(shards):
    half = shards // 2
    if half == 4:
        return [(-1, 4, 2), (-1, 7, 1), (0, 1, 0), (0, 2, 1)]
    direct = [(-1, half + n, n + 1) for n in range(0, half, 2)]
    return direct + [(n, 1, 1) for n in range(half // 2)]


def origins(shards):
    found = []
    for what, other, own in plan(shards):
        before = found[what] if what >= 0 else (0, 0)
        found.append((before[0] ^ other, before[1] ^ own if own else 0))
    return found


def gram_kernel(message_ref, grads_ref, ins_ref, scores_ref, *refs):
    blocks, (out_ref, scores_out_ref) = refs[:-2], refs[-2:]
    scores_out_ref[...] = scores_ref[...]
    half = len(blocks)
    rank = message_ref.shape[0] - EXTRA
    shard, core = lax.axis_index("dp"), lax.axis_index("tensor")
    own_half = lax.div(shard, half) == core
    onehot = members(message_ref[rank : rank + 1, :], DOCS_DEV).astype(jnp.bfloat16)
    doubled = jnp.concatenate([onehot, onehot], axis=1)
    found = origins(2 * half)
    total = None
    width = min(4, half)
    for first in range(0, half, width):
        codes, ids, scales = [], [], []
        for n in range(first, first + width):
            block, (far, near) = blocks[n][...], found[n]
            if near == 0:
                block = jnp.where(own_half, message_ref[...], block)
            place = lax.rem(lax.bitwise_xor(shard, jnp.where(own_half, near, far)), half)
            codes.append(block[:rank, :])
            ids.append(block[rank : rank + 1, :] + place * DOCS_DEV)
            grades = block[rank + 1 : rank + 2, :] + block[rank + 2 : rank + 3, :]
            scales.append(grades.astype(jnp.float32))
        codes, ids, scales = (jnp.concatenate(part, axis=1) for part in (codes, ids, scales))
        product = None
        for units, left in (
            (lax.shift_right_arithmetic(codes, 16), grads_ref),
            (lax.shift_right_arithmetic(lax.shift_left(codes, 16), 16), ins_ref),
        ):
            high, low = halves(units.astype(jnp.float32))
            part = dot(left[...], jnp.concatenate([high, low, high, low], axis=0), NN)
            product = part if product is None else product * part
        high, low = halves(product)
        by_doc = dot(doubled, jnp.concatenate([high, low], axis=0), NN)
        by_doc = by_doc * (jnp.exp2(scales * (1.0 / STEPS)) * (1.0 / (TOP * TOP * rank * rank)))
        high, low = halves(by_doc)
        theirs = members(ids, half * DOCS_DEV).astype(jnp.bfloat16)
        part = dot(jnp.concatenate([high, low], axis=0), theirs, NT)
        total = part if total is None else total + part
    out_ref[...] = total[:DOCS_DEV, :] + total[DOCS_DEV:, :]


def gram_of(message, grads, ins, scores, blocks):
    half = len(blocks)
    return pl.pallas_call(
        gram_kernel,
        out_shape=(
            jax.ShapeDtypeStruct((DOCS_DEV, half * DOCS_DEV), jnp.float32),
            jax.ShapeDtypeStruct(scores.shape, scores.dtype),
        ),
        in_specs=[VMEM] * (4 + half),
        out_specs=(VMEM, VMEM),
        compiler_params=SMALL,
        name="gram_rows",
    )(message, grads, ins, scores, *blocks)


def local(inputs, out_grads, proj_in, proj_out, doc_ids, queries):
    shards = lax.axis_size("dp")
    half = shards // 2
    mine = partial_codes(inputs, out_grads, proj_in.T, proj_out.T)
    other = lax.ppermute(mine, "tensor", [(0, 1), (1, 0)])
    own, message = pack(mine, other, doc_ids)
    blocks = []
    groups = lax.axis_size("groups")
    for what, far, near in plan(shards):
        moves = []
        for group in range(groups):
            for s in range(shards):
                side = s // half
                for core in range(2):
                    to = s ^ (near if core == side else far)
                    to_group = (group + 1) % groups if to == s else group
                    to_core = core if to // half == side else 1 - core
                    by = 1 - core if what < 0 and side == 1 else core
                    moves.append((2 * (shards * group + s) + by, 2 * (shards * to_group + to) + to_core))
        blocks.append(lax.ppermute(blocks[what] if what >= 0 else message, ("groups", "dp", "tensor"), moves))
    scores, grads, ins = score_docs(own, message, queries)
    return gram_of(message, grads, ins, scores, blocks)


def solution(mesh):
    return jax.shard_map(
        local,
        mesh=mesh,
        in_specs=(
            P(("groups", "dp"), "tensor"),
            P(("groups", "dp"), "tensor"),
            P(),
            P(),
            P(("groups", "dp"), None),
            P(),
        ),
        out_specs=(P(("groups", "dp"), "tensor"), P(("groups", "dp"), None)),
        check_vma=False,
    )
```

```python
import functools

import jax
import jax.numpy as jnp
from jax import lax
from jax.experimental import pallas as pl
from jax.experimental.pallas import tpu as pltpu
from jax.sharding import PartitionSpec as P

DOCS_DEV = 8
EXTRA = 8
STEPS = 8.0
TOP = 32767.0
NT = (((1,), (1,)), ((), ()))
NN = (((1,), (0,)), ((), ()))
VMEM = pl.BlockSpec(memory_space=pltpu.VMEM)
HBM = pl.BlockSpec(memory_space=pltpu.HBM)
SMALL = pltpu.CompilerParams(vmem_limit_bytes=16 << 20)

dot = functools.partial(lax.dot_general, preferred_element_type=jnp.float32)


def pieces_of(depth):
    size = next(size for size in (2048, 1792, 1024, 512, 256, 128, depth) if depth % size == 0)
    return [(at, size) for at in range(0, depth, size)]


def sum_of(parts):
    while len(parts) > 1:
        parts = [sum(parts[n : n + 2]) for n in range(0, len(parts), 2)]
    return parts[0]


def halves(values):
    high = values.astype(jnp.bfloat16)
    return high, (values - high.astype(jnp.float32)).astype(jnp.bfloat16)


def members(ids, docs):
    rows = lax.broadcasted_iota(jnp.int32, (docs, ids.shape[1]), 0)
    return (rows == ids).astype(jnp.float32)


def codes_kernel(x_hbm, y_hbm, wx_hbm, wy_hbm, out_ref, x, y, wx, wy, sems):
    at_core = lax.axis_index("tensor")
    rank = wx.shape[0]
    jobs = []
    for src, w_src, dst, w_dst, row in ((y_hbm, wy_hbm, y, wy, 0), (x_hbm, wx_hbm, x, wx, rank)):
        depth = dst.shape[1]
        for at, size in pieces_of(depth):
            there = pl.multiple_of(at_core * depth + at, 128)
            here = pl.ds(at, size)
            sem = 2 * len(jobs)
            copies = (
                pltpu.make_async_copy(w_src.at[:, pl.ds(there, size)], w_dst.at[:, here], sems.at[sem]),
                pltpu.make_async_copy(src.at[:, here], dst.at[:, here], sems.at[sem + 1]),
            )
            for copy in copies:
                copy.start()
            jobs.append((copies, dst, w_dst, row, at, size))
    totals = {}
    for copies, dst, w_dst, row, at, size in jobs:
        for copy in copies:
            copy.wait()
        here = slice(at, at + size)
        totals.setdefault(row, []).append(dot(w_dst[:, here], dst[:, here], NT))
    for row, parts in totals.items():
        out_ref[row : row + rank, :] = sum_of(parts)


def partial_codes(inputs, out_grads, proj_in_t, proj_out_t):
    tokens, depth_in = inputs.shape
    depth_out = out_grads.shape[1]
    rank = proj_in_t.shape[0]
    copies = 2 * (len(pieces_of(depth_in)) + len(pieces_of(depth_out)))
    return pl.pallas_call(
        codes_kernel,
        out_shape=jax.ShapeDtypeStruct((2 * rank, tokens), jnp.float32),
        in_specs=[HBM] * 4,
        out_specs=VMEM,
        scratch_shapes=[
            pltpu.VMEM((tokens, depth_in), inputs.dtype),
            pltpu.VMEM((tokens, depth_out), out_grads.dtype),
            pltpu.VMEM((rank, depth_in), proj_in_t.dtype),
            pltpu.VMEM((rank, depth_out), proj_out_t.dtype),
            pltpu.SemaphoreType.DMA((copies,)),
        ],
        compiler_params=pltpu.CompilerParams(vmem_limit_bytes=56_000_000),
        name="partial_codes",
    )(inputs, out_grads, proj_in_t, proj_out_t)


def fixed_point(values):
    largest = jnp.max(jnp.abs(values), axis=0, keepdims=True)
    grade = jnp.ceil(jnp.log(jnp.maximum(largest, 1e-30)) * (STEPS / 0.6931471805599453) + 0.01)
    units = values * (TOP * jnp.exp2(grade * (-1.0 / STEPS)))
    units = jnp.clip(jnp.floor(units + 0.5), -TOP, TOP)
    return units.astype(jnp.int32), grade.astype(jnp.int32)


def pack_kernel(mine_ref, other_ref, ids_ref, own_ref, message_ref):
    rows, tokens = mine_ref.shape
    rank = rows // 2
    ids = ids_ref[...]
    onehot = members(ids, DOCS_DEV)
    count = jnp.maximum(jnp.sum(onehot, axis=1, keepdims=True), 1.0)
    weight = jnp.sum(onehot / jnp.sqrt(count), axis=0, keepdims=True)
    grads = mine_ref[:rank, :] + other_ref[:rank, :]
    ins = (mine_ref[rank:, :] + other_ref[rank:, :]) * weight
    own_ref[:rank, :] = grads
    own_ref[rank:, :] = ins
    grad_units, grad_grade = fixed_point(grads)
    in_units, in_grade = fixed_point(ins)
    message_ref[:rank, :] = lax.shift_left(grad_units, 16) | (in_units & 0xFFFF)
    line = lax.broadcasted_iota(jnp.int32, (EXTRA, tokens), 0)
    message_ref[rank:, :] = jnp.where(
        line == 0, ids, jnp.where(line == 1, grad_grade, in_grade)
    )


def pack(mine, other, doc_ids):
    rows, tokens = mine.shape
    rank = rows // 2
    return pl.pallas_call(
        pack_kernel,
        out_shape=(
            jax.ShapeDtypeStruct((rows, tokens), jnp.float32),
            jax.ShapeDtypeStruct((rank + EXTRA, tokens), jnp.int32),
        ),
        in_specs=[VMEM] * 3,
        out_specs=(VMEM, VMEM),
        compiler_params=SMALL,
        name="pack_codes",
    )(mine, other, doc_ids)


def scores_kernel(own_ref, message_ref, queries, scores_ref, grads_ref, ins_ref):
    rows, tokens = own_ref.shape
    rank = rows // 2
    grads = own_ref[:rank, :]
    ins = own_ref[rank:, :]
    onehot = members(message_ref[rank : rank + 1, :], DOCS_DEV)
    for values, ref in ((grads, grads_ref), (ins, ins_ref)):
        high, low = halves(values)
        stacked = jnp.concatenate([high, high, low, low], axis=0)
        ref[...] = stacked.T
    weighted = (grads[:, None, :] * onehot[None, :, :]).reshape(rank * DOCS_DEV, tokens)
    w_high, w_low = halves(weighted)
    i_high, i_low = halves(jnp.concatenate([ins, ins], axis=0))
    feats = dot(
        jnp.concatenate([w_high, w_high, w_low], axis=1),
        jnp.concatenate([i_high, i_low, i_high], axis=1),
        NT,
    )
    left = lax.broadcasted_iota(jnp.int32, (DOCS_DEV, 2 * rank), 1) < rank
    pairs = [
        jnp.where(
            left,
            feats[i * DOCS_DEV : (i + 1) * DOCS_DEV],
            feats[(i + 1) * DOCS_DEV : (i + 2) * DOCS_DEV],
        )
        for i in range(0, rank, 2)
    ]
    count = queries.shape[0]
    sums = [None] * count
    for n, pair in enumerate(pairs):
        block = queries[:, n * 2 * rank : (n + 1) * 2 * rank]
        for q in range(count):
            term = pair * block[q : q + 1, :]
            sums[q] = term if n == 0 else sums[q] + term
    columns = [jnp.sum(total, axis=1, keepdims=True) for total in sums]
    scores_ref[...] = jnp.concatenate(columns, axis=1) * (1.0 / rank)


def score_docs(own, message, queries):
    rows, tokens = own.shape
    rank = rows // 2
    operand = jax.ShapeDtypeStruct((tokens, 4 * rank), jnp.bfloat16)
    return pl.pallas_call(
        scores_kernel,
        out_shape=(
            jax.ShapeDtypeStruct((DOCS_DEV, queries.shape[0]), jnp.float32),
            operand,
            operand,
        ),
        in_specs=[VMEM] * 3,
        out_specs=(VMEM, VMEM, VMEM),
        compiler_params=SMALL,
        cost_estimate=pl.CostEstimate(flops=1 << 26, bytes_accessed=1 << 19, transcendentals=0),
        name="score_docs",
    )(own, message, queries)


def plan(shards):
    half = shards // 2
    if half == 4:
        return [(-1, 4, 2, (0, 1)), (-1, 7, 1, (1,)), (0, 1, 1, ()), (0, 2, 0, ())]
    direct = [(-1, half + n, n + 1, ()) for n in range(0, half, 2)]
    return direct + [(n, 1, 1, ()) for n in range(half // 2)]


def origins(shards):
    found = []
    for what, other, own, _ in plan(shards):
        before = found[what] if what >= 0 else (0, 0)
        found.append((before[0] ^ other, before[1] ^ own if own else 0))
    return found


def gram_kernel(message_ref, grads_ref, ins_ref, scores_ref, *refs):
    blocks, (out_ref, scores_out_ref) = refs[:-2], refs[-2:]
    scores_out_ref[...] = scores_ref[...]
    half = len(blocks)
    rank = message_ref.shape[0] - EXTRA
    shard, core = lax.axis_index("dp"), lax.axis_index("tensor")
    own_half = lax.div(shard, half) == core
    onehot = members(message_ref[rank : rank + 1, :], DOCS_DEV).astype(jnp.bfloat16)
    doubled = jnp.concatenate([onehot, onehot], axis=1)
    found = origins(2 * half)
    total = None
    width = min(4, half)
    for first in range(0, half, width):
        codes, ids, scales = [], [], []
        for n in range(first, first + width):
            block, (far, near) = blocks[n][...], found[n]
            if near == 0:
                block = jnp.where(own_half, message_ref[...], block)
            place = lax.rem(lax.bitwise_xor(shard, jnp.where(own_half, near, far)), half)
            codes.append(block[:rank, :])
            ids.append(block[rank : rank + 1, :] + place * DOCS_DEV)
            grades = block[rank + 1 : rank + 2, :] + block[rank + 2 : rank + 3, :]
            scales.append(grades.astype(jnp.float32))
        codes, ids, scales = (jnp.concatenate(part, axis=1) for part in (codes, ids, scales))
        product = None
        for units, left in (
            (lax.shift_right_arithmetic(codes, 16), grads_ref),
            (lax.shift_right_arithmetic(lax.shift_left(codes, 16), 16), ins_ref),
        ):
            high, low = halves(units.astype(jnp.float32))
            part = dot(left[...], jnp.concatenate([high, low, high, low], axis=0), NN)
            product = part if product is None else product * part
        high, low = halves(product)
        by_doc = dot(doubled, jnp.concatenate([high, low], axis=0), NN)
        by_doc = by_doc * (jnp.exp2(scales * (1.0 / STEPS)) * (1.0 / (TOP * TOP * rank * rank)))
        high, low = halves(by_doc)
        theirs = members(ids, half * DOCS_DEV).astype(jnp.bfloat16)
        part = dot(jnp.concatenate([high, low], axis=0), theirs, NT)
        total = part if total is None else total + part
    out_ref[...] = total[:DOCS_DEV, :] + total[DOCS_DEV:, :]


def gram_of(message, grads, ins, scores, blocks):
    half = len(blocks)
    return pl.pallas_call(
        gram_kernel,
        out_shape=(
            jax.ShapeDtypeStruct((DOCS_DEV, half * DOCS_DEV), jnp.float32),
            jax.ShapeDtypeStruct(scores.shape, scores.dtype),
        ),
        in_specs=[VMEM] * (4 + half),
        out_specs=(VMEM, VMEM),
        compiler_params=SMALL,
        name="gram_rows",
    )(message, grads, ins, scores, *blocks)


def local(inputs, out_grads, proj_in, proj_out, doc_ids, queries):
    shards = lax.axis_size("dp")
    half = shards // 2
    mine = partial_codes(inputs, out_grads, proj_in.T, proj_out.T)
    other = lax.ppermute(mine, "tensor", [(0, 1), (1, 0)])
    own, message = pack(mine, other, doc_ids)
    blocks = []
    groups = lax.axis_size("groups")
    for what, far, near, crossed in plan(shards):
        moves = []
        for group in range(groups):
            for s in range(shards):
                side = s // half
                for core in range(2):
                    to = s ^ (near if core == side else far)
                    to_group = (group + 1) % groups if to == s else group
                    to_core = core if to // half == side else 1 - core
                    by = 1 - core if side in crossed else core
                    moves.append((2 * (shards * group + s) + by, 2 * (shards * to_group + to) + to_core))
        blocks.append(lax.ppermute(blocks[what] if what >= 0 else message, ("groups", "dp", "tensor"), moves))
    scores, grads, ins = score_docs(own, message, queries)
    return gram_of(message, grads, ins, scores, blocks)


def solution(mesh):
    return jax.shard_map(
        local,
        mesh=mesh,
        in_specs=(
            P(("groups", "dp"), "tensor"),
            P(("groups", "dp"), "tensor"),
            P(),
            P(),
            P(("groups", "dp"), None),
            P(),
        ),
        out_specs=(P(("groups", "dp"), "tensor"), P(("groups", "dp"), None)),
        check_vma=False,
    )
```

```python
import functools

import jax
import jax.numpy as jnp
from jax import lax
from jax.experimental import pallas as pl
from jax.experimental.pallas import tpu as pltpu
from jax.sharding import PartitionSpec as P

DOCS_DEV = 8
EXTRA = 8
STEPS = 8.0
TOP = 32767.0
NT = (((1,), (1,)), ((), ()))
NN = (((1,), (0,)), ((), ()))
VMEM = pl.BlockSpec(memory_space=pltpu.VMEM)
HBM = pl.BlockSpec(memory_space=pltpu.HBM)
SMALL = pltpu.CompilerParams(vmem_limit_bytes=16 << 20)

dot = functools.partial(lax.dot_general, preferred_element_type=jnp.float32)


def pieces_of(depth):
    size = next(size for size in (2048, 1792, 1024, 512, 256, 128, depth) if depth % size == 0)
    return [(at, size) for at in range(0, depth, size)]


def sum_of(parts):
    while len(parts) > 1:
        parts = [sum(parts[n : n + 2]) for n in range(0, len(parts), 2)]
    return parts[0]


def halves(values):
    high = values.astype(jnp.bfloat16)
    return high, (values - high.astype(jnp.float32)).astype(jnp.bfloat16)


def members(ids, docs):
    rows = lax.broadcasted_iota(jnp.int32, (docs, ids.shape[1]), 0)
    return (rows == ids).astype(jnp.float32)


def codes_kernel(x_hbm, y_hbm, wx_hbm, wy_hbm, out_ref, x, y, wx, wy, sems):
    at_core = lax.axis_index("tensor")
    rank = wx.shape[0]
    jobs = []
    for src, w_src, dst, w_dst, row in ((y_hbm, wy_hbm, y, wy, 0), (x_hbm, wx_hbm, x, wx, rank)):
        depth = dst.shape[1]
        for at, size in pieces_of(depth):
            there = pl.multiple_of(at_core * depth + at, 128)
            here = pl.ds(at, size)
            sem = 2 * len(jobs)
            copies = (
                pltpu.make_async_copy(w_src.at[:, pl.ds(there, size)], w_dst.at[:, here], sems.at[sem]),
                pltpu.make_async_copy(src.at[:, here], dst.at[:, here], sems.at[sem + 1]),
            )
            for copy in copies:
                copy.start()
            jobs.append((copies, dst, w_dst, row, at, size))
    totals = {}
    for copies, dst, w_dst, row, at, size in jobs:
        for copy in copies:
            copy.wait()
        here = slice(at, at + size)
        totals.setdefault(row, []).append(dot(w_dst[:, here], dst[:, here], NT))
    for row, parts in totals.items():
        out_ref[row : row + rank, :] = sum_of(parts)


def partial_codes(inputs, out_grads, proj_in_t, proj_out_t):
    tokens, depth_in = inputs.shape
    depth_out = out_grads.shape[1]
    rank = proj_in_t.shape[0]
    copies = 2 * (len(pieces_of(depth_in)) + len(pieces_of(depth_out)))
    return pl.pallas_call(
        codes_kernel,
        out_shape=jax.ShapeDtypeStruct((2 * rank, tokens), jnp.float32),
        in_specs=[HBM] * 4,
        out_specs=VMEM,
        scratch_shapes=[
            pltpu.VMEM((tokens, depth_in), inputs.dtype),
            pltpu.VMEM((tokens, depth_out), out_grads.dtype),
            pltpu.VMEM((rank, depth_in), proj_in_t.dtype),
            pltpu.VMEM((rank, depth_out), proj_out_t.dtype),
            pltpu.SemaphoreType.DMA((copies,)),
        ],
        compiler_params=pltpu.CompilerParams(vmem_limit_bytes=56_000_000),
        name="partial_codes",
    )(inputs, out_grads, proj_in_t, proj_out_t)


def fixed_point(values):
    largest = jnp.max(jnp.abs(values), axis=0, keepdims=True)
    grade = jnp.ceil(jnp.log(jnp.maximum(largest, 1e-30)) * (STEPS / 0.6931471805599453) + 0.01)
    units = values * (TOP * jnp.exp2(grade * (-1.0 / STEPS)))
    units = jnp.clip(jnp.floor(units + 0.5), -TOP, TOP)
    return units.astype(jnp.int32), grade.astype(jnp.int32)


def pack_kernel(mine_ref, other_ref, ids_ref, own_ref, message_ref):
    rows, tokens = mine_ref.shape
    rank = rows // 2
    ids = ids_ref[...]
    onehot = members(ids, DOCS_DEV)
    count = jnp.maximum(jnp.sum(onehot, axis=1, keepdims=True), 1.0)
    weight = jnp.sum(onehot / jnp.sqrt(count), axis=0, keepdims=True)
    grads = mine_ref[:rank, :] + other_ref[:rank, :]
    ins = (mine_ref[rank:, :] + other_ref[rank:, :]) * weight
    own_ref[:rank, :] = grads
    own_ref[rank:, :] = ins
    grad_units, grad_grade = fixed_point(grads)
    in_units, in_grade = fixed_point(ins)
    message_ref[:rank, :] = lax.shift_left(grad_units, 16) | (in_units & 0xFFFF)
    line = lax.broadcasted_iota(jnp.int32, (EXTRA, tokens), 0)
    message_ref[rank:, :] = jnp.where(
        line == 0, ids, jnp.where(line == 1, grad_grade, in_grade)
    )


def pack(mine, other, doc_ids):
    rows, tokens = mine.shape
    rank = rows // 2
    return pl.pallas_call(
        pack_kernel,
        out_shape=(
            jax.ShapeDtypeStruct((rows, tokens), jnp.float32),
            jax.ShapeDtypeStruct((rank + EXTRA, tokens), jnp.int32),
        ),
        in_specs=[VMEM] * 3,
        out_specs=(VMEM, VMEM),
        compiler_params=SMALL,
        name="pack_codes",
    )(mine, other, doc_ids)


def scores_kernel(own_ref, message_ref, queries, scores_ref, grads_ref, ins_ref):
    rows, tokens = own_ref.shape
    rank = rows // 2
    grads = own_ref[:rank, :]
    ins = own_ref[rank:, :]
    onehot = members(message_ref[rank : rank + 1, :], DOCS_DEV)
    for values, ref in ((grads, grads_ref), (ins, ins_ref)):
        high, low = halves(values)
        stacked = jnp.concatenate([high, high, low, low], axis=0)
        ref[...] = stacked.T
    weighted = (grads[:, None, :] * onehot[None, :, :]).reshape(rank * DOCS_DEV, tokens)
    w_high, w_low = halves(weighted)
    i_high, i_low = halves(jnp.concatenate([ins, ins], axis=0))
    feats = dot(
        jnp.concatenate([w_high, w_high, w_low], axis=1),
        jnp.concatenate([i_high, i_low, i_high], axis=1),
        NT,
    )
    left = lax.broadcasted_iota(jnp.int32, (DOCS_DEV, 2 * rank), 1) < rank
    pairs = [
        jnp.where(
            left,
            feats[i * DOCS_DEV : (i + 1) * DOCS_DEV],
            feats[(i + 1) * DOCS_DEV : (i + 2) * DOCS_DEV],
        )
        for i in range(0, rank, 2)
    ]
    count = queries.shape[0]
    sums = [None] * count
    for n, pair in enumerate(pairs):
        block = queries[:, n * 2 * rank : (n + 1) * 2 * rank]
        for q in range(count):
            term = pair * block[q : q + 1, :]
            sums[q] = term if n == 0 else sums[q] + term
    columns = [jnp.sum(total, axis=1, keepdims=True) for total in sums]
    scores_ref[...] = jnp.concatenate(columns, axis=1) * (1.0 / rank)


def score_docs(own, message, queries):
    rows, tokens = own.shape
    rank = rows // 2
    operand = jax.ShapeDtypeStruct((tokens, 4 * rank), jnp.bfloat16)
    return pl.pallas_call(
        scores_kernel,
        out_shape=(
            jax.ShapeDtypeStruct((DOCS_DEV, queries.shape[0]), jnp.float32),
            operand,
            operand,
        ),
        in_specs=[VMEM] * 3,
        out_specs=(VMEM, VMEM, VMEM),
        compiler_params=SMALL,
        cost_estimate=pl.CostEstimate(flops=1 << 26, bytes_accessed=1 << 19, transcendentals=0),
        name="score_docs",
    )(own, message, queries)


def plan(shards):
    half = shards // 2
    if half == 4:
        return [(-1, 4, 2, (1,)), (-1, 7, 1, (1,)), (0, 2, 1, ()), (0, 1, 0, ())]
    direct = [(-1, half + n, n + 1, ()) for n in range(0, half, 2)]
    return direct + [(n, 1, 1, ()) for n in reversed(range(half // 2))]


def origins(shards):
    found = []
    for what, other, own, _ in plan(shards):
        before = found[what] if what >= 0 else (0, 0)
        found.append((before[0] ^ other, before[1] ^ own if own else 0))
    return found


def gram_sum(half, message_ref, grads_ref, ins_ref, parts):
    rank = message_ref.shape[0] - EXTRA
    onehot = members(message_ref[rank : rank + 1, :], DOCS_DEV).astype(jnp.bfloat16)
    doubled = jnp.concatenate([onehot, onehot], axis=1)
    total = None
    for first in range(0, len(parts), 4):
        codes, ids, scales = [], [], []
        for block, place in parts[first : first + 4]:
            codes.append(block[:rank, :])
            ids.append(block[rank : rank + 1, :] + place * DOCS_DEV)
            grades = block[rank + 1 : rank + 2, :] + block[rank + 2 : rank + 3, :]
            scales.append(grades.astype(jnp.float32))
        codes, ids, scales = (jnp.concatenate(part, axis=1) for part in (codes, ids, scales))
        product = None
        for units, left in (
            (lax.shift_right_arithmetic(codes, 16), grads_ref),
            (lax.shift_right_arithmetic(lax.shift_left(codes, 16), 16), ins_ref),
        ):
            high, low = halves(units.astype(jnp.float32))
            part = dot(left[...], jnp.concatenate([high, low, high, low], axis=0), NN)
            product = part if product is None else product * part
        high, low = halves(product)
        by_doc = dot(doubled, jnp.concatenate([high, low], axis=0), NN)
        by_doc = by_doc * (jnp.exp2(scales * (1.0 / STEPS)) * (1.0 / (TOP * TOP * rank * rank)))
        high, low = halves(by_doc)
        theirs = members(ids, half * DOCS_DEV).astype(jnp.bfloat16)
        part = dot(jnp.concatenate([high, low], axis=0), theirs, NT)
        total = part if total is None else total + part
    return total[:DOCS_DEV, :] + total[DOCS_DEV:, :]


def place_of(shard, half, own_half, origin):
    far, near = origin
    return lax.rem(lax.bitwise_xor(shard, jnp.where(own_half, near, far)), half)


def gram_kernel(message_ref, grads_ref, ins_ref, scores_ref, *refs):
    blocks, (sum_ref, out_ref, scores_out_ref, sems) = refs[:-4], refs[-4:]
    scores_copy = pltpu.make_async_copy(scores_ref, scores_out_ref, sems.at[0])
    scores_copy.start()
    half = len(blocks) + 1
    shard, core = lax.axis_index("dp"), lax.axis_index("tensor")
    own_half = lax.div(shard, half) == core
    found = origins(2 * half)
    parts = [
        (block[...], place_of(shard, half, own_half, origin)) for block, origin in zip(blocks, found)
    ]
    parts.append((message_ref[...], jnp.where(own_half, lax.rem(shard, half), -half)))
    sum_ref[...] = gram_sum(half, message_ref, grads_ref, ins_ref, parts)

    @pl.when(own_half)
    def _():
        copy = pltpu.make_async_copy(sum_ref, out_ref, sems.at[1])
        copy.start()
        copy.wait()

    scores_copy.wait()


def last_kernel(half, message_ref, grads_ref, ins_ref, block_ref, sum_ref, _, out_ref, total, sem):
    shard, core = lax.axis_index("dp"), lax.axis_index("tensor")
    own_half = lax.div(shard, half) == core

    @pl.when(jnp.logical_not(own_half))
    def _():
        place = place_of(shard, half, own_half, origins(2 * half)[-1])
        parts = [(block_ref[...], place)]
        total[...] = sum_ref[...] + gram_sum(half, message_ref, grads_ref, ins_ref, parts)
        copy = pltpu.make_async_copy(total, out_ref, sem)
        copy.start()
        copy.wait()


def gram_of(message, grads, ins, scores, blocks):
    half = len(blocks)
    rows = jax.ShapeDtypeStruct((DOCS_DEV, half * DOCS_DEV), jnp.float32)
    so_far, gram, scores = pl.pallas_call(
        gram_kernel,
        out_shape=(rows, rows, jax.ShapeDtypeStruct(scores.shape, scores.dtype)),
        in_specs=[VMEM] * (3 + half),
        out_specs=(VMEM, HBM, HBM),
        scratch_shapes=[pltpu.SemaphoreType.DMA((2,))],
        compiler_params=SMALL,
        name="gram_rows",
    )(message, grads, ins, scores, *blocks[:-1])
    gram = pl.pallas_call(
        functools.partial(last_kernel, half),
        out_shape=rows,
        in_specs=[VMEM] * 5 + [HBM],
        out_specs=HBM,
        scratch_shapes=[pltpu.VMEM(rows.shape, rows.dtype), pltpu.SemaphoreType.DMA],
        input_output_aliases={5: 0},
        compiler_params=SMALL,
        name="gram_last",
    )(message, grads, ins, blocks[-1], so_far, gram)
    return gram, scores


def local(inputs, out_grads, proj_in, proj_out, doc_ids, queries):
    shards = lax.axis_size("dp")
    half = shards // 2
    mine = partial_codes(inputs, out_grads, proj_in.T, proj_out.T)
    other = lax.ppermute(mine, "tensor", [(0, 1), (1, 0)])
    own, message = pack(mine, other, doc_ids)
    blocks = []
    groups = lax.axis_size("groups")
    for what, far, near, crossed in plan(shards):
        moves = []
        for group in range(groups):
            for s in range(shards):
                side = s // half
                for core in range(2):
                    to = s ^ (near if core == side else far)
                    to_group = (group + 1) % groups if to == s else group
                    to_core = core if to // half == side else 1 - core
                    by = 1 - core if side in crossed else core
                    moves.append((2 * (shards * group + s) + by, 2 * (shards * to_group + to) + to_core))
        blocks.append(lax.ppermute(blocks[what] if what >= 0 else message, ("groups", "dp", "tensor"), moves))
    scores, grads, ins = score_docs(own, message, queries)
    return gram_of(message, grads, ins, scores, blocks)


def solution(mesh):
    return jax.shard_map(
        local,
        mesh=mesh,
        in_specs=(
            P(("groups", "dp"), "tensor"),
            P(("groups", "dp"), "tensor"),
            P(),
            P(),
            P(("groups", "dp"), None),
            P(),
        ),
        out_specs=(P(("groups", "dp"), "tensor"), P(("groups", "dp"), None)),
        check_vma=False,
    )
```

```python
import functools

import jax
import jax.numpy as jnp
from jax import lax
from jax.experimental import pallas as pl
from jax.experimental.pallas import tpu as pltpu
from jax.sharding import PartitionSpec as P

DOCS_DEV = 8
EXTRA = 8
STEPS = 8.0
TOP = 32767.0
NT = (((1,), (1,)), ((), ()))
NN = (((1,), (0,)), ((), ()))
VMEM = pl.BlockSpec(memory_space=pltpu.VMEM)
HBM = pl.BlockSpec(memory_space=pltpu.HBM)
SMALL = pltpu.CompilerParams(vmem_limit_bytes=16 << 20)

dot = functools.partial(lax.dot_general, preferred_element_type=jnp.float32)


def pieces_of(depth):
    size = next(size for size in (1792, 1024, 512, 256, 128, depth) if depth % size == 0)
    return [(at, size) for at in range(0, depth, size)]


def weights_of(depth):
    pieces = pieces_of(depth)
    return [
        (at, sum(size for _, size in pieces[n : n + 2])) if n % 2 == 0 else None
        for n, (at, _) in enumerate(pieces)
    ]


def sum_of(parts):
    while len(parts) > 1:
        parts = [sum(parts[n : n + 2]) for n in range(0, len(parts), 2)]
    return parts[0]


def halves(values):
    high = values.astype(jnp.bfloat16)
    return high, (values - high.astype(jnp.float32)).astype(jnp.bfloat16)


def members(ids, docs):
    rows = lax.broadcasted_iota(jnp.int32, (docs, ids.shape[1]), 0)
    return (rows == ids).astype(jnp.float32)


def codes_kernel(x_hbm, y_hbm, wx_hbm, wy_hbm, out_ref, x, y, wx, wy, sems):
    at_core = lax.axis_index("tensor")
    rank = wx.shape[0]
    jobs, sent = [], 0
    for src, w_src, dst, w_dst, row in ((y_hbm, wy_hbm, y, wy, 0), (x_hbm, wx_hbm, x, wx, rank)):
        depth = dst.shape[1]
        for (at, size), ahead in zip(pieces_of(depth), weights_of(depth)):
            copies = []
            if ahead:
                there = pl.multiple_of(at_core * depth + ahead[0], 128)
                copies.append((w_src.at[:, pl.ds(there, ahead[1])], w_dst.at[:, pl.ds(*ahead)]))
            copies.append((src.at[:, pl.ds(at, size)], dst.at[:, pl.ds(at, size)]))
            copies = [pltpu.make_async_copy(*ends, sems.at[sent + n]) for n, ends in enumerate(copies)]
            sent += len(copies)
            for copy in copies:
                copy.start()
            jobs.append((copies, dst, w_dst, row, at, size))
    totals = {}
    for copies, dst, w_dst, row, at, size in jobs:
        for copy in copies:
            copy.wait()
        here = slice(at, at + size)
        totals.setdefault(row, []).append(dot(w_dst[:, here], dst[:, here], NT))
    for row, parts in totals.items():
        out_ref[row : row + rank, :] = sum_of(parts)


def partial_codes(inputs, out_grads, proj_in_t, proj_out_t):
    tokens, depth_in = inputs.shape
    depth_out = out_grads.shape[1]
    rank = proj_in_t.shape[0]
    copies = 2 * (len(pieces_of(depth_in)) + len(pieces_of(depth_out)))
    return pl.pallas_call(
        codes_kernel,
        out_shape=jax.ShapeDtypeStruct((2 * rank, tokens), jnp.float32),
        in_specs=[HBM] * 4,
        out_specs=VMEM,
        scratch_shapes=[
            pltpu.VMEM((tokens, depth_in), inputs.dtype),
            pltpu.VMEM((tokens, depth_out), out_grads.dtype),
            pltpu.VMEM((rank, depth_in), proj_in_t.dtype),
            pltpu.VMEM((rank, depth_out), proj_out_t.dtype),
            pltpu.SemaphoreType.DMA((copies,)),
        ],
        compiler_params=pltpu.CompilerParams(vmem_limit_bytes=56_000_000),
        name="partial_codes",
    )(inputs, out_grads, proj_in_t, proj_out_t)


def fixed_point(values):
    largest = jnp.max(jnp.abs(values), axis=0, keepdims=True)
    grade = jnp.ceil(jnp.log(jnp.maximum(largest, 1e-30)) * (STEPS / 0.6931471805599453) + 0.01)
    units = values * (TOP * jnp.exp2(grade * (-1.0 / STEPS)))
    units = jnp.clip(jnp.floor(units + 0.5), -TOP, TOP)
    return units.astype(jnp.int32), grade.astype(jnp.int32)


def pack_kernel(mine_ref, other_ref, ids_ref, own_ref, message_ref):
    rows, tokens = mine_ref.shape
    rank = rows // 2
    ids = ids_ref[...]
    onehot = members(ids, DOCS_DEV)
    count = jnp.maximum(jnp.sum(onehot, axis=1, keepdims=True), 1.0)
    weight = jnp.sum(onehot / jnp.sqrt(count), axis=0, keepdims=True)
    grads = mine_ref[:rank, :] + other_ref[:rank, :]
    ins = (mine_ref[rank:, :] + other_ref[rank:, :]) * weight
    own_ref[:rank, :] = grads
    own_ref[rank:, :] = ins
    grad_units, grad_grade = fixed_point(grads)
    in_units, in_grade = fixed_point(ins)
    message_ref[:rank, :] = lax.shift_left(grad_units, 16) | (in_units & 0xFFFF)
    line = lax.broadcasted_iota(jnp.int32, (EXTRA, tokens), 0)
    message_ref[rank:, :] = jnp.where(
        line == 0, ids, jnp.where(line == 1, grad_grade, in_grade)
    )


def pack(mine, other, doc_ids):
    rows, tokens = mine.shape
    rank = rows // 2
    return pl.pallas_call(
        pack_kernel,
        out_shape=(
            jax.ShapeDtypeStruct((rows, tokens), jnp.float32),
            jax.ShapeDtypeStruct((rank + EXTRA, tokens), jnp.int32),
        ),
        in_specs=[VMEM] * 3,
        out_specs=(VMEM, VMEM),
        compiler_params=SMALL,
        name="pack_codes",
    )(mine, other, doc_ids)


def scores_kernel(own_ref, message_ref, queries, scores_ref, grads_ref, ins_ref):
    rows, tokens = own_ref.shape
    rank = rows // 2
    grads = own_ref[:rank, :]
    ins = own_ref[rank:, :]
    onehot = members(message_ref[rank : rank + 1, :], DOCS_DEV)
    for values, ref in ((grads, grads_ref), (ins, ins_ref)):
        high, low = halves(values)
        stacked = jnp.concatenate([high, high, low, low], axis=0)
        ref[...] = stacked.T
    weighted = (grads[:, None, :] * onehot[None, :, :]).reshape(rank * DOCS_DEV, tokens)
    w_high, w_low = halves(weighted)
    i_high, i_low = halves(jnp.concatenate([ins, ins], axis=0))
    feats = dot(
        jnp.concatenate([w_high, w_high, w_low], axis=1),
        jnp.concatenate([i_high, i_low, i_high], axis=1),
        NT,
    )
    left = lax.broadcasted_iota(jnp.int32, (DOCS_DEV, 2 * rank), 1) < rank
    pairs = [
        jnp.where(
            left,
            feats[i * DOCS_DEV : (i + 1) * DOCS_DEV],
            feats[(i + 1) * DOCS_DEV : (i + 2) * DOCS_DEV],
        )
        for i in range(0, rank, 2)
    ]
    count = queries.shape[0]
    sums = [None] * count
    for n, pair in enumerate(pairs):
        block = queries[:, n * 2 * rank : (n + 1) * 2 * rank]
        for q in range(count):
            term = pair * block[q : q + 1, :]
            sums[q] = term if n == 0 else sums[q] + term
    columns = [jnp.sum(total, axis=1, keepdims=True) for total in sums]
    scores_ref[...] = jnp.concatenate(columns, axis=1) * (1.0 / rank)


def score_docs(own, message, queries):
    rows, tokens = own.shape
    rank = rows // 2
    operand = jax.ShapeDtypeStruct((tokens, 4 * rank), jnp.bfloat16)
    return pl.pallas_call(
        scores_kernel,
        out_shape=(
            jax.ShapeDtypeStruct((DOCS_DEV, queries.shape[0]), jnp.float32),
            operand,
            operand,
        ),
        in_specs=[VMEM] * 3,
        out_specs=(VMEM, VMEM, VMEM),
        compiler_params=SMALL,
        cost_estimate=pl.CostEstimate(flops=1 << 26, bytes_accessed=1 << 19, transcendentals=0),
        name="score_docs",
    )(own, message, queries)


def plan(shards):
    half = shards // 2
    if half == 4:
        return [(-1, 4, 2, (1,)), (-1, 7, 1, (1,)), (0, 2, 1, ()), (0, 1, 0, ())]
    direct = [(-1, half + n, n + 1, ()) for n in range(0, half, 2)]
    return direct + [(n, 1, 1, ()) for n in reversed(range(half // 2))]


def origins(shards):
    found = []
    for what, other, own, _ in plan(shards):
        before = found[what] if what >= 0 else (0, 0)
        found.append((before[0] ^ other, before[1] ^ own if own else 0))
    return found


def gram_sum(half, message_ref, grads_ref, ins_ref, parts):
    rank = message_ref.shape[0] - EXTRA
    onehot = members(message_ref[rank : rank + 1, :], DOCS_DEV).astype(jnp.bfloat16)
    doubled = jnp.concatenate([onehot, onehot], axis=1)
    total = None
    for first in range(0, len(parts), 4):
        codes, ids, scales = [], [], []
        for block, place in parts[first : first + 4]:
            codes.append(block[:rank, :])
            ids.append(block[rank : rank + 1, :] + place * DOCS_DEV)
            grades = block[rank + 1 : rank + 2, :] + block[rank + 2 : rank + 3, :]
            scales.append(grades.astype(jnp.float32))
        codes, ids, scales = (jnp.concatenate(part, axis=1) for part in (codes, ids, scales))
        product = None
        for units, left in (
            (lax.shift_right_arithmetic(codes, 16), grads_ref),
            (lax.shift_right_arithmetic(lax.shift_left(codes, 16), 16), ins_ref),
        ):
            high, low = halves(units.astype(jnp.float32))
            part = dot(left[...], jnp.concatenate([high, low, high, low], axis=0), NN)
            product = part if product is None else product * part
        high, low = halves(product)
        by_doc = dot(doubled, jnp.concatenate([high, low], axis=0), NN)
        by_doc = by_doc * (jnp.exp2(scales * (1.0 / STEPS)) * (1.0 / (TOP * TOP * rank * rank)))
        high, low = halves(by_doc)
        theirs = members(ids, half * DOCS_DEV).astype(jnp.bfloat16)
        part = dot(jnp.concatenate([high, low], axis=0), theirs, NT)
        total = part if total is None else total + part
    return total[:DOCS_DEV, :] + total[DOCS_DEV:, :]


def place_of(shard, half, own_half, origin):
    far, near = origin
    return lax.rem(lax.bitwise_xor(shard, jnp.where(own_half, near, far)), half)


def blocks_at(shard, half, own_half, numbers, refs):
    parts = []
    for ref, n in zip(refs, numbers):
        far, near = origins(2 * half)[n]
        place = lax.rem(lax.bitwise_xor(shard, jnp.where(own_half, near, far)), half)
        parts.append((ref[...], place))
    return parts


def position(half):
    shard, core = lax.axis_index("dp"), lax.axis_index("tensor")
    return shard, lax.div(shard, half) == core


def early_kernel(half, numbers, message_ref, grads_ref, ins_ref, *refs):
    blocks, sum_ref = refs[:-1], refs[-1]
    shard, own_half = position(half)
    parts = blocks_at(shard, half, own_half, numbers, blocks)
    parts.append((message_ref[...], jnp.where(own_half, lax.rem(shard, half), -half)))
    sum_ref[...] = gram_sum(half, message_ref, grads_ref, ins_ref, parts)


def finish_kernel(half, numbers, on_own, message_ref, grads_ref, ins_ref, scores_ref, sum_ref, *refs):
    blocks, (out_ref, scores_out_ref, total, sems) = refs[: len(numbers)], refs[-4:]
    shard, own_half = position(half)

    @pl.when(own_half if on_own else jnp.logical_not(own_half))
    def _():
        scores_copy = pltpu.make_async_copy(scores_ref, scores_out_ref, sems.at[0])
        scores_copy.start()
        parts = blocks_at(shard, half, own_half, numbers, blocks)
        total[...] = sum_ref[...] + gram_sum(half, message_ref, grads_ref, ins_ref, parts)
        copy = pltpu.make_async_copy(total, out_ref, sems.at[1])
        copy.start()
        copy.wait()
        scores_copy.wait()


def gram_of(message, grads, ins, scores, blocks):
    half = len(blocks)
    rows = jax.ShapeDtypeStruct((DOCS_DEV, half * DOCS_DEV), jnp.float32)
    operands = (message, grads, ins)
    early, late = range(half - 3), [*range(half - 3, half)]
    so_far = pl.pallas_call(
        functools.partial(early_kernel, half, early),
        out_shape=rows,
        in_specs=[VMEM] * (3 + len(early)),
        out_specs=VMEM,
        compiler_params=SMALL,
        name="gram_early",
    )(*operands, *(blocks[n] for n in early))
    results = ()
    for on_own, numbers in ((True, late[:-1]), (False, late)):
        first = 5 + len(numbers)
        results = pl.pallas_call(
            functools.partial(finish_kernel, half, numbers, on_own),
            out_shape=(rows, jax.ShapeDtypeStruct(scores.shape, scores.dtype)),
            in_specs=[VMEM] * first + [HBM] * len(results),
            out_specs=(HBM, HBM),
            scratch_shapes=[pltpu.VMEM(rows.shape, rows.dtype), pltpu.SemaphoreType.DMA((2,))],
            input_output_aliases={first + n: n for n in range(len(results))},
            compiler_params=SMALL,
            name="gram_own" if on_own else "gram_other",
        )(*operands, scores, so_far, *(blocks[n] for n in numbers), *results)
    return results


def local(inputs, out_grads, proj_in, proj_out, doc_ids, queries):
    shards = lax.axis_size("dp")
    half = shards // 2
    mine = partial_codes(inputs, out_grads, proj_in.T, proj_out.T)
    other = lax.ppermute(mine, "tensor", [(0, 1), (1, 0)])
    own, message = pack(mine, other, doc_ids)
    blocks = []
    groups = lax.axis_size("groups")
    for what, far, near, crossed in plan(shards):
        moves = []
        for group in range(groups):
            for s in range(shards):
                side = s // half
                for core in range(2):
                    to = s ^ (near if core == side else far)
                    to_group = (group + 1) % groups if to == s else group
                    to_core = core if to // half == side else 1 - core
                    by = 1 - core if side in crossed else core
                    moves.append((2 * (shards * group + s) + by, 2 * (shards * to_group + to) + to_core))
        blocks.append(lax.ppermute(blocks[what] if what >= 0 else message, ("groups", "dp", "tensor"), moves))
    scores, grads, ins = score_docs(own, message, queries)
    return gram_of(message, grads, ins, scores, blocks)


def solution(mesh):
    return jax.shard_map(
        local,
        mesh=mesh,
        in_specs=(
            P(("groups", "dp"), "tensor"),
            P(("groups", "dp"), "tensor"),
            P(),
            P(),
            P(("groups", "dp"), None),
            P(),
        ),
        out_specs=(P(("groups", "dp"), "tensor"), P(("groups", "dp"), None)),
        check_vma=False,
    )
```

```python
import functools

import jax
import jax.numpy as jnp
from jax import lax
from jax.experimental import pallas as pl
from jax.experimental.pallas import tpu as pltpu
from jax.sharding import PartitionSpec as P

DOCS_DEV = 8
EXTRA = 8
STEPS = 8.0
TOP = 32767.0
NT = (((1,), (1,)), ((), ()))
NN = (((1,), (0,)), ((), ()))
VMEM = pl.BlockSpec(memory_space=pltpu.VMEM)
HBM = pl.BlockSpec(memory_space=pltpu.HBM)
SMALL = pltpu.CompilerParams(vmem_limit_bytes=16 << 20)

dot = functools.partial(lax.dot_general, preferred_element_type=jnp.float32)


def pieces_of(depth):
    size = next(size for size in (2048, 1792, 1024, 512, 256, 128, depth) if depth % size == 0)
    return [(at, size) for at in range(0, depth, size)]


def sum_of(parts):
    while len(parts) > 1:
        parts = [sum(parts[n : n + 2]) for n in range(0, len(parts), 2)]
    return parts[0]


def halves(values):
    high = values.astype(jnp.bfloat16)
    return high, (values - high.astype(jnp.float32)).astype(jnp.bfloat16)


def members(ids, docs):
    rows = lax.broadcasted_iota(jnp.int32, (docs, ids.shape[1]), 0)
    return (rows == ids).astype(jnp.float32)


def codes_kernel(x_hbm, y_hbm, wx_hbm, wy_hbm, out_ref, x, y, wx, wy, sems):
    at_core = lax.axis_index("tensor")
    rank = wx.shape[0]
    jobs = []
    for src, w_src, dst, w_dst, row in ((y_hbm, wy_hbm, y, wy, 0), (x_hbm, wx_hbm, x, wx, rank)):
        depth = dst.shape[1]
        for at, size in pieces_of(depth):
            there = pl.multiple_of(at_core * depth + at, 128)
            here = pl.ds(at, size)
            sem = 2 * len(jobs)
            copies = (
                pltpu.make_async_copy(w_src.at[:, pl.ds(there, size)], w_dst.at[:, here], sems.at[sem]),
                pltpu.make_async_copy(src.at[:, here], dst.at[:, here], sems.at[sem + 1]),
            )
            for copy in copies:
                copy.start()
            jobs.append((copies, dst, w_dst, row, at, size))
    totals = {}
    for copies, dst, w_dst, row, at, size in jobs:
        for copy in copies:
            copy.wait()
        here = slice(at, at + size)
        totals.setdefault(row, []).append(dot(w_dst[:, here], dst[:, here], NT))
    for row, parts in totals.items():
        out_ref[row : row + rank, :] = sum_of(parts)


def partial_codes(inputs, out_grads, proj_in_t, proj_out_t):
    tokens, depth_in = inputs.shape
    depth_out = out_grads.shape[1]
    rank = proj_in_t.shape[0]
    copies = 2 * (len(pieces_of(depth_in)) + len(pieces_of(depth_out)))
    return pl.pallas_call(
        codes_kernel,
        out_shape=jax.ShapeDtypeStruct((2 * rank, tokens), jnp.float32),
        in_specs=[HBM] * 4,
        out_specs=VMEM,
        scratch_shapes=[
            pltpu.VMEM((tokens, depth_in), inputs.dtype),
            pltpu.VMEM((tokens, depth_out), out_grads.dtype),
            pltpu.VMEM((rank, depth_in), proj_in_t.dtype),
            pltpu.VMEM((rank, depth_out), proj_out_t.dtype),
            pltpu.SemaphoreType.DMA((copies,)),
        ],
        compiler_params=pltpu.CompilerParams(vmem_limit_bytes=56_000_000),
        name="partial_codes",
    )(inputs, out_grads, proj_in_t, proj_out_t)


def fixed_point(values):
    largest = jnp.max(jnp.abs(values), axis=0, keepdims=True)
    grade = jnp.ceil(jnp.log(jnp.maximum(largest, 1e-30)) * (STEPS / 0.6931471805599453) + 0.01)
    units = values * (TOP * jnp.exp2(grade * (-1.0 / STEPS)))
    units = jnp.clip(jnp.floor(units + 0.5), -TOP, TOP)
    return units.astype(jnp.int32), grade.astype(jnp.int32)


def pack_kernel(mine_ref, other_ref, ids_ref, own_ref, message_ref):
    rows, tokens = mine_ref.shape
    rank = rows // 2
    ids = ids_ref[...]
    onehot = members(ids, DOCS_DEV)
    count = jnp.maximum(jnp.sum(onehot, axis=1, keepdims=True), 1.0)
    weight = jnp.sum(onehot / jnp.sqrt(count), axis=0, keepdims=True)
    grads = mine_ref[:rank, :] + other_ref[:rank, :]
    ins = (mine_ref[rank:, :] + other_ref[rank:, :]) * weight
    own_ref[:rank, :] = grads
    own_ref[rank:, :] = ins
    grad_units, grad_grade = fixed_point(grads)
    in_units, in_grade = fixed_point(ins)
    message_ref[:rank, :] = lax.shift_left(grad_units, 16) | (in_units & 0xFFFF)
    line = lax.broadcasted_iota(jnp.int32, (EXTRA, tokens), 0)
    message_ref[rank:, :] = jnp.where(
        line == 0, ids, jnp.where(line == 1, grad_grade, in_grade)
    )


def pack(mine, other, doc_ids):
    rows, tokens = mine.shape
    rank = rows // 2
    return pl.pallas_call(
        pack_kernel,
        out_shape=(
            jax.ShapeDtypeStruct((rows, tokens), jnp.float32),
            jax.ShapeDtypeStruct((rank + EXTRA, tokens), jnp.int32),
        ),
        in_specs=[VMEM] * 3,
        out_specs=(VMEM, VMEM),
        compiler_params=SMALL,
        name="pack_codes",
    )(mine, other, doc_ids)


def scores_kernel(own_ref, message_ref, queries, scores_ref, grads_ref, ins_ref):
    rows, tokens = own_ref.shape
    rank = rows // 2
    grads = own_ref[:rank, :]
    ins = own_ref[rank:, :]
    onehot = members(message_ref[rank : rank + 1, :], DOCS_DEV)
    for values, ref in ((grads, grads_ref), (ins, ins_ref)):
        high, low = halves(values)
        stacked = jnp.concatenate([high, high, low, low], axis=0)
        ref[...] = stacked.T
    weighted = (grads[:, None, :] * onehot[None, :, :]).reshape(rank * DOCS_DEV, tokens)
    w_high, w_low = halves(weighted)
    i_high, i_low = halves(jnp.concatenate([ins, ins], axis=0))
    feats = dot(
        jnp.concatenate([w_high, w_high, w_low], axis=1),
        jnp.concatenate([i_high, i_low, i_high], axis=1),
        NT,
    )
    left = lax.broadcasted_iota(jnp.int32, (DOCS_DEV, 2 * rank), 1) < rank
    pairs = [
        jnp.where(
            left,
            feats[i * DOCS_DEV : (i + 1) * DOCS_DEV],
            feats[(i + 1) * DOCS_DEV : (i + 2) * DOCS_DEV],
        )
        for i in range(0, rank, 2)
    ]
    count = queries.shape[0]
    sums = [None] * count
    for n, pair in enumerate(pairs):
        block = queries[:, n * 2 * rank : (n + 1) * 2 * rank]
        for q in range(count):
            term = pair * block[q : q + 1, :]
            sums[q] = term if n == 0 else sums[q] + term
    columns = [jnp.sum(total, axis=1, keepdims=True) for total in sums]
    scores_ref[...] = jnp.concatenate(columns, axis=1) * (1.0 / rank)


def score_docs(own, message, queries):
    rows, tokens = own.shape
    rank = rows // 2
    operand = jax.ShapeDtypeStruct((tokens, 4 * rank), jnp.bfloat16)
    return pl.pallas_call(
        scores_kernel,
        out_shape=(
            jax.ShapeDtypeStruct((DOCS_DEV, queries.shape[0]), jnp.float32),
            operand,
            operand,
        ),
        in_specs=[VMEM] * 3,
        out_specs=(VMEM, VMEM, VMEM),
        compiler_params=SMALL,
        cost_estimate=pl.CostEstimate(flops=1 << 26, bytes_accessed=1 << 19, transcendentals=0),
        name="score_docs",
    )(own, message, queries)


def plan(shards):
    half = shards // 2
    if half == 4:
        return [
            (-1, (4, 4), (2, 1), (1,)),
            (-1, (7, 7), (1, 2), (1,)),
            (0, (2, 1), (1, 2), ()),
            (0, (1, 2), (2, 1), ()),
        ]
    direct = [(-1, (half + n,) * 2, (n + 1,) * 2, ()) for n in range(0, half, 2)]
    return direct + [(n, (1, 1), (1, 1), ()) for n in reversed(range(half // 2))]


def origins(shards):
    found = []
    for what, other, own, _ in plan(shards):
        before = found[what] if what >= 0 else ((0, 0), (0, 0))
        found.append([[a ^ b for a, b in zip(*pair)] for pair in zip(before, (other, own))])
    return found


def gram_sum(half, message_ref, grads_ref, ins_ref, parts):
    rank = message_ref.shape[0] - EXTRA
    onehot = members(message_ref[rank : rank + 1, :], DOCS_DEV).astype(jnp.bfloat16)
    doubled = jnp.concatenate([onehot, onehot], axis=1)
    total = None
    for first in range(0, len(parts), 4):
        codes, ids, scales = [], [], []
        for block, place in parts[first : first + 4]:
            codes.append(block[:rank, :])
            ids.append(block[rank : rank + 1, :] + place * DOCS_DEV)
            grades = block[rank + 1 : rank + 2, :] + block[rank + 2 : rank + 3, :]
            scales.append(grades.astype(jnp.float32))
        codes, ids, scales = (jnp.concatenate(part, axis=1) for part in (codes, ids, scales))
        product = None
        for units, left in (
            (lax.shift_right_arithmetic(codes, 16), grads_ref),
            (lax.shift_right_arithmetic(lax.shift_left(codes, 16), 16), ins_ref),
        ):
            high, low = halves(units.astype(jnp.float32))
            part = dot(left[...], jnp.concatenate([high, low, high, low], axis=0), NN)
            product = part if product is None else product * part
        high, low = halves(product)
        by_doc = dot(doubled, jnp.concatenate([high, low], axis=0), NN)
        by_doc = by_doc * (jnp.exp2(scales * (1.0 / STEPS)) * (1.0 / (TOP * TOP * rank * rank)))
        high, low = halves(by_doc)
        theirs = members(ids, half * DOCS_DEV).astype(jnp.bfloat16)
        part = dot(jnp.concatenate([high, low], axis=0), theirs, NT)
        total = part if total is None else total + part
    return total[:DOCS_DEV, :] + total[DOCS_DEV:, :]


def place_of(shard, half, own_half, origin):
    far, near = origin
    return lax.rem(lax.bitwise_xor(shard, jnp.where(own_half, near, far)), half)


def blocks_at(shard, half, own_half, numbers, refs):
    parts = []
    for ref, n in zip(refs, numbers):
        far, near = (jnp.where(shard < half, *bits) for bits in origins(2 * half)[n])
        place = lax.rem(lax.bitwise_xor(shard, jnp.where(own_half, near, far)), half)
        parts.append((ref[...], place))
    return parts


def position(half):
    shard, core = lax.axis_index("dp"), lax.axis_index("tensor")
    return shard, lax.div(shard, half) == core


def early_kernel(half, numbers, message_ref, grads_ref, ins_ref, *refs):
    blocks, sum_ref = refs[:-1], refs[-1]
    shard, own_half = position(half)
    parts = blocks_at(shard, half, own_half, numbers, blocks)
    parts.append((message_ref[...], jnp.where(own_half, lax.rem(shard, half), -half)))
    sum_ref[...] = gram_sum(half, message_ref, grads_ref, ins_ref, parts)


def finish_kernel(half, numbers, on_own, message_ref, grads_ref, ins_ref, scores_ref, sum_ref, *refs):
    blocks, (out_ref, scores_out_ref, total, sems) = refs[: len(numbers)], refs[-4:]
    shard, own_half = position(half)

    @pl.when(own_half if on_own else jnp.logical_not(own_half))
    def _():
        scores_copy = pltpu.make_async_copy(scores_ref, scores_out_ref, sems.at[0])
        scores_copy.start()
        parts = blocks_at(shard, half, own_half, numbers, blocks)
        total[...] = sum_ref[...] + gram_sum(half, message_ref, grads_ref, ins_ref, parts)
        copy = pltpu.make_async_copy(total, out_ref, sems.at[1])
        copy.start()
        copy.wait()
        scores_copy.wait()


def gram_of(message, grads, ins, scores, blocks):
    half = len(blocks)
    rows = jax.ShapeDtypeStruct((DOCS_DEV, half * DOCS_DEV), jnp.float32)
    operands = (message, grads, ins)
    early, late = range(half - 3), [*range(half - 3, half)]
    so_far = pl.pallas_call(
        functools.partial(early_kernel, half, early),
        out_shape=rows,
        in_specs=[VMEM] * (3 + len(early)),
        out_specs=VMEM,
        compiler_params=SMALL,
        name="gram_early",
    )(*operands, *(blocks[n] for n in early))
    results = ()
    for on_own, numbers in ((True, late[:-1]), (False, late)):
        first = 5 + len(numbers)
        results = pl.pallas_call(
            functools.partial(finish_kernel, half, numbers, on_own),
            out_shape=(rows, jax.ShapeDtypeStruct(scores.shape, scores.dtype)),
            in_specs=[VMEM] * first + [HBM] * len(results),
            out_specs=(HBM, HBM),
            scratch_shapes=[pltpu.VMEM(rows.shape, rows.dtype), pltpu.SemaphoreType.DMA((2,))],
            input_output_aliases={first + n: n for n in range(len(results))},
            compiler_params=SMALL,
            name="gram_own" if on_own else "gram_other",
        )(*operands, scores, so_far, *(blocks[n] for n in numbers), *results)
    return results


def local(inputs, out_grads, proj_in, proj_out, doc_ids, queries):
    shards = lax.axis_size("dp")
    half = shards // 2
    mine = partial_codes(inputs, out_grads, proj_in.T, proj_out.T)
    other = lax.ppermute(mine, "tensor", [(0, 1), (1, 0)])
    own, message = pack(mine, other, doc_ids)
    blocks = []
    for what, far, near, crossed in plan(shards):
        moves = []
        for s in range(shards):
            side = s // half
            for core in range(2):
                to = s ^ (near if core == side else far)[side]
                to_core = core if to // half == side else 1 - core
                by = 1 - core if side in crossed else core
                moves.append((2 * s + by, 2 * to + to_core))
        blocks.append(lax.ppermute(blocks[what] if what >= 0 else message, ("dp", "tensor"), moves))
    scores, grads, ins = score_docs(own, message, queries)
    return gram_of(message, grads, ins, scores, blocks)


def solution(mesh):
    return jax.shard_map(
        local,
        mesh=mesh,
        in_specs=(
            P(("groups", "dp"), "tensor"),
            P(("groups", "dp"), "tensor"),
            P(),
            P(),
            P(("groups", "dp"), None),
            P(),
        ),
        out_specs=(P(("groups", "dp"), "tensor"), P(("groups", "dp"), None)),
        check_vma=False,
    )
```

```python
import functools

import jax
import jax.numpy as jnp
from jax import lax
from jax.experimental import pallas as pl
from jax.experimental.pallas import tpu as pltpu
from jax.sharding import PartitionSpec as P

DOCS_DEV = 8
EXTRA = 8
STEPS = 8.0
TOP = 32767.0
NT = (((1,), (1,)), ((), ()))
NN = (((1,), (0,)), ((), ()))
VMEM = pl.BlockSpec(memory_space=pltpu.VMEM)
HBM = pl.BlockSpec(memory_space=pltpu.HBM)
SMALL = pltpu.CompilerParams(vmem_limit_bytes=16 << 20)

dot = functools.partial(lax.dot_general, preferred_element_type=jnp.float32)


def pieces_of(depth):
    size = next(size for size in (2048, 1792, 1024, 512, 256, 128, depth) if depth % size == 0)
    return [(at, size) for at in range(0, depth, size)]


def sum_of(parts):
    while len(parts) > 1:
        parts = [sum(parts[n : n + 2]) for n in range(0, len(parts), 2)]
    return parts[0]


def halves(values):
    high = values.astype(jnp.bfloat16)
    return high, (values - high.astype(jnp.float32)).astype(jnp.bfloat16)


def members(ids, docs):
    rows = lax.broadcasted_iota(jnp.int32, (docs, ids.shape[1]), 0)
    return (rows == ids).astype(jnp.float32)


def codes_kernel(x_hbm, y_hbm, wx_hbm, wy_hbm, out_ref, x, y, wx, wy, sems):
    at_core = lax.axis_index("tensor")
    rank = wx.shape[0]
    jobs = []
    for src, w_src, dst, w_dst, row in ((y_hbm, wy_hbm, y, wy, 0), (x_hbm, wx_hbm, x, wx, rank)):
        depth = dst.shape[1]
        for at, size in pieces_of(depth):
            there = pl.multiple_of(at_core * depth + at, 128)
            here = pl.ds(at, size)
            sem = 2 * len(jobs)
            copies = (
                pltpu.make_async_copy(w_src.at[:, pl.ds(there, size)], w_dst.at[:, here], sems.at[sem]),
                pltpu.make_async_copy(src.at[:, here], dst.at[:, here], sems.at[sem + 1]),
            )
            for copy in copies:
                copy.start()
            jobs.append((copies, dst, w_dst, row, at, size))
    totals = {}
    for copies, dst, w_dst, row, at, size in jobs:
        for copy in copies:
            copy.wait()
        here = slice(at, at + size)
        totals.setdefault(row, []).append(dot(w_dst[:, here], dst[:, here], NT))
    for row, parts in totals.items():
        out_ref[row : row + rank, :] = sum_of(parts)


def partial_codes(inputs, out_grads, proj_in_t, proj_out_t):
    tokens, depth_in = inputs.shape
    depth_out = out_grads.shape[1]
    rank = proj_in_t.shape[0]
    copies = 2 * (len(pieces_of(depth_in)) + len(pieces_of(depth_out)))
    return pl.pallas_call(
        codes_kernel,
        out_shape=jax.ShapeDtypeStruct((2 * rank, tokens), jnp.float32),
        in_specs=[HBM] * 4,
        out_specs=VMEM,
        scratch_shapes=[
            pltpu.VMEM((tokens, depth_in), inputs.dtype),
            pltpu.VMEM((tokens, depth_out), out_grads.dtype),
            pltpu.VMEM((rank, depth_in), proj_in_t.dtype),
            pltpu.VMEM((rank, depth_out), proj_out_t.dtype),
            pltpu.SemaphoreType.DMA((copies,)),
        ],
        compiler_params=pltpu.CompilerParams(vmem_limit_bytes=56_000_000),
        name="partial_codes",
    )(inputs, out_grads, proj_in_t, proj_out_t)


def fixed_point(values):
    largest = jnp.max(jnp.abs(values), axis=0, keepdims=True)
    grade = jnp.ceil(jnp.log(jnp.maximum(largest, 1e-30)) * (STEPS / 0.6931471805599453) + 0.01)
    units = values * (TOP * jnp.exp2(grade * (-1.0 / STEPS)))
    units = jnp.clip(jnp.floor(units + 0.5), -TOP, TOP)
    return units.astype(jnp.int32), grade.astype(jnp.int32)


def pack_kernel(mine_ref, other_ref, ids_ref, own_ref, message_ref):
    rows, tokens = mine_ref.shape
    rank = rows // 2
    ids = ids_ref[...]
    onehot = members(ids, DOCS_DEV)
    count = jnp.maximum(jnp.sum(onehot, axis=1, keepdims=True), 1.0)
    weight = jnp.sum(onehot / jnp.sqrt(count), axis=0, keepdims=True)
    grads = mine_ref[:rank, :] + other_ref[:rank, :]
    ins = (mine_ref[rank:, :] + other_ref[rank:, :]) * weight
    own_ref[:rank, :] = grads
    own_ref[rank:, :] = ins
    grad_units, grad_grade = fixed_point(grads)
    in_units, in_grade = fixed_point(ins)
    message_ref[:rank, :] = lax.shift_left(grad_units, 16) | (in_units & 0xFFFF)
    line = lax.broadcasted_iota(jnp.int32, (EXTRA, tokens), 0)
    message_ref[rank:, :] = jnp.where(
        line == 0, ids, jnp.where(line == 1, grad_grade, in_grade)
    )


def pack(mine, other, doc_ids):
    rows, tokens = mine.shape
    rank = rows // 2
    return pl.pallas_call(
        pack_kernel,
        out_shape=(
            jax.ShapeDtypeStruct((rows, tokens), jnp.float32),
            jax.ShapeDtypeStruct((rank + EXTRA, tokens), jnp.int32),
        ),
        in_specs=[VMEM] * 3,
        out_specs=(VMEM, VMEM),
        compiler_params=SMALL,
        name="pack_codes",
    )(mine, other, doc_ids)


def scores_kernel(own_ref, message_ref, queries, scores_ref, grads_ref, ins_ref):
    rows, tokens = own_ref.shape
    rank = rows // 2
    grads = own_ref[:rank, :]
    ins = own_ref[rank:, :]
    onehot = members(message_ref[rank : rank + 1, :], DOCS_DEV)
    for values, ref in ((grads, grads_ref), (ins, ins_ref)):
        high, low = halves(values)
        stacked = jnp.concatenate([high, high, low, low], axis=0)
        ref[...] = stacked.T
    weighted = (grads[:, None, :] * onehot[None, :, :]).reshape(rank * DOCS_DEV, tokens)
    w_high, w_low = halves(weighted)
    i_high, i_low = halves(jnp.concatenate([ins, ins], axis=0))
    feats = dot(
        jnp.concatenate([w_high, w_high, w_low], axis=1),
        jnp.concatenate([i_high, i_low, i_high], axis=1),
        NT,
    )
    left = lax.broadcasted_iota(jnp.int32, (DOCS_DEV, 2 * rank), 1) < rank
    pairs = [
        jnp.where(
            left,
            feats[i * DOCS_DEV : (i + 1) * DOCS_DEV],
            feats[(i + 1) * DOCS_DEV : (i + 2) * DOCS_DEV],
        )
        for i in range(0, rank, 2)
    ]
    count = queries.shape[0]
    sums = [None] * count
    for n, pair in enumerate(pairs):
        block = queries[:, n * 2 * rank : (n + 1) * 2 * rank]
        for q in range(count):
            term = pair * block[q : q + 1, :]
            sums[q] = term if n == 0 else sums[q] + term
    columns = [jnp.sum(total, axis=1, keepdims=True) for total in sums]
    scores_ref[...] = jnp.concatenate(columns, axis=1) * (1.0 / rank)


def score_docs(own, message, queries):
    rows, tokens = own.shape
    rank = rows // 2
    operand = jax.ShapeDtypeStruct((tokens, 4 * rank), jnp.bfloat16)
    return pl.pallas_call(
        scores_kernel,
        out_shape=(
            jax.ShapeDtypeStruct((DOCS_DEV, queries.shape[0]), jnp.float32),
            operand,
            operand,
        ),
        in_specs=[VMEM] * 3,
        out_specs=(VMEM, VMEM, VMEM),
        compiler_params=SMALL,
        cost_estimate=pl.CostEstimate(flops=1 << 26, bytes_accessed=1 << 19, transcendentals=0),
        name="score_docs",
    )(own, message, queries)


def plan(shards):
    half = shards // 2
    if half == 4:
        return [
            (-1, (4, 4), (1, 1), (1,)),
            (-1, (7, 7), (2, 2), (1,)),
            (0, (2, 1), (2, 2), ()),
            (0, (1, 2), (2, 1), ()),
        ]
    direct = [(-1, (half + n,) * 2, (n + 1,) * 2, ()) for n in range(0, half, 2)]
    return direct + [(n, (1, 1), (1, 1), ()) for n in reversed(range(half // 2))]


def origins(shards):
    found = []
    for what, other, own, _ in plan(shards):
        before = found[what] if what >= 0 else ((0, 0), (0, 0))
        found.append([[a ^ b for a, b in zip(*pair)] for pair in zip(before, (other, own))])
    return found


def gram_sum(half, message_ref, grads_ref, ins_ref, parts):
    rank = message_ref.shape[0] - EXTRA
    onehot = members(message_ref[rank : rank + 1, :], DOCS_DEV).astype(jnp.bfloat16)
    doubled = jnp.concatenate([onehot, onehot], axis=1)
    total = None
    for first in range(0, len(parts), 4):
        codes, ids, scales = [], [], []
        for block, place in parts[first : first + 4]:
            codes.append(block[:rank, :])
            ids.append(block[rank : rank + 1, :] + place * DOCS_DEV)
            grades = block[rank + 1 : rank + 2, :] + block[rank + 2 : rank + 3, :]
            scales.append(grades.astype(jnp.float32))
        codes, ids, scales = (jnp.concatenate(part, axis=1) for part in (codes, ids, scales))
        product = None
        for units, left in (
            (lax.shift_right_arithmetic(codes, 16), grads_ref),
            (lax.shift_right_arithmetic(lax.shift_left(codes, 16), 16), ins_ref),
        ):
            high, low = halves(units.astype(jnp.float32))
            part = dot(left[...], jnp.concatenate([high, low, high, low], axis=0), NN)
            product = part if product is None else product * part
        high, low = halves(product)
        by_doc = dot(doubled, jnp.concatenate([high, low], axis=0), NN)
        by_doc = by_doc * (jnp.exp2(scales * (1.0 / STEPS)) * (1.0 / (TOP * TOP * rank * rank)))
        high, low = halves(by_doc)
        theirs = members(ids, half * DOCS_DEV).astype(jnp.bfloat16)
        part = dot(jnp.concatenate([high, low], axis=0), theirs, NT)
        total = part if total is None else total + part
    return total[:DOCS_DEV, :] + total[DOCS_DEV:, :]


def place_of(shard, half, own_half, origin):
    far, near = origin
    return lax.rem(lax.bitwise_xor(shard, jnp.where(own_half, near, far)), half)


def blocks_at(shard, half, own_half, numbers, refs):
    parts = []
    for ref, n in zip(refs, numbers):
        far, near = (jnp.where(shard < half, *bits) for bits in origins(2 * half)[n])
        place = lax.rem(lax.bitwise_xor(shard, jnp.where(own_half, near, far)), half)
        parts.append((ref[...], place))
    return parts


def position(half):
    shard, core = lax.axis_index("dp"), lax.axis_index("tensor")
    return shard, lax.div(shard, half) == core


def early_kernel(half, numbers, message_ref, grads_ref, ins_ref, *refs):
    blocks, sum_ref = refs[:-1], refs[-1]
    shard, own_half = position(half)
    parts = blocks_at(shard, half, own_half, numbers, blocks)
    parts.append((message_ref[...], jnp.where(own_half, lax.rem(shard, half), -half)))
    sum_ref[...] = gram_sum(half, message_ref, grads_ref, ins_ref, parts)


def write_out(total_ref, scores_ref, out_ref, scores_out_ref, sems):
    copies = (
        pltpu.make_async_copy(scores_ref, scores_out_ref, sems.at[0]),
        pltpu.make_async_copy(total_ref, out_ref, sems.at[1]),
    )
    for copy in copies:
        copy.start()
    for copy in copies:
        copy.wait()


def middle_kernel(half, numbers, message_ref, grads_ref, ins_ref, scores_ref, sum_ref, *refs):
    blocks, (out_ref, scores_out_ref, total_ref, sems) = refs[:-4], refs[-4:]
    shard, own_half = position(half)
    parts = blocks_at(shard, half, own_half, numbers, blocks)
    total_ref[...] = sum_ref[...] + gram_sum(half, message_ref, grads_ref, ins_ref, parts)

    @pl.when(own_half)
    def _():
        write_out(total_ref, scores_ref, out_ref, scores_out_ref, sems)


def last_kernel(half, message_ref, grads_ref, ins_ref, scores_ref, sum_ref, block_ref, *refs):
    out_ref, scores_out_ref, total_ref, sems = refs[-4:]
    shard, own_half = position(half)

    @pl.when(jnp.logical_not(own_half))
    def _():
        parts = blocks_at(shard, half, own_half, [half - 1], [block_ref])
        total_ref[...] = sum_ref[...] + gram_sum(half, message_ref, grads_ref, ins_ref, parts)
        write_out(total_ref, scores_ref, out_ref, scores_out_ref, sems)


def gram_of(message, grads, ins, scores, blocks):
    half = len(blocks)
    rows = jax.ShapeDtypeStruct((DOCS_DEV, half * DOCS_DEV), jnp.float32)
    results = (rows, jax.ShapeDtypeStruct(scores.shape, scores.dtype))
    operands = (message, grads, ins)
    early, middle = range(half - 3), range(half - 3, half - 1)
    so_far = pl.pallas_call(
        functools.partial(early_kernel, half, early),
        out_shape=rows,
        in_specs=[VMEM] * (3 + len(early)),
        out_specs=VMEM,
        compiler_params=SMALL,
        name="gram_early",
    )(*operands, *(blocks[n] for n in early))
    *results_own, so_far = pl.pallas_call(
        functools.partial(middle_kernel, half, middle),
        out_shape=(*results, rows),
        in_specs=[VMEM] * (5 + len(middle)),
        out_specs=(HBM, HBM, VMEM),
        scratch_shapes=[pltpu.SemaphoreType.DMA((2,))],
        compiler_params=SMALL,
        name="gram_middle",
    )(*operands, scores, so_far, *(blocks[n] for n in middle))
    return pl.pallas_call(
        functools.partial(last_kernel, half),
        out_shape=results,
        in_specs=[VMEM] * 6 + [HBM] * 2,
        out_specs=(HBM, HBM),
        scratch_shapes=[pltpu.VMEM(rows.shape, rows.dtype), pltpu.SemaphoreType.DMA((2,))],
        input_output_aliases={6: 0, 7: 1},
        compiler_params=SMALL,
        name="gram_last",
    )(*operands, scores, so_far, blocks[-1], *results_own)


def local(inputs, out_grads, proj_in, proj_out, doc_ids, queries):
    shards = lax.axis_size("dp")
    half = shards // 2
    mine = partial_codes(inputs, out_grads, proj_in.T, proj_out.T)
    other = lax.ppermute(mine, "tensor", [(0, 1), (1, 0)])
    own, message = pack(mine, other, doc_ids)
    blocks = []
    for what, far, near, crossed in plan(shards):
        moves = []
        for s in range(shards):
            side = s // half
            for core in range(2):
                to = s ^ (near if core == side else far)[side]
                to_core = core if to // half == side else 1 - core
                by = 1 - core if side in crossed else core
                moves.append((2 * s + by, 2 * to + to_core))
        blocks.append(lax.ppermute(blocks[what] if what >= 0 else message, ("dp", "tensor"), moves))
    scores, grads, ins = score_docs(own, message, queries)
    return gram_of(message, grads, ins, scores, blocks)


def solution(mesh):
    return jax.shard_map(
        local,
        mesh=mesh,
        in_specs=(
            P(("groups", "dp"), "tensor"),
            P(("groups", "dp"), "tensor"),
            P(),
            P(),
            P(("groups", "dp"), None),
            P(),
        ),
        out_specs=(P(("groups", "dp"), "tensor"), P(("groups", "dp"), None)),
        check_vma=False,
    )
```

```python
import functools

import jax
import jax.numpy as jnp
from jax import lax
from jax.experimental import pallas as pl
from jax.experimental.pallas import tpu as pltpu
from jax.sharding import PartitionSpec as P

DOCS_DEV = 8
EXTRA = 8
STEPS = 8.0
TOP = 32767.0
NT = (((1,), (1,)), ((), ()))
NN = (((1,), (0,)), ((), ()))
VMEM = pl.BlockSpec(memory_space=pltpu.VMEM)
HBM = pl.BlockSpec(memory_space=pltpu.HBM)
SMALL = pltpu.CompilerParams(vmem_limit_bytes=16 << 20)

dot = functools.partial(lax.dot_general, preferred_element_type=jnp.float32)


def pieces_of(depth):
    count = -(-depth // 2432)
    size = -(-depth // (count * 128)) * 128
    return [(at, min(size, depth - at)) for at in range(0, depth, size)]


def sum_of(parts):
    while len(parts) > 1:
        parts = [sum(parts[n : n + 2]) for n in range(0, len(parts), 2)]
    return parts[0]


def halves(values):
    high = values.astype(jnp.bfloat16)
    return high, (values - high.astype(jnp.float32)).astype(jnp.bfloat16)


def members(ids, docs):
    rows = lax.broadcasted_iota(jnp.int32, (docs, ids.shape[1]), 0)
    return (rows == ids).astype(jnp.float32)


def codes_kernel(x_hbm, y_hbm, wx_hbm, wy_hbm, out_ref, x, y, wx, wy, sems):
    at_core = lax.axis_index("tensor")
    rank = wx.shape[0]
    jobs = []
    for src, w_src, dst, w_dst, row in ((y_hbm, wy_hbm, y, wy, 0), (x_hbm, wx_hbm, x, wx, rank)):
        depth = dst.shape[1]
        for at, size in pieces_of(depth):
            there = pl.multiple_of(at_core * depth + at, 128)
            here = pl.ds(at, size)
            sem = 2 * len(jobs)
            copies = (
                pltpu.make_async_copy(w_src.at[:, pl.ds(there, size)], w_dst.at[:, here], sems.at[sem]),
                pltpu.make_async_copy(src.at[:, here], dst.at[:, here], sems.at[sem + 1]),
            )
            for copy in copies:
                copy.start()
            jobs.append((copies, dst, w_dst, row, at, size))
    totals = {}
    for copies, dst, w_dst, row, at, size in jobs:
        for copy in copies:
            copy.wait()
        here = slice(at, at + size)
        totals.setdefault(row, []).append(dot(w_dst[:, here], dst[:, here], NT))
    for row, parts in totals.items():
        out_ref[row : row + rank, :] = sum_of(parts)


def partial_codes(inputs, out_grads, proj_in_t, proj_out_t):
    tokens, depth_in = inputs.shape
    depth_out = out_grads.shape[1]
    rank = proj_in_t.shape[0]
    copies = 2 * (len(pieces_of(depth_in)) + len(pieces_of(depth_out)))
    return pl.pallas_call(
        codes_kernel,
        out_shape=jax.ShapeDtypeStruct((2 * rank, tokens), jnp.float32),
        in_specs=[HBM] * 4,
        out_specs=VMEM,
        scratch_shapes=[
            pltpu.VMEM((tokens, depth_in), inputs.dtype),
            pltpu.VMEM((tokens, depth_out), out_grads.dtype),
            pltpu.VMEM((rank, depth_in), proj_in_t.dtype),
            pltpu.VMEM((rank, depth_out), proj_out_t.dtype),
            pltpu.SemaphoreType.DMA((copies,)),
        ],
        compiler_params=pltpu.CompilerParams(vmem_limit_bytes=56_000_000),
        name="partial_codes",
    )(inputs, out_grads, proj_in_t, proj_out_t)


def fixed_point(values):
    largest = jnp.max(jnp.abs(values), axis=0, keepdims=True)
    grade = jnp.ceil(jnp.log(jnp.maximum(largest, 1e-30)) * (STEPS / 0.6931471805599453) + 0.01)
    units = values * (TOP * jnp.exp2(grade * (-1.0 / STEPS)))
    units = jnp.clip(jnp.floor(units + 0.5), -TOP, TOP)
    return units.astype(jnp.int32), grade.astype(jnp.int32)


def pack_kernel(mine_ref, other_ref, ids_ref, own_ref, message_ref):
    rows, tokens = mine_ref.shape
    rank = rows // 2
    ids = ids_ref[...]
    onehot = members(ids, DOCS_DEV)
    count = jnp.maximum(jnp.sum(onehot, axis=1, keepdims=True), 1.0)
    weight = jnp.sum(onehot / jnp.sqrt(count), axis=0, keepdims=True)
    grads = mine_ref[:rank, :] + other_ref[:rank, :]
    ins = (mine_ref[rank:, :] + other_ref[rank:, :]) * weight
    own_ref[:rank, :] = grads
    own_ref[rank:, :] = ins
    grad_units, grad_grade = fixed_point(grads)
    in_units, in_grade = fixed_point(ins)
    message_ref[:rank, :] = lax.shift_left(grad_units, 16) | (in_units & 0xFFFF)
    line = lax.broadcasted_iota(jnp.int32, (EXTRA, tokens), 0)
    message_ref[rank:, :] = jnp.where(
        line == 0, ids, jnp.where(line == 1, grad_grade, in_grade)
    )


def pack(mine, other, doc_ids):
    rows, tokens = mine.shape
    rank = rows // 2
    return pl.pallas_call(
        pack_kernel,
        out_shape=(
            jax.ShapeDtypeStruct((rows, tokens), jnp.float32),
            jax.ShapeDtypeStruct((rank + EXTRA, tokens), jnp.int32),
        ),
        in_specs=[VMEM] * 3,
        out_specs=(VMEM, VMEM),
        compiler_params=SMALL,
        name="pack_codes",
    )(mine, other, doc_ids)


def scores_kernel(own_ref, message_ref, queries, scores_ref, grads_ref, ins_ref):
    rows, tokens = own_ref.shape
    rank = rows // 2
    grads = own_ref[:rank, :]
    ins = own_ref[rank:, :]
    onehot = members(message_ref[rank : rank + 1, :], DOCS_DEV)
    for values, ref in ((grads, grads_ref), (ins, ins_ref)):
        high, low = halves(values)
        stacked = jnp.concatenate([high, high, low, low], axis=0)
        ref[...] = stacked.T
    weighted = (grads[:, None, :] * onehot[None, :, :]).reshape(rank * DOCS_DEV, tokens)
    w_high, w_low = halves(weighted)
    i_high, i_low = halves(jnp.concatenate([ins, ins], axis=0))
    feats = dot(
        jnp.concatenate([w_high, w_high, w_low], axis=1),
        jnp.concatenate([i_high, i_low, i_high], axis=1),
        NT,
    )
    left = lax.broadcasted_iota(jnp.int32, (DOCS_DEV, 2 * rank), 1) < rank
    pairs = [
        jnp.where(
            left,
            feats[i * DOCS_DEV : (i + 1) * DOCS_DEV],
            feats[(i + 1) * DOCS_DEV : (i + 2) * DOCS_DEV],
        )
        for i in range(0, rank, 2)
    ]
    count = queries.shape[0]
    sums = [None] * count
    for n, pair in enumerate(pairs):
        block = queries[:, n * 2 * rank : (n + 1) * 2 * rank]
        for q in range(count):
            term = pair * block[q : q + 1, :]
            sums[q] = term if n == 0 else sums[q] + term
    columns = [jnp.sum(total, axis=1, keepdims=True) for total in sums]
    scores_ref[...] = jnp.concatenate(columns, axis=1) * (1.0 / rank)


def score_docs(own, message, queries):
    rows, tokens = own.shape
    rank = rows // 2
    operand = jax.ShapeDtypeStruct((tokens, 4 * rank), jnp.bfloat16)
    return pl.pallas_call(
        scores_kernel,
        out_shape=(
            jax.ShapeDtypeStruct((DOCS_DEV, queries.shape[0]), jnp.float32),
            operand,
            operand,
        ),
        in_specs=[VMEM] * 3,
        out_specs=(VMEM, VMEM, VMEM),
        compiler_params=SMALL,
        cost_estimate=pl.CostEstimate(flops=1 << 26, bytes_accessed=1 << 19, transcendentals=0),
        name="score_docs",
    )(own, message, queries)


def plan(shards):
    half = shards // 2
    if half == 4:
        return [
            (-1, (4, 4), (1, 1), (1,)),
            (-1, (7, 7), (2, 2), (1,)),
            (0, (2, 1), (2, 2), ()),
            (0, (1, 2), (2, 1), ()),
        ]
    direct = [(-1, (half + n,) * 2, (n + 1,) * 2, ()) for n in range(0, half, 2)]
    return direct + [(n, (1, 1), (1, 1), ()) for n in reversed(range(half // 2))]


def origins(shards):
    found = []
    for what, other, own, _ in plan(shards):
        before = found[what] if what >= 0 else ((0, 0), (0, 0))
        found.append([[a ^ b for a, b in zip(*pair)] for pair in zip(before, (other, own))])
    return found


def gram_sum(half, message_ref, grads_ref, ins_ref, parts):
    rank = message_ref.shape[0] - EXTRA
    onehot = members(message_ref[rank : rank + 1, :], DOCS_DEV).astype(jnp.bfloat16)
    doubled = jnp.concatenate([onehot, onehot], axis=1)
    total = None
    for first in range(0, len(parts), 4):
        codes, ids, scales = [], [], []
        for block, place in parts[first : first + 4]:
            codes.append(block[:rank, :])
            ids.append(block[rank : rank + 1, :] + place * DOCS_DEV)
            grades = block[rank + 1 : rank + 2, :] + block[rank + 2 : rank + 3, :]
            scales.append(grades.astype(jnp.float32))
        codes, ids, scales = (jnp.concatenate(part, axis=1) for part in (codes, ids, scales))
        product = None
        for units, left in (
            (lax.shift_right_arithmetic(codes, 16), grads_ref),
            (lax.shift_right_arithmetic(lax.shift_left(codes, 16), 16), ins_ref),
        ):
            high, low = halves(units.astype(jnp.float32))
            part = dot(left[...], jnp.concatenate([high, low, high, low], axis=0), NN)
            product = part if product is None else product * part
        high, low = halves(product)
        by_doc = dot(doubled, jnp.concatenate([high, low], axis=0), NN)
        by_doc = by_doc * (jnp.exp2(scales * (1.0 / STEPS)) * (1.0 / (TOP * TOP * rank * rank)))
        high, low = halves(by_doc)
        theirs = members(ids, half * DOCS_DEV).astype(jnp.bfloat16)
        part = dot(jnp.concatenate([high, low], axis=0), theirs, NT)
        total = part if total is None else total + part
    return total[:DOCS_DEV, :] + total[DOCS_DEV:, :]


def place_of(shard, half, own_half, origin):
    far, near = origin
    return lax.rem(lax.bitwise_xor(shard, jnp.where(own_half, near, far)), half)


def blocks_at(shard, half, own_half, numbers, refs):
    parts = []
    for ref, n in zip(refs, numbers):
        far, near = (jnp.where(shard < half, *bits) for bits in origins(2 * half)[n])
        place = lax.rem(lax.bitwise_xor(shard, jnp.where(own_half, near, far)), half)
        parts.append((ref[...], place))
    return parts


def position(half):
    shard, core = lax.axis_index("dp"), lax.axis_index("tensor")
    return shard, lax.div(shard, half) == core


def early_kernel(half, numbers, message_ref, grads_ref, ins_ref, *refs):
    blocks, sum_ref = refs[:-1], refs[-1]
    shard, own_half = position(half)
    parts = blocks_at(shard, half, own_half, numbers, blocks)
    parts.append((message_ref[...], jnp.where(own_half, lax.rem(shard, half), -half)))
    sum_ref[...] = gram_sum(half, message_ref, grads_ref, ins_ref, parts)


def finish_kernel(half, numbers, on_own, message_ref, grads_ref, ins_ref, scores_ref, sum_ref, *refs):
    blocks, (out_ref, scores_out_ref, total, sems) = refs[: len(numbers)], refs[-4:]
    shard, own_half = position(half)

    @pl.when(own_half if on_own else jnp.logical_not(own_half))
    def _():
        scores_copy = pltpu.make_async_copy(scores_ref, scores_out_ref, sems.at[0])
        scores_copy.start()
        parts = blocks_at(shard, half, own_half, numbers, blocks)
        total[...] = sum_ref[...] + gram_sum(half, message_ref, grads_ref, ins_ref, parts)
        copy = pltpu.make_async_copy(total, out_ref, sems.at[1])
        copy.start()
        copy.wait()
        scores_copy.wait()


def gram_of(message, grads, ins, scores, blocks):
    half = len(blocks)
    rows = jax.ShapeDtypeStruct((DOCS_DEV, half * DOCS_DEV), jnp.float32)
    operands = (message, grads, ins)
    early, late = range(half - 3), [*range(half - 3, half)]
    so_far = pl.pallas_call(
        functools.partial(early_kernel, half, early),
        out_shape=rows,
        in_specs=[VMEM] * (3 + len(early)),
        out_specs=VMEM,
        compiler_params=SMALL,
        name="gram_early",
    )(*operands, *(blocks[n] for n in early))
    results = ()
    for on_own, numbers in ((True, late[:-1]), (False, late)):
        first = 5 + len(numbers)
        results = pl.pallas_call(
            functools.partial(finish_kernel, half, numbers, on_own),
            out_shape=(rows, jax.ShapeDtypeStruct(scores.shape, scores.dtype)),
            in_specs=[VMEM] * first + [HBM] * len(results),
            out_specs=(HBM, HBM),
            scratch_shapes=[pltpu.VMEM(rows.shape, rows.dtype), pltpu.SemaphoreType.DMA((2,))],
            input_output_aliases={first + n: n for n in range(len(results))},
            compiler_params=SMALL,
            name="gram_own" if on_own else "gram_other",
        )(*operands, scores, so_far, *(blocks[n] for n in numbers), *results)
    return results


def local(inputs, out_grads, proj_in, proj_out, doc_ids, queries):
    shards = lax.axis_size("dp")
    half = shards // 2
    mine = partial_codes(inputs, out_grads, proj_in.T, proj_out.T)
    other = lax.ppermute(mine, "tensor", [(0, 1), (1, 0)])
    own, message = pack(mine, other, doc_ids)
    blocks = []
    for what, far, near, crossed in plan(shards):
        moves = []
        for s in range(shards):
            side = s // half
            for core in range(2):
                to = s ^ (near if core == side else far)[side]
                to_core = core if to // half == side else 1 - core
                by = 1 - core if side in crossed else core
                moves.append((2 * s + by, 2 * to + to_core))
        blocks.append(lax.ppermute(blocks[what] if what >= 0 else message, ("dp", "tensor"), moves))
    scores, grads, ins = score_docs(own, message, queries)
    return gram_of(message, grads, ins, scores, blocks)


def solution(mesh):
    return jax.shard_map(
        local,
        mesh=mesh,
        in_specs=(
            P(("groups", "dp"), "tensor"),
            P(("groups", "dp"), "tensor"),
            P(),
            P(),
            P(("groups", "dp"), None),
            P(),
        ),
        out_specs=(P(("groups", "dp"), "tensor"), P(("groups", "dp"), None)),
        check_vma=False,
    )
```

```python
import functools

import jax
import jax.numpy as jnp
from jax import lax
from jax.experimental import pallas as pl
from jax.experimental.pallas import tpu as pltpu
from jax.sharding import PartitionSpec as P

DOCS_DEV = 8
EXTRA = 8
STEPS = 8.0
TOP = 32767.0
NT = (((1,), (1,)), ((), ()))
NN = (((1,), (0,)), ((), ()))
VMEM = pl.BlockSpec(memory_space=pltpu.VMEM)
HBM = pl.BlockSpec(memory_space=pltpu.HBM)
SMALL = pltpu.CompilerParams(vmem_limit_bytes=16 << 20)

dot = functools.partial(lax.dot_general, preferred_element_type=jnp.float32)


def pieces_of(depth):
    count = -(-depth // 2432)
    size = -(-depth // (count * 128)) * 128
    return [(at, min(size, depth - at)) for at in range(0, depth, size)]


def sum_of(parts):
    while len(parts) > 1:
        parts = [sum(parts[n : n + 2]) for n in range(0, len(parts), 2)]
    return parts[0]


def halves(values):
    high = values.astype(jnp.bfloat16)
    return high, (values - high.astype(jnp.float32)).astype(jnp.bfloat16)


def members(ids, docs):
    rows = lax.broadcasted_iota(jnp.int32, (docs, ids.shape[1]), 0)
    return (rows == ids).astype(jnp.float32)


def codes_kernel(x_hbm, y_hbm, wx_hbm, wy_hbm, out_ref, x, y, wx, wy, sems):
    at_core = lax.axis_index("tensor")
    rank = wx.shape[0]
    jobs = []
    for src, w_src, dst, w_dst, row in ((y_hbm, wy_hbm, y, wy, 0), (x_hbm, wx_hbm, x, wx, rank)):
        depth = dst.shape[1]
        for at, size in pieces_of(depth):
            there = pl.multiple_of(at_core * depth + at, 128)
            here = pl.ds(at, size)
            sem = 2 * len(jobs)
            copies = (
                pltpu.make_async_copy(w_src.at[:, pl.ds(there, size)], w_dst.at[:, here], sems.at[sem]),
                pltpu.make_async_copy(src.at[:, here], dst.at[:, here], sems.at[sem + 1]),
            )
            for copy in copies:
                copy.start()
            jobs.append((copies, dst, w_dst, row, at, size))
    totals = {}
    for copies, dst, w_dst, row, at, size in jobs:
        for copy in copies:
            copy.wait()
        here = slice(at, at + size)
        totals.setdefault(row, []).append(dot(w_dst[:, here], dst[:, here], NT))
    for row, parts in totals.items():
        out_ref[row : row + rank, :] = sum_of(parts)


def partial_codes(inputs, out_grads, proj_in_t, proj_out_t):
    tokens, depth_in = inputs.shape
    depth_out = out_grads.shape[1]
    rank = proj_in_t.shape[0]
    copies = 2 * (len(pieces_of(depth_in)) + len(pieces_of(depth_out)))
    return pl.pallas_call(
        codes_kernel,
        out_shape=jax.ShapeDtypeStruct((2 * rank, tokens), jnp.float32),
        in_specs=[HBM] * 4,
        out_specs=VMEM,
        scratch_shapes=[
            pltpu.VMEM((tokens, depth_in), inputs.dtype),
            pltpu.VMEM((tokens, depth_out), out_grads.dtype),
            pltpu.VMEM((rank, depth_in), proj_in_t.dtype),
            pltpu.VMEM((rank, depth_out), proj_out_t.dtype),
            pltpu.SemaphoreType.DMA((copies,)),
        ],
        compiler_params=pltpu.CompilerParams(vmem_limit_bytes=56_000_000),
        name="partial_codes",
    )(inputs, out_grads, proj_in_t, proj_out_t)


def fixed_point(values):
    largest = jnp.max(jnp.abs(values), axis=0, keepdims=True)
    grade = jnp.ceil(jnp.log(jnp.maximum(largest, 1e-30)) * (STEPS / 0.6931471805599453) + 0.01)
    units = values * (TOP * jnp.exp2(grade * (-1.0 / STEPS)))
    units = jnp.clip(jnp.floor(units + 0.5), -TOP, TOP)
    return units.astype(jnp.int32), grade.astype(jnp.int32)


def pack_kernel(mine_ref, other_ref, ids_ref, own_ref, message_ref):
    rows, tokens = mine_ref.shape
    rank = rows // 2
    ids = ids_ref[...]
    onehot = members(ids, DOCS_DEV)
    count = jnp.maximum(jnp.sum(onehot, axis=1, keepdims=True), 1.0)
    weight = jnp.sum(onehot / jnp.sqrt(count), axis=0, keepdims=True)
    grads = mine_ref[:rank, :] + other_ref[:rank, :]
    ins = (mine_ref[rank:, :] + other_ref[rank:, :]) * weight
    own_ref[:rank, :] = grads
    own_ref[rank:, :] = ins
    grad_units, grad_grade = fixed_point(grads)
    in_units, in_grade = fixed_point(ins)
    message_ref[:rank, :] = lax.shift_left(grad_units, 16) | (in_units & 0xFFFF)
    line = lax.broadcasted_iota(jnp.int32, (EXTRA, tokens), 0)
    message_ref[rank:, :] = jnp.where(
        line == 0, ids, jnp.where(line == 1, grad_grade, in_grade)
    )


def pack(mine, other, doc_ids):
    rows, tokens = mine.shape
    rank = rows // 2
    return pl.pallas_call(
        pack_kernel,
        out_shape=(
            jax.ShapeDtypeStruct((rows, tokens), jnp.float32),
            jax.ShapeDtypeStruct((rank + EXTRA, tokens), jnp.int32),
        ),
        in_specs=[VMEM] * 3,
        out_specs=(VMEM, VMEM),
        compiler_params=SMALL,
        name="pack_codes",
    )(mine, other, doc_ids)


def scores_kernel(own_ref, message_ref, queries, scores_ref, grads_ref, ins_ref, feats_ref):
    rows, tokens = own_ref.shape
    rank = rows // 2
    grads = own_ref[:rank, :]
    ins = own_ref[rank:, :]
    onehot = members(message_ref[rank : rank + 1, :], DOCS_DEV)
    for values, ref in ((grads, grads_ref), (ins, ins_ref)):
        high, low = halves(values)
        stacked = jnp.concatenate([high, high, low, low], axis=0)
        ref[...] = stacked.T
    weighted = (grads[:, None, :] * onehot[None, :, :]).reshape(rank * DOCS_DEV, tokens)
    w_high, w_low = halves(weighted)
    i_high, i_low = halves(jnp.concatenate([ins, ins], axis=0))
    feats = dot(
        jnp.concatenate([w_high, w_high, w_low], axis=1),
        jnp.concatenate([i_high, i_low, i_high], axis=1),
        NT,
    )
    feats_ref[...] = jnp.concatenate(halves(feats), axis=1)
    left = lax.broadcasted_iota(jnp.int32, (DOCS_DEV, 2 * rank), 1) < rank
    pairs = [
        jnp.where(
            left,
            feats[i * DOCS_DEV : (i + 1) * DOCS_DEV],
            feats[(i + 1) * DOCS_DEV : (i + 2) * DOCS_DEV],
        )
        for i in range(0, rank, 2)
    ]
    count = queries.shape[0]
    sums = [None] * count
    for n, pair in enumerate(pairs):
        block = queries[:, n * 2 * rank : (n + 1) * 2 * rank]
        for q in range(count):
            term = pair * block[q : q + 1, :]
            sums[q] = term if n == 0 else sums[q] + term
    columns = [jnp.sum(total, axis=1, keepdims=True) for total in sums]
    scores_ref[...] = jnp.concatenate(columns, axis=1) * (1.0 / rank)


def score_docs(own, message, queries):
    rows, tokens = own.shape
    rank = rows // 2
    operand = jax.ShapeDtypeStruct((tokens, 4 * rank), jnp.bfloat16)
    return pl.pallas_call(
        scores_kernel,
        out_shape=(
            jax.ShapeDtypeStruct((DOCS_DEV, queries.shape[0]), jnp.float32),
            operand,
            operand,
            jax.ShapeDtypeStruct((rank * DOCS_DEV, 4 * rank), jnp.bfloat16),
        ),
        in_specs=[VMEM] * 3,
        out_specs=(VMEM,) * 4,
        compiler_params=SMALL,
        cost_estimate=pl.CostEstimate(flops=1 << 26, bytes_accessed=1 << 19, transcendentals=0),
        name="score_docs",
    )(own, message, queries)


def plan(shards):
    half = shards // 2
    if half == 4:
        return [
            (-1, (4, 4), (1, 1), (1,)),
            (-1, (7, 7), (2, 2), (1,)),
            (0, (2, 1), (2, 2), ()),
            (0, (1, 2), (2, 1), ()),
        ]
    direct = [(-1, (half + n,) * 2, (n + 1,) * 2, ()) for n in range(0, half, 2)]
    return direct + [(n, (1, 1), (1, 1), ()) for n in reversed(range(half // 2))]


def origins(shards):
    found = []
    for what, other, own, _ in plan(shards):
        before = found[what] if what >= 0 else ((0, 0), (0, 0))
        found.append([[a ^ b for a, b in zip(*pair)] for pair in zip(before, (other, own))])
    return found


def gram_sum(half, message_ref, grads_ref, ins_ref, parts):
    rank = message_ref.shape[0] - EXTRA
    onehot = members(message_ref[rank : rank + 1, :], DOCS_DEV).astype(jnp.bfloat16)
    doubled = jnp.concatenate([onehot, onehot], axis=1)
    total = None
    for first in range(0, len(parts), 4):
        codes, ids, scales = [], [], []
        for block, place in parts[first : first + 4]:
            codes.append(block[:rank, :])
            ids.append(block[rank : rank + 1, :] + place * DOCS_DEV)
            grades = block[rank + 1 : rank + 2, :] + block[rank + 2 : rank + 3, :]
            scales.append(grades.astype(jnp.float32))
        codes, ids, scales = (jnp.concatenate(part, axis=1) for part in (codes, ids, scales))
        product = None
        for units, left in (
            (lax.shift_right_arithmetic(codes, 16), grads_ref),
            (lax.shift_right_arithmetic(lax.shift_left(codes, 16), 16), ins_ref),
        ):
            high, low = halves(units.astype(jnp.float32))
            part = dot(left[...], jnp.concatenate([high, low, high, low], axis=0), NN)
            product = part if product is None else product * part
        high, low = halves(product)
        by_doc = dot(doubled, jnp.concatenate([high, low], axis=0), NN)
        by_doc = by_doc * (jnp.exp2(scales * (1.0 / STEPS)) * (1.0 / (TOP * TOP * rank * rank)))
        high, low = halves(by_doc)
        theirs = members(ids, half * DOCS_DEV).astype(jnp.bfloat16)
        part = dot(jnp.concatenate([high, low], axis=0), theirs, NT)
        total = part if total is None else total + part
    return total[:DOCS_DEV, :] + total[DOCS_DEV:, :]


def place_of(shard, half, own_half, origin):
    far, near = origin
    return lax.rem(lax.bitwise_xor(shard, jnp.where(own_half, near, far)), half)


def blocks_at(shard, half, own_half, numbers, refs):
    parts = []
    for ref, n in zip(refs, numbers):
        far, near = (jnp.where(shard < half, *bits) for bits in origins(2 * half)[n])
        place = lax.rem(lax.bitwise_xor(shard, jnp.where(own_half, near, far)), half)
        parts.append((ref[...], place))
    return parts


def position(half):
    shard, core = lax.axis_index("dp"), lax.axis_index("tensor")
    return shard, lax.div(shard, half) == core


def early_kernel(half, numbers, message_ref, grads_ref, ins_ref, *refs):
    blocks, sum_ref = refs[:-1], refs[-1]
    shard, own_half = position(half)
    parts = blocks_at(shard, half, own_half, numbers, blocks)
    parts.append((message_ref[...], jnp.where(own_half, lax.rem(shard, half), -half)))
    sum_ref[...] = gram_sum(half, message_ref, grads_ref, ins_ref, parts)


def write_out(total_ref, scores_ref, out_ref, scores_out_ref, sems):
    copies = (
        pltpu.make_async_copy(scores_ref, scores_out_ref, sems.at[0]),
        pltpu.make_async_copy(total_ref, out_ref, sems.at[1]),
    )
    for copy in copies:
        copy.start()
    for copy in copies:
        copy.wait()


def middle_kernel(half, numbers, message_ref, grads_ref, ins_ref, scores_ref, sum_ref, *refs):
    blocks, (out_ref, scores_out_ref, total_ref, sems) = refs[:-4], refs[-4:]
    shard, own_half = position(half)
    parts = blocks_at(shard, half, own_half, numbers, blocks)
    total_ref[...] = sum_ref[...] + gram_sum(half, message_ref, grads_ref, ins_ref, parts)

    @pl.when(own_half)
    def _():
        write_out(total_ref, scores_ref, out_ref, scores_out_ref, sems)


def last_kernel(half, feats_ref, scores_ref, sum_ref, block_ref, *refs):
    out_ref, scores_out_ref, total_ref, sems = refs[-4:]
    shard, own_half = position(half)
    rank = feats_ref.shape[1] // 4

    @pl.when(jnp.logical_not(own_half))
    def _():
        ((block, place),) = blocks_at(shard, half, own_half, [half - 1], [block_ref])
        codes = block[:rank, :]
        grads = lax.shift_right_arithmetic(codes, 16).astype(jnp.float32)
        ins = lax.shift_right_arithmetic(lax.shift_left(codes, 16), 16).astype(jnp.float32)
        high, low = halves(ins)
        shares = dot(feats_ref[...], jnp.concatenate([high, low, high, low], axis=0), NN)
        terms = [shares[i * DOCS_DEV : (i + 1) * DOCS_DEV, :] * grads[i : i + 1, :] for i in range(rank)]
        grades = block[rank + 1 : rank + 2, :] + block[rank + 2 : rank + 3, :]
        scales = jnp.exp2(grades.astype(jnp.float32) * (1.0 / STEPS)) * (1.0 / (TOP * TOP * rank * rank))
        high, low = halves(sum_of(terms) * scales)
        theirs = members(block[rank : rank + 1, :] + place * DOCS_DEV, half * DOCS_DEV).astype(jnp.bfloat16)
        part = dot(jnp.concatenate([high, low], axis=0), theirs, NT)
        total_ref[...] = sum_ref[...] + (part[:DOCS_DEV, :] + part[DOCS_DEV:, :])
        write_out(total_ref, scores_ref, out_ref, scores_out_ref, sems)


def gram_of(message, grads, ins, feats, scores, blocks):
    half = len(blocks)
    rows = jax.ShapeDtypeStruct((DOCS_DEV, half * DOCS_DEV), jnp.float32)
    results = (rows, jax.ShapeDtypeStruct(scores.shape, scores.dtype))
    operands = (message, grads, ins)
    early, middle = range(half - 3), range(half - 3, half - 1)
    so_far = pl.pallas_call(
        functools.partial(early_kernel, half, early),
        out_shape=rows,
        in_specs=[VMEM] * (3 + len(early)),
        out_specs=VMEM,
        compiler_params=SMALL,
        name="gram_early",
    )(*operands, *(blocks[n] for n in early))
    *results_own, so_far = pl.pallas_call(
        functools.partial(middle_kernel, half, middle),
        out_shape=(*results, rows),
        in_specs=[VMEM] * (5 + len(middle)),
        out_specs=(HBM, HBM, VMEM),
        scratch_shapes=[pltpu.SemaphoreType.DMA((2,))],
        compiler_params=SMALL,
        name="gram_middle",
    )(*operands, scores, so_far, *(blocks[n] for n in middle))
    return pl.pallas_call(
        functools.partial(last_kernel, half),
        out_shape=results,
        in_specs=[VMEM] * 4 + [HBM] * 2,
        out_specs=(HBM, HBM),
        scratch_shapes=[pltpu.VMEM(rows.shape, rows.dtype), pltpu.SemaphoreType.DMA((2,))],
        input_output_aliases={4: 0, 5: 1},
        compiler_params=SMALL,
        name="gram_last",
    )(feats, scores, so_far, blocks[-1], *results_own)


def local(inputs, out_grads, proj_in, proj_out, doc_ids, queries):
    shards = lax.axis_size("dp")
    half = shards // 2
    mine = partial_codes(inputs, out_grads, proj_in.T, proj_out.T)
    other = lax.ppermute(mine, "tensor", [(0, 1), (1, 0)])
    own, message = pack(mine, other, doc_ids)
    blocks = []
    for what, far, near, crossed in plan(shards):
        moves = []
        for s in range(shards):
            side = s // half
            for core in range(2):
                to = s ^ (near if core == side else far)[side]
                to_core = core if to // half == side else 1 - core
                by = 1 - core if side in crossed else core
                moves.append((2 * s + by, 2 * to + to_core))
        blocks.append(lax.ppermute(blocks[what] if what >= 0 else message, ("dp", "tensor"), moves))
    scores, grads, ins, feats = score_docs(own, message, queries)
    return gram_of(message, grads, ins, feats, scores, blocks)


def solution(mesh):
    return jax.shard_map(
        local,
        mesh=mesh,
        in_specs=(
            P(("groups", "dp"), "tensor"),
            P(("groups", "dp"), "tensor"),
            P(),
            P(),
            P(("groups", "dp"), None),
            P(),
        ),
        out_specs=(P(("groups", "dp"), "tensor"), P(("groups", "dp"), None)),
        check_vma=False,
    )
```

```python
import functools

import jax
import jax.numpy as jnp
from jax import lax
from jax.experimental import pallas as pl
from jax.experimental.pallas import tpu as pltpu
from jax.sharding import PartitionSpec as P

DOCS_DEV = 8
EXTRA = 8
STEPS = 8.0
TOP = 32767.0
NT = (((1,), (1,)), ((), ()))
NN = (((1,), (0,)), ((), ()))
VMEM = pl.BlockSpec(memory_space=pltpu.VMEM)
HBM = pl.BlockSpec(memory_space=pltpu.HBM)
SMALL = pltpu.CompilerParams(vmem_limit_bytes=16 << 20)

dot = functools.partial(lax.dot_general, preferred_element_type=jnp.float32)


def pieces_of(depth):
    count = -(-depth // 3584)
    size = -(-depth // (count * 128)) * 128
    return [(at, min(size, depth - at)) for at in range(0, depth, size)]


def sum_of(parts):
    while len(parts) > 1:
        ends = parts[-1:] if len(parts) % 2 else []
        parts = [a + b for a, b in zip(parts[::2], parts[1::2])] + ends
    return parts[0]


def halves(values):
    high = values.astype(jnp.bfloat16)
    return high, (values - high.astype(jnp.float32)).astype(jnp.bfloat16)


def members(ids, docs):
    rows = lax.broadcasted_iota(jnp.int32, (docs, ids.shape[1]), 0)
    return (rows == ids).astype(jnp.float32)


def codes_kernel(x_hbm, y_hbm, wx_hbm, wy_hbm, out_ref, x, y, wx, wy, sems):
    at_core = lax.axis_index("tensor")
    rank = wx.shape[0]
    jobs = []
    for src, w_src, dst, w_dst, row in ((y_hbm, wy_hbm, y, wy, 0), (x_hbm, wx_hbm, x, wx, rank)):
        depth = dst.shape[1]
        for at, size in pieces_of(depth):
            there = pl.multiple_of(at_core * depth + at, 128)
            here = pl.ds(at, size)
            sem = 2 * len(jobs)
            copies = (
                pltpu.make_async_copy(w_src.at[:, pl.ds(there, size)], w_dst.at[:, here], sems.at[sem]),
                pltpu.make_async_copy(src.at[:, here], dst.at[:, here], sems.at[sem + 1]),
            )
            for copy in copies:
                copy.start()
            jobs.append((copies, dst, w_dst, row, at, size))
    totals = {}
    for copies, dst, w_dst, row, at, size in jobs:
        for copy in copies:
            copy.wait()
        here = slice(at, at + size)
        totals.setdefault(row, []).append(dot(w_dst[:, here], dst[:, here], NT))
    for row, parts in totals.items():
        out_ref[row : row + rank, :] = sum_of(parts)


def partial_codes(inputs, out_grads, proj_in_t, proj_out_t):
    tokens, depth_in = inputs.shape
    depth_out = out_grads.shape[1]
    rank = proj_in_t.shape[0]
    copies = 2 * (len(pieces_of(depth_in)) + len(pieces_of(depth_out)))
    return pl.pallas_call(
        codes_kernel,
        out_shape=jax.ShapeDtypeStruct((2 * rank, tokens), jnp.float32),
        in_specs=[HBM] * 4,
        out_specs=VMEM,
        scratch_shapes=[
            pltpu.VMEM((tokens, depth_in), inputs.dtype),
            pltpu.VMEM((tokens, depth_out), out_grads.dtype),
            pltpu.VMEM((rank, depth_in), proj_in_t.dtype),
            pltpu.VMEM((rank, depth_out), proj_out_t.dtype),
            pltpu.SemaphoreType.DMA((copies,)),
        ],
        compiler_params=pltpu.CompilerParams(vmem_limit_bytes=56_000_000),
        name="partial_codes",
    )(inputs, out_grads, proj_in_t, proj_out_t)


def fixed_point(values):
    largest = jnp.max(jnp.abs(values), axis=0, keepdims=True)
    grade = jnp.ceil(jnp.log(jnp.maximum(largest, 1e-30)) * (STEPS / 0.6931471805599453) + 0.01)
    units = values * (TOP * jnp.exp2(grade * (-1.0 / STEPS)))
    units = jnp.clip(jnp.floor(units + 0.5), -TOP, TOP)
    return units.astype(jnp.int32), grade.astype(jnp.int32)


def pack_kernel(mine_ref, other_ref, ids_ref, own_ref, message_ref):
    rows, tokens = mine_ref.shape
    rank = rows // 2
    ids = ids_ref[...]
    onehot = members(ids, DOCS_DEV)
    count = jnp.maximum(jnp.sum(onehot, axis=1, keepdims=True), 1.0)
    weight = jnp.sum(onehot / jnp.sqrt(count), axis=0, keepdims=True)
    grads = mine_ref[:rank, :] + other_ref[:rank, :]
    ins = (mine_ref[rank:, :] + other_ref[rank:, :]) * weight
    own_ref[:rank, :] = grads
    own_ref[rank:, :] = ins
    grad_units, grad_grade = fixed_point(grads)
    in_units, in_grade = fixed_point(ins)
    message_ref[:rank, :] = lax.shift_left(grad_units, 16) | (in_units & 0xFFFF)
    line = lax.broadcasted_iota(jnp.int32, (EXTRA, tokens), 0)
    message_ref[rank:, :] = jnp.where(
        line == 0, ids, jnp.where(line == 1, grad_grade, in_grade)
    )


def pack(mine, other, doc_ids):
    rows, tokens = mine.shape
    rank = rows // 2
    return pl.pallas_call(
        pack_kernel,
        out_shape=(
            jax.ShapeDtypeStruct((rows, tokens), jnp.float32),
            jax.ShapeDtypeStruct((rank + EXTRA, tokens), jnp.int32),
        ),
        in_specs=[VMEM] * 3,
        out_specs=(VMEM, VMEM),
        compiler_params=SMALL,
        name="pack_codes",
    )(mine, other, doc_ids)


def scores_kernel(own_ref, message_ref, queries, scores_ref, grads_ref, ins_ref, feats_ref):
    rows, tokens = own_ref.shape
    rank = rows // 2
    grads = own_ref[:rank, :]
    ins = own_ref[rank:, :]
    onehot = members(message_ref[rank : rank + 1, :], DOCS_DEV)
    for values, ref in ((grads, grads_ref), (ins, ins_ref)):
        high, low = halves(values)
        stacked = jnp.concatenate([high, high, low, low], axis=0)
        ref[...] = stacked.T
    weighted = (grads[:, None, :] * onehot[None, :, :]).reshape(rank * DOCS_DEV, tokens)
    w_high, w_low = halves(weighted)
    i_high, i_low = halves(jnp.concatenate([ins, ins], axis=0))
    feats = dot(
        jnp.concatenate([w_high, w_high, w_low], axis=1),
        jnp.concatenate([i_high, i_low, i_high], axis=1),
        NT,
    )
    feats_ref[...] = jnp.concatenate(halves(feats), axis=1)
    left = lax.broadcasted_iota(jnp.int32, (DOCS_DEV, 2 * rank), 1) < rank
    pairs = [
        jnp.where(
            left,
            feats[i * DOCS_DEV : (i + 1) * DOCS_DEV],
            feats[(i + 1) * DOCS_DEV : (i + 2) * DOCS_DEV],
        )
        for i in range(0, rank, 2)
    ]
    count = queries.shape[0]
    sums = [None] * count
    for n, pair in enumerate(pairs):
        block = queries[:, n * 2 * rank : (n + 1) * 2 * rank]
        for q in range(count):
            term = pair * block[q : q + 1, :]
            sums[q] = term if n == 0 else sums[q] + term
    columns = [jnp.sum(total, axis=1, keepdims=True) for total in sums]
    scores_ref[...] = jnp.concatenate(columns, axis=1) * (1.0 / rank)


def score_docs(own, message, queries):
    rows, tokens = own.shape
    rank = rows // 2
    operand = jax.ShapeDtypeStruct((tokens, 4 * rank), jnp.bfloat16)
    return pl.pallas_call(
        scores_kernel,
        out_shape=(
            jax.ShapeDtypeStruct((DOCS_DEV, queries.shape[0]), jnp.float32),
            operand,
            operand,
            jax.ShapeDtypeStruct((rank * DOCS_DEV, 4 * rank), jnp.bfloat16),
        ),
        in_specs=[VMEM] * 3,
        out_specs=(VMEM,) * 4,
        compiler_params=SMALL,
        cost_estimate=pl.CostEstimate(flops=1 << 26, bytes_accessed=1 << 19, transcendentals=0),
        name="score_docs",
    )(own, message, queries)


def plan(shards):
    half = shards // 2
    if half == 4:
        return [
            (-1, (4, 4), (1, 1), (1,)),
            (-1, (7, 7), (2, 2), (1,)),
            (0, (2, 1), (2, 2), ()),
            (0, (1, 2), (2, 1), ()),
        ]
    direct = [(-1, (half + n,) * 2, (n + 1,) * 2, ()) for n in range(0, half, 2)]
    return direct + [(n, (1, 1), (1, 1), ()) for n in reversed(range(half // 2))]


def origins(shards):
    found = []
    for what, other, own, _ in plan(shards):
        before = found[what] if what >= 0 else ((0, 0), (0, 0))
        found.append([[a ^ b for a, b in zip(*pair)] for pair in zip(before, (other, own))])
    return found


def gram_sum(half, message_ref, grads_ref, ins_ref, parts):
    rank = message_ref.shape[0] - EXTRA
    onehot = members(message_ref[rank : rank + 1, :], DOCS_DEV).astype(jnp.bfloat16)
    doubled = jnp.concatenate([onehot, onehot], axis=1)
    total = None
    for first in range(0, len(parts), 4):
        codes, ids, scales = [], [], []
        for block, place in parts[first : first + 4]:
            codes.append(block[:rank, :])
            ids.append(block[rank : rank + 1, :] + place * DOCS_DEV)
            grades = block[rank + 1 : rank + 2, :] + block[rank + 2 : rank + 3, :]
            scales.append(grades.astype(jnp.float32))
        codes, ids, scales = (jnp.concatenate(part, axis=1) for part in (codes, ids, scales))
        product = None
        for units, left in (
            (lax.shift_right_arithmetic(codes, 16), grads_ref),
            (lax.shift_right_arithmetic(lax.shift_left(codes, 16), 16), ins_ref),
        ):
            high, low = halves(units.astype(jnp.float32))
            part = dot(left[...], jnp.concatenate([high, low, high, low], axis=0), NN)
            product = part if product is None else product * part
        high, low = halves(product)
        by_doc = dot(doubled, jnp.concatenate([high, low], axis=0), NN)
        by_doc = by_doc * (jnp.exp2(scales * (1.0 / STEPS)) * (1.0 / (TOP * TOP * rank * rank)))
        high, low = halves(by_doc)
        theirs = members(ids, half * DOCS_DEV).astype(jnp.bfloat16)
        part = dot(jnp.concatenate([high, low], axis=0), theirs, NT)
        total = part if total is None else total + part
    return total[:DOCS_DEV, :] + total[DOCS_DEV:, :]


def place_of(shard, half, own_half, origin):
    far, near = origin
    return lax.rem(lax.bitwise_xor(shard, jnp.where(own_half, near, far)), half)


def blocks_at(shard, half, own_half, numbers, refs):
    parts = []
    for ref, n in zip(refs, numbers):
        far, near = (jnp.where(shard < half, *bits) for bits in origins(2 * half)[n])
        place = lax.rem(lax.bitwise_xor(shard, jnp.where(own_half, near, far)), half)
        parts.append((ref[...], place))
    return parts


def position(half):
    shard, core = lax.axis_index("dp"), lax.axis_index("tensor")
    return shard, lax.div(shard, half) == core


def early_kernel(half, numbers, message_ref, grads_ref, ins_ref, *refs):
    blocks, sum_ref = refs[:-1], refs[-1]
    shard, own_half = position(half)
    parts = blocks_at(shard, half, own_half, numbers, blocks)
    parts.append((message_ref[...], jnp.where(own_half, lax.rem(shard, half), -half)))
    sum_ref[...] = gram_sum(half, message_ref, grads_ref, ins_ref, parts)


def sent(src_ref, dst_ref, sem):
    copy = pltpu.make_async_copy(src_ref, dst_ref, sem)
    copy.start()
    return copy


def middle_kernel(half, numbers, message_ref, grads_ref, ins_ref, scores_ref, sum_ref, *refs):
    blocks, (out_ref, scores_out_ref, total_ref, sems) = refs[:-4], refs[-4:]
    shard, own_half = position(half)

    def total():
        parts = blocks_at(shard, half, own_half, numbers, blocks)
        total_ref[...] = sum_ref[...] + gram_sum(half, message_ref, grads_ref, ins_ref, parts)

    @pl.when(own_half)
    def _():
        scores_copy = sent(scores_ref, scores_out_ref, sems.at[0])
        total()
        sent(total_ref, out_ref, sems.at[1]).wait()
        scores_copy.wait()

    @pl.when(jnp.logical_not(own_half))
    def _():
        total()


def last_kernel(half, feats_ref, scores_ref, sum_ref, block_ref, *refs):
    out_ref, scores_out_ref, total_ref, sems = refs[-4:]
    shard, own_half = position(half)
    rank = feats_ref.shape[1] // 4

    @pl.when(jnp.logical_not(own_half))
    def _():
        scores_copy = sent(scores_ref, scores_out_ref, sems.at[0])
        ((block, place),) = blocks_at(shard, half, own_half, [half - 1], [block_ref])
        codes = block[:rank, :]
        grads = lax.shift_right_arithmetic(codes, 16).astype(jnp.float32)
        ins = lax.shift_right_arithmetic(lax.shift_left(codes, 16), 16).astype(jnp.float32)
        high, low = halves(ins)
        shares = dot(feats_ref[...], jnp.concatenate([high, low, high, low], axis=0), NN)
        terms = [shares[i * DOCS_DEV : (i + 1) * DOCS_DEV, :] * grads[i : i + 1, :] for i in range(rank)]
        grades = block[rank + 1 : rank + 2, :] + block[rank + 2 : rank + 3, :]
        scales = jnp.exp2(grades.astype(jnp.float32) * (1.0 / STEPS)) * (1.0 / (TOP * TOP * rank * rank))
        high, low = halves(sum_of(terms) * scales)
        theirs = members(block[rank : rank + 1, :] + place * DOCS_DEV, half * DOCS_DEV).astype(jnp.bfloat16)
        part = dot(jnp.concatenate([high, low], axis=0), theirs, NT)
        total_ref[...] = sum_ref[...] + (part[:DOCS_DEV, :] + part[DOCS_DEV:, :])
        sent(total_ref, out_ref, sems.at[1]).wait()
        scores_copy.wait()


def gram_of(message, grads, ins, feats, scores, blocks):
    half = len(blocks)
    rows = jax.ShapeDtypeStruct((DOCS_DEV, half * DOCS_DEV), jnp.float32)
    results = (rows, jax.ShapeDtypeStruct(scores.shape, scores.dtype))
    operands = (message, grads, ins)
    early, middle = range(half - 3), range(half - 3, half - 1)
    so_far = pl.pallas_call(
        functools.partial(early_kernel, half, early),
        out_shape=rows,
        in_specs=[VMEM] * (3 + len(early)),
        out_specs=VMEM,
        compiler_params=SMALL,
        name="gram_early",
    )(*operands, *(blocks[n] for n in early))
    *results_own, so_far = pl.pallas_call(
        functools.partial(middle_kernel, half, middle),
        out_shape=(*results, rows),
        in_specs=[VMEM] * (5 + len(middle)),
        out_specs=(HBM, HBM, VMEM),
        scratch_shapes=[pltpu.SemaphoreType.DMA((2,))],
        compiler_params=SMALL,
        name="gram_middle",
    )(*operands, scores, so_far, *(blocks[n] for n in middle))
    return pl.pallas_call(
        functools.partial(last_kernel, half),
        out_shape=results,
        in_specs=[VMEM] * 4 + [HBM] * 2,
        out_specs=(HBM, HBM),
        scratch_shapes=[pltpu.VMEM(rows.shape, rows.dtype), pltpu.SemaphoreType.DMA((2,))],
        input_output_aliases={4: 0, 5: 1},
        compiler_params=SMALL,
        name="gram_last",
    )(feats, scores, so_far, blocks[-1], *results_own)


def local(inputs, out_grads, proj_in, proj_out, doc_ids, queries):
    shards = lax.axis_size("dp")
    half = shards // 2
    mine = partial_codes(inputs, out_grads, proj_in.T, proj_out.T)
    other = lax.ppermute(mine, "tensor", [(0, 1), (1, 0)])
    own, message = pack(mine, other, doc_ids)
    blocks = []
    for what, far, near, crossed in plan(shards):
        moves = []
        for s in range(shards):
            side = s // half
            for core in range(2):
                to = s ^ (near if core == side else far)[side]
                to_core = core if to // half == side else 1 - core
                by = 1 - core if side in crossed else core
                moves.append((2 * s + by, 2 * to + to_core))
        blocks.append(lax.ppermute(blocks[what] if what >= 0 else message, ("dp", "tensor"), moves))
    scores, grads, ins, feats = score_docs(own, message, queries)
    return gram_of(message, grads, ins, feats, scores, blocks)


def solution(mesh):
    return jax.shard_map(
        local,
        mesh=mesh,
        in_specs=(
            P(("groups", "dp"), "tensor"),
            P(("groups", "dp"), "tensor"),
            P(),
            P(),
            P(("groups", "dp"), None),
            P(),
        ),
        out_specs=(P(("groups", "dp"), "tensor"), P(("groups", "dp"), None)),
        check_vma=False,
    )
```

```python
import functools

import jax
import jax.numpy as jnp
from jax import lax
from jax.experimental import pallas as pl
from jax.experimental.pallas import tpu as pltpu
from jax.sharding import PartitionSpec as P

DOCS_DEV = 8
EXTRA = 8
STEPS = 8.0
TOP = 32767.0
NT = (((1,), (1,)), ((), ()))
NN = (((1,), (0,)), ((), ()))
VMEM = pl.BlockSpec(memory_space=pltpu.VMEM)
HBM = pl.BlockSpec(memory_space=pltpu.HBM)
SMALL = pltpu.CompilerParams(vmem_limit_bytes=16 << 20)

dot = functools.partial(lax.dot_general, preferred_element_type=jnp.float32)


def pieces_of(depth):
    count = -(-depth // 2432)
    size = -(-depth // (count * 128)) * 128
    return [(at, min(size, depth - at)) for at in range(0, depth, size)]


def sum_of(parts):
    while len(parts) > 1:
        parts = [sum(parts[n : n + 2]) for n in range(0, len(parts), 2)]
    return parts[0]


def halves(values):
    high = values.astype(jnp.bfloat16)
    return high, (values - high.astype(jnp.float32)).astype(jnp.bfloat16)


def members(ids, docs):
    rows = lax.broadcasted_iota(jnp.int32, (docs, ids.shape[1]), 0)
    return (rows == ids).astype(jnp.float32)


def codes_kernel(x_hbm, y_hbm, wx_hbm, wy_hbm, out_ref, x, y, wx, wy, sems):
    at_core = lax.axis_index("tensor")
    rank = wx.shape[0]
    jobs = []
    for src, w_src, dst, w_dst, row in ((y_hbm, wy_hbm, y, wy, 0), (x_hbm, wx_hbm, x, wx, rank)):
        depth = dst.shape[1]
        for at, size in pieces_of(depth):
            there = pl.multiple_of(at_core * depth + at, 128)
            here = pl.ds(at, size)
            sem = 2 * len(jobs)
            copies = (
                pltpu.make_async_copy(w_src.at[:, pl.ds(there, size)], w_dst.at[:, here], sems.at[sem]),
                pltpu.make_async_copy(src.at[:, here], dst.at[:, here], sems.at[sem + 1]),
            )
            for copy in copies:
                copy.start()
            jobs.append((copies, dst, w_dst, row, at, size))
    totals = {}
    for copies, dst, w_dst, row, at, size in jobs:
        for copy in copies:
            copy.wait()
        here = slice(at, at + size)
        totals.setdefault(row, []).append(dot(w_dst[:, here], dst[:, here], NT))
    for row, parts in totals.items():
        out_ref[row : row + rank, :] = sum_of(parts)


def partial_codes(inputs, out_grads, proj_in_t, proj_out_t):
    tokens, depth_in = inputs.shape
    depth_out = out_grads.shape[1]
    rank = proj_in_t.shape[0]
    copies = 2 * (len(pieces_of(depth_in)) + len(pieces_of(depth_out)))
    return pl.pallas_call(
        codes_kernel,
        out_shape=jax.ShapeDtypeStruct((2 * rank, tokens), jnp.float32),
        in_specs=[HBM] * 4,
        out_specs=VMEM,
        scratch_shapes=[
            pltpu.VMEM((tokens, depth_in), inputs.dtype),
            pltpu.VMEM((tokens, depth_out), out_grads.dtype),
            pltpu.VMEM((rank, depth_in), proj_in_t.dtype),
            pltpu.VMEM((rank, depth_out), proj_out_t.dtype),
            pltpu.SemaphoreType.DMA((copies,)),
        ],
        compiler_params=pltpu.CompilerParams(vmem_limit_bytes=56_000_000),
        name="partial_codes",
    )(inputs, out_grads, proj_in_t, proj_out_t)


def fixed_point(values):
    largest = jnp.max(jnp.abs(values), axis=0, keepdims=True)
    grade = jnp.ceil(jnp.log(jnp.maximum(largest, 1e-30)) * (STEPS / 0.6931471805599453) + 0.01)
    units = values * (TOP * jnp.exp2(grade * (-1.0 / STEPS)))
    units = jnp.clip(jnp.floor(units + 0.5), -TOP, TOP)
    return units.astype(jnp.int32), grade.astype(jnp.int32)


def pack_kernel(mine_ref, other_ref, ids_ref, own_ref, message_ref):
    rows, tokens = mine_ref.shape
    rank = rows // 2
    ids = ids_ref[...]
    onehot = members(ids, DOCS_DEV)
    count = jnp.maximum(jnp.sum(onehot, axis=1, keepdims=True), 1.0)
    weight = jnp.sum(onehot / jnp.sqrt(count), axis=0, keepdims=True)
    grads = mine_ref[:rank, :] + other_ref[:rank, :]
    ins = (mine_ref[rank:, :] + other_ref[rank:, :]) * weight
    own_ref[:rank, :] = grads
    own_ref[rank:, :] = ins
    grad_units, grad_grade = fixed_point(grads)
    in_units, in_grade = fixed_point(ins)
    message_ref[:rank, :] = lax.shift_left(grad_units, 16) | (in_units & 0xFFFF)
    line = lax.broadcasted_iota(jnp.int32, (EXTRA, tokens), 0)
    message_ref[rank:, :] = jnp.where(
        line == 0, ids, jnp.where(line == 1, grad_grade, in_grade)
    )


def pack(mine, other, doc_ids):
    rows, tokens = mine.shape
    rank = rows // 2
    return pl.pallas_call(
        pack_kernel,
        out_shape=(
            jax.ShapeDtypeStruct((rows, tokens), jnp.float32),
            jax.ShapeDtypeStruct((rank + EXTRA, tokens), jnp.int32),
        ),
        in_specs=[VMEM] * 3,
        out_specs=(VMEM, VMEM),
        compiler_params=SMALL,
        name="pack_codes",
    )(mine, other, doc_ids)


def scores_kernel(own_ref, message_ref, queries, scores_ref, grads_ref, ins_ref, feats_ref):
    rows, tokens = own_ref.shape
    rank = rows // 2
    grads = own_ref[:rank, :]
    ins = own_ref[rank:, :]
    onehot = members(message_ref[rank : rank + 1, :], DOCS_DEV)
    for values, ref in ((grads, grads_ref), (ins, ins_ref)):
        high, low = halves(values)
        stacked = jnp.concatenate([high, high, low, low], axis=0)
        ref[...] = stacked.T
    weighted = (grads[:, None, :] * onehot[None, :, :]).reshape(rank * DOCS_DEV, tokens)
    w_high, w_low = halves(weighted)
    i_high, i_low = halves(jnp.concatenate([ins, ins], axis=0))
    feats = dot(
        jnp.concatenate([w_high, w_high, w_low], axis=1),
        jnp.concatenate([i_high, i_low, i_high], axis=1),
        NT,
    )
    feats_ref[...] = jnp.concatenate(halves(feats), axis=1)
    left = lax.broadcasted_iota(jnp.int32, (DOCS_DEV, 2 * rank), 1) < rank
    pairs = [
        jnp.where(
            left,
            feats[i * DOCS_DEV : (i + 1) * DOCS_DEV],
            feats[(i + 1) * DOCS_DEV : (i + 2) * DOCS_DEV],
        )
        for i in range(0, rank, 2)
    ]
    count = queries.shape[0]
    sums = [None] * count
    for n, pair in enumerate(pairs):
        block = queries[:, n * 2 * rank : (n + 1) * 2 * rank]
        for q in range(count):
            term = pair * block[q : q + 1, :]
            sums[q] = term if n == 0 else sums[q] + term
    columns = [jnp.sum(total, axis=1, keepdims=True) for total in sums]
    scores_ref[...] = jnp.concatenate(columns, axis=1) * (1.0 / rank)


def score_docs(own, message, queries):
    rows, tokens = own.shape
    rank = rows // 2
    operand = jax.ShapeDtypeStruct((tokens, 4 * rank), jnp.bfloat16)
    return pl.pallas_call(
        scores_kernel,
        out_shape=(
            jax.ShapeDtypeStruct((DOCS_DEV, queries.shape[0]), jnp.float32),
            operand,
            operand,
            jax.ShapeDtypeStruct((rank * DOCS_DEV, 4 * rank), jnp.bfloat16),
        ),
        in_specs=[VMEM] * 3,
        out_specs=(VMEM,) * 4,
        compiler_params=SMALL,
        cost_estimate=pl.CostEstimate(flops=1 << 26, bytes_accessed=1 << 19, transcendentals=0),
        name="score_docs",
    )(own, message, queries)


def plan(shards):
    half = shards // 2
    if half == 4:
        return [
            (-1, (4, 4), (1, 2), (1,)),
            (-1, (7, 7), (2, 1), (1,)),
            (0, (2, 2), (2, 1), ()),
            (0, (1, 1), (2, 2), ()),
        ]
    direct = [(-1, (half + n,) * 2, (n + 1,) * 2, ()) for n in range(0, half, 2)]
    return direct + [(n, (1, 1), (1, 1), ()) for n in reversed(range(half // 2))]


def origins(shards):
    found = []
    for what, other, own, _ in plan(shards):
        before = found[what] if what >= 0 else ((0, 0), (0, 0))
        found.append([[a ^ b for a, b in zip(*pair)] for pair in zip(before, (other, own))])
    return found


def gram_sum(half, message_ref, grads_ref, ins_ref, parts):
    rank = message_ref.shape[0] - EXTRA
    onehot = members(message_ref[rank : rank + 1, :], DOCS_DEV).astype(jnp.bfloat16)
    doubled = jnp.concatenate([onehot, onehot], axis=1)
    total = None
    for first in range(0, len(parts), 4):
        codes, ids, scales = [], [], []
        for block, place in parts[first : first + 4]:
            codes.append(block[:rank, :])
            ids.append(block[rank : rank + 1, :] + place * DOCS_DEV)
            grades = block[rank + 1 : rank + 2, :] + block[rank + 2 : rank + 3, :]
            scales.append(grades.astype(jnp.float32))
        codes, ids, scales = (jnp.concatenate(part, axis=1) for part in (codes, ids, scales))
        product = None
        for units, left in (
            (lax.shift_right_arithmetic(codes, 16), grads_ref),
            (lax.shift_right_arithmetic(lax.shift_left(codes, 16), 16), ins_ref),
        ):
            high, low = halves(units.astype(jnp.float32))
            part = dot(left[...], jnp.concatenate([high, low, high, low], axis=0), NN)
            product = part if product is None else product * part
        high, low = halves(product)
        by_doc = dot(doubled, jnp.concatenate([high, low], axis=0), NN)
        by_doc = by_doc * (jnp.exp2(scales * (1.0 / STEPS)) * (1.0 / (TOP * TOP * rank * rank)))
        high, low = halves(by_doc)
        theirs = members(ids, half * DOCS_DEV).astype(jnp.bfloat16)
        part = dot(jnp.concatenate([high, low], axis=0), theirs, NT)
        total = part if total is None else total + part
    return total[:DOCS_DEV, :] + total[DOCS_DEV:, :]


def place_of(shard, half, own_half, origin):
    far, near = origin
    return lax.rem(lax.bitwise_xor(shard, jnp.where(own_half, near, far)), half)


def blocks_at(shard, half, own_half, numbers, refs):
    parts = []
    for ref, n in zip(refs, numbers):
        far, near = (jnp.where(shard < half, *bits) for bits in origins(2 * half)[n])
        place = lax.rem(lax.bitwise_xor(shard, jnp.where(own_half, near, far)), half)
        parts.append((ref[...], place))
    return parts


def position(half):
    shard, core = lax.axis_index("dp"), lax.axis_index("tensor")
    return shard, lax.div(shard, half) == core


def early_kernel(half, numbers, message_ref, grads_ref, ins_ref, *refs):
    blocks, sum_ref = refs[:-1], refs[-1]
    shard, own_half = position(half)
    parts = blocks_at(shard, half, own_half, numbers, blocks)
    parts.append((message_ref[...], jnp.where(own_half, lax.rem(shard, half), -half)))
    sum_ref[...] = gram_sum(half, message_ref, grads_ref, ins_ref, parts)


def write_out(total_ref, scores_ref, out_ref, scores_out_ref, sems):
    copies = (
        pltpu.make_async_copy(scores_ref, scores_out_ref, sems.at[0]),
        pltpu.make_async_copy(total_ref, out_ref, sems.at[1]),
    )
    for copy in copies:
        copy.start()
    for copy in copies:
        copy.wait()


def middle_kernel(half, numbers, message_ref, grads_ref, ins_ref, scores_ref, sum_ref, *refs):
    blocks, (out_ref, scores_out_ref, total_ref, sems) = refs[:-4], refs[-4:]
    shard, own_half = position(half)
    parts = blocks_at(shard, half, own_half, numbers, blocks)
    total_ref[...] = sum_ref[...] + gram_sum(half, message_ref, grads_ref, ins_ref, parts)

    @pl.when(own_half)
    def _():
        write_out(total_ref, scores_ref, out_ref, scores_out_ref, sems)


def last_kernel(half, feats_ref, scores_ref, sum_ref, block_ref, *refs):
    out_ref, scores_out_ref, total_ref, sems = refs[-4:]
    shard, own_half = position(half)
    rank = feats_ref.shape[1] // 4

    @pl.when(jnp.logical_not(own_half))
    def _():
        ((block, place),) = blocks_at(shard, half, own_half, [half - 1], [block_ref])
        codes = block[:rank, :]
        grads = lax.shift_right_arithmetic(codes, 16).astype(jnp.float32)
        ins = lax.shift_right_arithmetic(lax.shift_left(codes, 16), 16).astype(jnp.float32)
        high, low = halves(ins)
        shares = dot(feats_ref[...], jnp.concatenate([high, low, high, low], axis=0), NN)
        terms = [shares[i * DOCS_DEV : (i + 1) * DOCS_DEV, :] * grads[i : i + 1, :] for i in range(rank)]
        grades = block[rank + 1 : rank + 2, :] + block[rank + 2 : rank + 3, :]
        scales = jnp.exp2(grades.astype(jnp.float32) * (1.0 / STEPS)) * (1.0 / (TOP * TOP * rank * rank))
        high, low = halves(sum_of(terms) * scales)
        theirs = members(block[rank : rank + 1, :] + place * DOCS_DEV, half * DOCS_DEV).astype(jnp.bfloat16)
        part = dot(jnp.concatenate([high, low], axis=0), theirs, NT)
        total_ref[...] = sum_ref[...] + (part[:DOCS_DEV, :] + part[DOCS_DEV:, :])
        write_out(total_ref, scores_ref, out_ref, scores_out_ref, sems)


def gram_of(message, grads, ins, feats, scores, blocks):
    half = len(blocks)
    rows = jax.ShapeDtypeStruct((DOCS_DEV, half * DOCS_DEV), jnp.float32)
    results = (rows, jax.ShapeDtypeStruct(scores.shape, scores.dtype))
    operands = (message, grads, ins)
    early, middle = range(half - 3), range(half - 3, half - 1)
    so_far = pl.pallas_call(
        functools.partial(early_kernel, half, early),
        out_shape=rows,
        in_specs=[VMEM] * (3 + len(early)),
        out_specs=VMEM,
        compiler_params=SMALL,
        name="gram_early",
    )(*operands, *(blocks[n] for n in early))
    *results_own, so_far = pl.pallas_call(
        functools.partial(middle_kernel, half, middle),
        out_shape=(*results, rows),
        in_specs=[VMEM] * (5 + len(middle)),
        out_specs=(HBM, HBM, VMEM),
        scratch_shapes=[pltpu.SemaphoreType.DMA((2,))],
        compiler_params=SMALL,
        name="gram_middle",
    )(*operands, scores, so_far, *(blocks[n] for n in middle))
    return pl.pallas_call(
        functools.partial(last_kernel, half),
        out_shape=results,
        in_specs=[VMEM] * 4 + [HBM] * 2,
        out_specs=(HBM, HBM),
        scratch_shapes=[pltpu.VMEM(rows.shape, rows.dtype), pltpu.SemaphoreType.DMA((2,))],
        input_output_aliases={4: 0, 5: 1},
        compiler_params=SMALL,
        name="gram_last",
    )(feats, scores, so_far, blocks[-1], *results_own)


def local(inputs, out_grads, proj_in, proj_out, doc_ids, queries):
    shards = lax.axis_size("dp")
    half = shards // 2
    mine = partial_codes(inputs, out_grads, proj_in.T, proj_out.T)
    other = lax.ppermute(mine, "tensor", [(0, 1), (1, 0)])
    own, message = pack(mine, other, doc_ids)
    blocks = []
    for what, far, near, crossed in plan(shards):
        moves = []
        for s in range(shards):
            side = s // half
            for core in range(2):
                to = s ^ (near if core == side else far)[side]
                to_core = core if to // half == side else 1 - core
                by = 1 - core if side in crossed else core
                moves.append((2 * s + by, 2 * to + to_core))
        blocks.append(lax.ppermute(blocks[what] if what >= 0 else message, ("dp", "tensor"), moves))
    scores, grads, ins, feats = score_docs(own, message, queries)
    return gram_of(message, grads, ins, feats, scores, blocks)


def solution(mesh):
    return jax.shard_map(
        local,
        mesh=mesh,
        in_specs=(
            P(("groups", "dp"), "tensor"),
            P(("groups", "dp"), "tensor"),
            P(),
            P(),
            P(("groups", "dp"), None),
            P(),
        ),
        out_specs=(P(("groups", "dp"), "tensor"), P(("groups", "dp"), None)),
        check_vma=False,
    )
```

```python
import functools

import jax
import jax.numpy as jnp
from jax import lax
from jax.experimental import pallas as pl
from jax.experimental.pallas import tpu as pltpu
from jax.sharding import PartitionSpec as P

DOCS_DEV = 8
EXTRA = 8
STEPS = 8.0
TOP = 32767.0
NT = (((1,), (1,)), ((), ()))
NN = (((1,), (0,)), ((), ()))
VMEM = pl.BlockSpec(memory_space=pltpu.VMEM)
HBM = pl.BlockSpec(memory_space=pltpu.HBM)
SMALL = pltpu.CompilerParams(vmem_limit_bytes=16 << 20)

dot = functools.partial(lax.dot_general, preferred_element_type=jnp.float32)


def pieces_of(depth):
    count = -(-depth // 2432)
    size = -(-depth // (count * 128)) * 128
    return [(at, min(size, depth - at)) for at in range(0, depth, size)]


def sum_of(parts):
    while len(parts) > 1:
        parts = [sum(parts[n : n + 2]) for n in range(0, len(parts), 2)]
    return parts[0]


def halves(values):
    high = values.astype(jnp.bfloat16)
    return high, (values - high.astype(jnp.float32)).astype(jnp.bfloat16)


def members(ids, docs):
    rows = lax.broadcasted_iota(jnp.int32, (docs, ids.shape[1]), 0)
    return (rows == ids).astype(jnp.float32)


def codes_kernel(x_hbm, y_hbm, wx_hbm, wy_hbm, out_ref, x, y, wx, wy, sems):
    at_core = lax.axis_index("tensor")
    rank = wx.shape[0]
    jobs = []
    for src, w_src, dst, w_dst, row in ((x_hbm, wx_hbm, x, wx, rank), (y_hbm, wy_hbm, y, wy, 0)):
        depth = dst.shape[1]
        for at, size in pieces_of(depth):
            there = pl.multiple_of(at_core * depth + at, 128)
            here = pl.ds(at, size)
            sem = 2 * len(jobs)
            copies = (
                pltpu.make_async_copy(w_src.at[:, pl.ds(there, size)], w_dst.at[:, here], sems.at[sem]),
                pltpu.make_async_copy(src.at[:, here], dst.at[:, here], sems.at[sem + 1]),
            )
            for copy in copies:
                copy.start()
            jobs.append((copies, dst, w_dst, row, at, size))
    totals = {}
    for copies, dst, w_dst, row, at, size in jobs:
        for copy in copies:
            copy.wait()
        here = slice(at, at + size)
        totals.setdefault(row, []).append(dot(w_dst[:, here], dst[:, here], NT))
    for row, parts in totals.items():
        out_ref[row : row + rank, :] = sum_of(parts)


def partial_codes(inputs, out_grads, proj_in_t, proj_out_t):
    tokens, depth_in = inputs.shape
    depth_out = out_grads.shape[1]
    rank = proj_in_t.shape[0]
    copies = 2 * (len(pieces_of(depth_in)) + len(pieces_of(depth_out)))
    return pl.pallas_call(
        codes_kernel,
        out_shape=jax.ShapeDtypeStruct((2 * rank, tokens), jnp.float32),
        in_specs=[HBM] * 4,
        out_specs=VMEM,
        scratch_shapes=[
            pltpu.VMEM((tokens, depth_in), inputs.dtype),
            pltpu.VMEM((tokens, depth_out), out_grads.dtype),
            pltpu.VMEM((rank, depth_in), proj_in_t.dtype),
            pltpu.VMEM((rank, depth_out), proj_out_t.dtype),
            pltpu.SemaphoreType.DMA((copies,)),
        ],
        compiler_params=pltpu.CompilerParams(vmem_limit_bytes=56_000_000),
        name="partial_codes",
    )(inputs, out_grads, proj_in_t, proj_out_t)


def fixed_point(values):
    largest = jnp.max(jnp.abs(values), axis=0, keepdims=True)
    grade = jnp.ceil(jnp.log(jnp.maximum(largest, 1e-30)) * (STEPS / 0.6931471805599453) + 0.01)
    units = values * (TOP * jnp.exp2(grade * (-1.0 / STEPS)))
    units = jnp.clip(jnp.floor(units + 0.5), -TOP, TOP)
    return units.astype(jnp.int32), grade.astype(jnp.int32)


def pack_kernel(mine_ref, other_ref, ids_ref, own_ref, message_ref):
    rows, tokens = mine_ref.shape
    rank = rows // 2
    ids = ids_ref[...]
    onehot = members(ids, DOCS_DEV)
    count = jnp.maximum(jnp.sum(onehot, axis=1, keepdims=True), 1.0)
    weight = jnp.sum(onehot / jnp.sqrt(count), axis=0, keepdims=True)
    grads = mine_ref[:rank, :] + other_ref[:rank, :]
    ins = (mine_ref[rank:, :] + other_ref[rank:, :]) * weight
    own_ref[:rank, :] = grads
    own_ref[rank:, :] = ins
    grad_units, grad_grade = fixed_point(grads)
    in_units, in_grade = fixed_point(ins)
    message_ref[:rank, :] = lax.shift_left(grad_units, 16) | (in_units & 0xFFFF)
    line = lax.broadcasted_iota(jnp.int32, (EXTRA, tokens), 0)
    message_ref[rank:, :] = jnp.where(
        line == 0, ids, jnp.where(line == 1, grad_grade, in_grade)
    )


def pack(mine, other, doc_ids):
    rows, tokens = mine.shape
    rank = rows // 2
    return pl.pallas_call(
        pack_kernel,
        out_shape=(
            jax.ShapeDtypeStruct((rows, tokens), jnp.float32),
            jax.ShapeDtypeStruct((rank + EXTRA, tokens), jnp.int32),
        ),
        in_specs=[VMEM] * 3,
        out_specs=(VMEM, VMEM),
        compiler_params=SMALL,
        name="pack_codes",
    )(mine, other, doc_ids)


def scores_kernel(own_ref, message_ref, queries, scores_ref, grads_ref, ins_ref, feats_ref):
    rows, tokens = own_ref.shape
    rank = rows // 2
    grads = own_ref[:rank, :]
    ins = own_ref[rank:, :]
    onehot = members(message_ref[rank : rank + 1, :], DOCS_DEV)
    for values, ref in ((grads, grads_ref), (ins, ins_ref)):
        high, low = halves(values)
        stacked = jnp.concatenate([high, high, low, low], axis=0)
        ref[...] = stacked.T
    weighted = (grads[:, None, :] * onehot[None, :, :]).reshape(rank * DOCS_DEV, tokens)
    w_high, w_low = halves(weighted)
    i_high, i_low = halves(jnp.concatenate([ins, ins], axis=0))
    feats = dot(
        jnp.concatenate([w_high, w_high, w_low], axis=1),
        jnp.concatenate([i_high, i_low, i_high], axis=1),
        NT,
    )
    feats_ref[...] = jnp.concatenate(halves(feats), axis=1)
    left = lax.broadcasted_iota(jnp.int32, (DOCS_DEV, 2 * rank), 1) < rank
    pairs = [
        jnp.where(
            left,
            feats[i * DOCS_DEV : (i + 1) * DOCS_DEV],
            feats[(i + 1) * DOCS_DEV : (i + 2) * DOCS_DEV],
        )
        for i in range(0, rank, 2)
    ]
    count = queries.shape[0]
    sums = [None] * count
    for n, pair in enumerate(pairs):
        block = queries[:, n * 2 * rank : (n + 1) * 2 * rank]
        for q in range(count):
            term = pair * block[q : q + 1, :]
            sums[q] = term if n == 0 else sums[q] + term
    columns = [jnp.sum(total, axis=1, keepdims=True) for total in sums]
    scores_ref[...] = jnp.concatenate(columns, axis=1) * (1.0 / rank)


def score_docs(own, message, queries):
    rows, tokens = own.shape
    rank = rows // 2
    operand = jax.ShapeDtypeStruct((tokens, 4 * rank), jnp.bfloat16)
    return pl.pallas_call(
        scores_kernel,
        out_shape=(
            jax.ShapeDtypeStruct((DOCS_DEV, queries.shape[0]), jnp.float32),
            operand,
            operand,
            jax.ShapeDtypeStruct((rank * DOCS_DEV, 4 * rank), jnp.bfloat16),
        ),
        in_specs=[VMEM] * 3,
        out_specs=(VMEM,) * 4,
        compiler_params=SMALL,
        cost_estimate=pl.CostEstimate(flops=1 << 26, bytes_accessed=1 << 19, transcendentals=0),
        name="score_docs",
    )(own, message, queries)


def plan(shards):
    half = shards // 2
    if half == 4:
        return [
            (-1, (4, 4), (1, 1), (1,)),
            (-1, (7, 7), (2, 2), (1,)),
            (0, (2, 1), (2, 2), ()),
            (0, (1, 2), (2, 1), ()),
        ]
    direct = [(-1, (half + n,) * 2, (n + 1,) * 2, ()) for n in range(0, half, 2)]
    return direct + [(n, (1, 1), (1, 1), ()) for n in reversed(range(half // 2))]


def origins(shards):
    found = []
    for what, other, own, _ in plan(shards):
        before = found[what] if what >= 0 else ((0, 0), (0, 0))
        found.append([[a ^ b for a, b in zip(*pair)] for pair in zip(before, (other, own))])
    return found


def gram_sum(half, message_ref, grads_ref, ins_ref, parts):
    rank = message_ref.shape[0] - EXTRA
    onehot = members(message_ref[rank : rank + 1, :], DOCS_DEV).astype(jnp.bfloat16)
    doubled = jnp.concatenate([onehot, onehot], axis=1)
    total = None
    for first in range(0, len(parts), 4):
        codes, ids, scales = [], [], []
        for block, place in parts[first : first + 4]:
            codes.append(block[:rank, :])
            ids.append(block[rank : rank + 1, :] + place * DOCS_DEV)
            grades = block[rank + 1 : rank + 2, :] + block[rank + 2 : rank + 3, :]
            scales.append(grades.astype(jnp.float32))
        codes, ids, scales = (jnp.concatenate(part, axis=1) for part in (codes, ids, scales))
        product = None
        for units, left in (
            (lax.shift_right_arithmetic(codes, 16), grads_ref),
            (lax.shift_right_arithmetic(lax.shift_left(codes, 16), 16), ins_ref),
        ):
            high, low = halves(units.astype(jnp.float32))
            part = dot(left[...], jnp.concatenate([high, low, high, low], axis=0), NN)
            product = part if product is None else product * part
        high, low = halves(product)
        by_doc = dot(doubled, jnp.concatenate([high, low], axis=0), NN)
        by_doc = by_doc * (jnp.exp2(scales * (1.0 / STEPS)) * (1.0 / (TOP * TOP * rank * rank)))
        high, low = halves(by_doc)
        theirs = members(ids, half * DOCS_DEV).astype(jnp.bfloat16)
        part = dot(jnp.concatenate([high, low], axis=0), theirs, NT)
        total = part if total is None else total + part
    return total[:DOCS_DEV, :] + total[DOCS_DEV:, :]


def place_of(shard, half, own_half, origin):
    far, near = origin
    return lax.rem(lax.bitwise_xor(shard, jnp.where(own_half, near, far)), half)


def blocks_at(shard, half, own_half, numbers, refs):
    parts = []
    for ref, n in zip(refs, numbers):
        far, near = (jnp.where(shard < half, *bits) for bits in origins(2 * half)[n])
        place = lax.rem(lax.bitwise_xor(shard, jnp.where(own_half, near, far)), half)
        parts.append((ref[...], place))
    return parts


def position(half):
    shard, core = lax.axis_index("dp"), lax.axis_index("tensor")
    return shard, lax.div(shard, half) == core


def early_kernel(half, numbers, message_ref, grads_ref, ins_ref, *refs):
    blocks, sum_ref = refs[:-1], refs[-1]
    shard, own_half = position(half)
    parts = blocks_at(shard, half, own_half, numbers, blocks)
    parts.append((message_ref[...], jnp.where(own_half, lax.rem(shard, half), -half)))
    sum_ref[...] = gram_sum(half, message_ref, grads_ref, ins_ref, parts)


def write_out(total_ref, scores_ref, out_ref, scores_out_ref, sems):
    copies = (
        pltpu.make_async_copy(scores_ref, scores_out_ref, sems.at[0]),
        pltpu.make_async_copy(total_ref, out_ref, sems.at[1]),
    )
    for copy in copies:
        copy.start()
    for copy in copies:
        copy.wait()


def middle_kernel(half, numbers, message_ref, grads_ref, ins_ref, scores_ref, sum_ref, *refs):
    blocks, (out_ref, scores_out_ref, total_ref, sems) = refs[:-4], refs[-4:]
    shard, own_half = position(half)
    parts = blocks_at(shard, half, own_half, numbers, blocks)
    total_ref[...] = sum_ref[...] + gram_sum(half, message_ref, grads_ref, ins_ref, parts)

    @pl.when(own_half)
    def _():
        write_out(total_ref, scores_ref, out_ref, scores_out_ref, sems)


def last_kernel(half, feats_ref, scores_ref, sum_ref, block_ref, *refs):
    out_ref, scores_out_ref, total_ref, sems = refs[-4:]
    shard, own_half = position(half)
    rank = feats_ref.shape[1] // 4

    @pl.when(jnp.logical_not(own_half))
    def _():
        ((block, place),) = blocks_at(shard, half, own_half, [half - 1], [block_ref])
        codes = block[:rank, :]
        grads = lax.shift_right_arithmetic(codes, 16).astype(jnp.float32)
        ins = lax.shift_right_arithmetic(lax.shift_left(codes, 16), 16).astype(jnp.float32)
        high, low = halves(ins)
        shares = dot(feats_ref[...], jnp.concatenate([high, low, high, low], axis=0), NN)
        terms = [shares[i * DOCS_DEV : (i + 1) * DOCS_DEV, :] * grads[i : i + 1, :] for i in range(rank)]
        grades = block[rank + 1 : rank + 2, :] + block[rank + 2 : rank + 3, :]
        scales = jnp.exp2(grades.astype(jnp.float32) * (1.0 / STEPS)) * (1.0 / (TOP * TOP * rank * rank))
        high, low = halves(sum_of(terms) * scales)
        theirs = members(block[rank : rank + 1, :] + place * DOCS_DEV, half * DOCS_DEV).astype(jnp.bfloat16)
        part = dot(jnp.concatenate([high, low], axis=0), theirs, NT)
        total_ref[...] = sum_ref[...] + (part[:DOCS_DEV, :] + part[DOCS_DEV:, :])
        write_out(total_ref, scores_ref, out_ref, scores_out_ref, sems)


def gram_of(message, grads, ins, feats, scores, blocks):
    half = len(blocks)
    rows = jax.ShapeDtypeStruct((DOCS_DEV, half * DOCS_DEV), jnp.float32)
    results = (rows, jax.ShapeDtypeStruct(scores.shape, scores.dtype))
    operands = (message, grads, ins)
    early, middle = range(half - 3), range(half - 3, half - 1)
    so_far = pl.pallas_call(
        functools.partial(early_kernel, half, early),
        out_shape=rows,
        in_specs=[VMEM] * (3 + len(early)),
        out_specs=VMEM,
        compiler_params=SMALL,
        name="gram_early",
    )(*operands, *(blocks[n] for n in early))
    *results_own, so_far = pl.pallas_call(
        functools.partial(middle_kernel, half, middle),
        out_shape=(*results, rows),
        in_specs=[VMEM] * (5 + len(middle)),
        out_specs=(HBM, HBM, VMEM),
        scratch_shapes=[pltpu.SemaphoreType.DMA((2,))],
        compiler_params=SMALL,
        name="gram_middle",
    )(*operands, scores, so_far, *(blocks[n] for n in middle))
    return pl.pallas_call(
        functools.partial(last_kernel, half),
        out_shape=results,
        in_specs=[VMEM] * 4 + [HBM] * 2,
        out_specs=(HBM, HBM),
        scratch_shapes=[pltpu.VMEM(rows.shape, rows.dtype), pltpu.SemaphoreType.DMA((2,))],
        input_output_aliases={4: 0, 5: 1},
        compiler_params=SMALL,
        name="gram_last",
    )(feats, scores, so_far, blocks[-1], *results_own)


def local(inputs, out_grads, proj_in, proj_out, doc_ids, queries):
    shards = lax.axis_size("dp")
    half = shards // 2
    mine = partial_codes(inputs, out_grads, proj_in.T, proj_out.T)
    other = lax.ppermute(mine, "tensor", [(0, 1), (1, 0)])
    own, message = pack(mine, other, doc_ids)
    blocks = []
    for what, far, near, crossed in plan(shards):
        moves = []
        for s in range(shards):
            side = s // half
            for core in range(2):
                to = s ^ (near if core == side else far)[side]
                to_core = core if to // half == side else 1 - core
                by = 1 - core if side in crossed else core
                moves.append((2 * s + by, 2 * to + to_core))
        blocks.append(lax.ppermute(blocks[what] if what >= 0 else message, ("dp", "tensor"), moves))
    scores, grads, ins, feats = score_docs(own, message, queries)
    return gram_of(message, grads, ins, feats, scores, blocks)


def solution(mesh):
    return jax.shard_map(
        local,
        mesh=mesh,
        in_specs=(
            P(("groups", "dp"), "tensor"),
            P(("groups", "dp"), "tensor"),
            P(),
            P(),
            P(("groups", "dp"), None),
            P(),
        ),
        out_specs=(P(("groups", "dp"), "tensor"), P(("groups", "dp"), None)),
        check_vma=False,
    )
```

```python
import functools

import jax
import jax.numpy as jnp
from jax import lax
from jax.experimental import pallas as pl
from jax.experimental.pallas import tpu as pltpu
from jax.sharding import PartitionSpec as P

DOCS_DEV = 8
EXTRA = 8
STEPS = 8.0
TOP = 32767.0
NT = (((1,), (1,)), ((), ()))
NN = (((1,), (0,)), ((), ()))
VMEM = pl.BlockSpec(memory_space=pltpu.VMEM)
HBM = pl.BlockSpec(memory_space=pltpu.HBM)
SMALL = pltpu.CompilerParams(vmem_limit_bytes=16 << 20)

dot = functools.partial(lax.dot_general, preferred_element_type=jnp.float32)


def pieces_of(depth):
    count = -(-depth // 2432)
    size = -(-depth // (count * 128)) * 128
    return [(at, min(size, depth - at)) for at in range(0, depth, size)]


def sum_of(parts):
    while len(parts) > 1:
        parts = [sum(parts[n : n + 2]) for n in range(0, len(parts), 2)]
    return parts[0]


def halves(values):
    high = values.astype(jnp.bfloat16)
    return high, (values - high.astype(jnp.float32)).astype(jnp.bfloat16)


def members(ids, docs):
    rows = lax.broadcasted_iota(jnp.int32, (docs, ids.shape[1]), 0)
    return (rows == ids).astype(jnp.float32)


def codes_kernel(x_hbm, y_hbm, wx_hbm, wy_hbm, out_ref, x, y, wx, wy, sems):
    at_core = lax.axis_index("tensor")
    rank = wx.shape[0]
    jobs = []
    for src, w_src, dst, w_dst, row in ((y_hbm, wy_hbm, y, wy, 0), (x_hbm, wx_hbm, x, wx, rank)):
        depth = dst.shape[1]
        for at, size in pieces_of(depth):
            there = pl.multiple_of(at_core * depth + at, 128)
            here = pl.ds(at, size)
            sem = 2 * len(jobs)
            copies = (
                pltpu.make_async_copy(w_src.at[:, pl.ds(there, size)], w_dst.at[:, here], sems.at[sem]),
                pltpu.make_async_copy(src.at[:, here], dst.at[:, here], sems.at[sem + 1]),
            )
            for copy in copies:
                copy.start()
            jobs.append((copies, dst, w_dst, row, at, size))
    totals = {}
    for copies, dst, w_dst, row, at, size in jobs:
        for copy in copies:
            copy.wait()
        here = slice(at, at + size)
        totals.setdefault(row, []).append(dot(w_dst[:, here], dst[:, here], NT))
    for row, parts in totals.items():
        out_ref[row : row + rank, :] = sum_of(parts)


def partial_codes(inputs, out_grads, proj_in_t, proj_out_t):
    tokens, depth_in = inputs.shape
    depth_out = out_grads.shape[1]
    rank = proj_in_t.shape[0]
    copies = 2 * (len(pieces_of(depth_in)) + len(pieces_of(depth_out)))
    return pl.pallas_call(
        codes_kernel,
        out_shape=jax.ShapeDtypeStruct((2 * rank, tokens), jnp.float32),
        in_specs=[HBM] * 4,
        out_specs=VMEM,
        scratch_shapes=[
            pltpu.VMEM((tokens, depth_in), inputs.dtype),
            pltpu.VMEM((tokens, depth_out), out_grads.dtype),
            pltpu.VMEM((rank, depth_in), proj_in_t.dtype),
            pltpu.VMEM((rank, depth_out), proj_out_t.dtype),
            pltpu.SemaphoreType.DMA((copies,)),
        ],
        compiler_params=pltpu.CompilerParams(vmem_limit_bytes=56_000_000),
        name="partial_codes",
    )(inputs, out_grads, proj_in_t, proj_out_t)


def fixed_point(values):
    largest = jnp.max(jnp.abs(values), axis=0, keepdims=True)
    grade = jnp.ceil(jnp.log(jnp.maximum(largest, 1e-30)) * (STEPS / 0.6931471805599453) + 0.01)
    units = values * (TOP * jnp.exp2(grade * (-1.0 / STEPS)))
    units = jnp.clip(jnp.floor(units + 0.5), -TOP, TOP)
    return units.astype(jnp.int32), grade.astype(jnp.int32)


def pack_kernel(mine_ref, other_ref, ids_ref, own_ref, message_ref):
    rows, tokens = mine_ref.shape
    rank = rows // 2
    ids = ids_ref[...]
    onehot = members(ids, DOCS_DEV)
    count = jnp.maximum(jnp.sum(onehot, axis=1, keepdims=True), 1.0)
    weight = jnp.sum(onehot / jnp.sqrt(count), axis=0, keepdims=True)
    grads = mine_ref[:rank, :] + other_ref[:rank, :]
    ins = (mine_ref[rank:, :] + other_ref[rank:, :]) * weight
    own_ref[:rank, :] = grads
    own_ref[rank:, :] = ins
    grad_units, grad_grade = fixed_point(grads)
    in_units, in_grade = fixed_point(ins)
    message_ref[:rank, :] = lax.shift_left(grad_units, 16) | (in_units & 0xFFFF)
    line = lax.broadcasted_iota(jnp.int32, (EXTRA, tokens), 0)
    message_ref[rank:, :] = jnp.where(
        line == 0, ids, jnp.where(line == 1, grad_grade, in_grade)
    )


def pack(mine, other, doc_ids):
    rows, tokens = mine.shape
    rank = rows // 2
    return pl.pallas_call(
        pack_kernel,
        out_shape=(
            jax.ShapeDtypeStruct((rows, tokens), jnp.float32),
            jax.ShapeDtypeStruct((rank + EXTRA, tokens), jnp.int32),
        ),
        in_specs=[VMEM] * 3,
        out_specs=(VMEM, VMEM),
        compiler_params=SMALL,
        name="pack_codes",
    )(mine, other, doc_ids)


def scores_kernel(own_ref, message_ref, queries, scores_ref, grads_ref, ins_ref, feats_ref):
    rows, tokens = own_ref.shape
    rank = rows // 2
    grads = own_ref[:rank, :]
    ins = own_ref[rank:, :]
    onehot = members(message_ref[rank : rank + 1, :], DOCS_DEV)
    for values, ref in ((grads, grads_ref), (ins, ins_ref)):
        high, low = halves(values)
        stacked = jnp.concatenate([high, high, low, low], axis=0)
        ref[...] = stacked.T
    weighted = (grads[:, None, :] * onehot[None, :, :]).reshape(rank * DOCS_DEV, tokens)
    w_high, w_low = halves(weighted)
    i_high, i_low = halves(jnp.concatenate([ins, ins], axis=0))
    feats = dot(
        jnp.concatenate([w_high, w_high, w_low], axis=1),
        jnp.concatenate([i_high, i_low, i_high], axis=1),
        NT,
    )
    feats_ref[...] = jnp.concatenate(halves(feats), axis=1)
    left = lax.broadcasted_iota(jnp.int32, (DOCS_DEV, 2 * rank), 1) < rank
    pairs = [
        jnp.where(
            left,
            feats[i * DOCS_DEV : (i + 1) * DOCS_DEV],
            feats[(i + 1) * DOCS_DEV : (i + 2) * DOCS_DEV],
        )
        for i in range(0, rank, 2)
    ]
    count = queries.shape[0]
    sums = [None] * count
    for n, pair in enumerate(pairs):
        block = queries[:, n * 2 * rank : (n + 1) * 2 * rank]
        for q in range(count):
            term = pair * block[q : q + 1, :]
            sums[q] = term if n == 0 else sums[q] + term
    columns = [jnp.sum(total, axis=1, keepdims=True) for total in sums]
    scores_ref[...] = jnp.concatenate(columns, axis=1) * (1.0 / rank)


def score_docs(own, message, queries):
    rows, tokens = own.shape
    rank = rows // 2
    operand = jax.ShapeDtypeStruct((tokens, 4 * rank), jnp.bfloat16)
    return pl.pallas_call(
        scores_kernel,
        out_shape=(
            jax.ShapeDtypeStruct((DOCS_DEV, queries.shape[0]), jnp.float32),
            operand,
            operand,
            jax.ShapeDtypeStruct((rank * DOCS_DEV, 4 * rank), jnp.bfloat16),
        ),
        in_specs=[VMEM] * 3,
        out_specs=(VMEM,) * 4,
        compiler_params=SMALL,
        cost_estimate=pl.CostEstimate(flops=1 << 26, bytes_accessed=1 << 19, transcendentals=0),
        name="score_docs",
    )(own, message, queries)


def plan(shards):
    half = shards // 2
    if half == 4:
        return [
            (-1, (4, 4), (1, 1), (1,)),
            (-1, (7, 7), (2, 2), (1,)),
            (0, (2, 1), (2, 2), ()),
            (0, (1, 2), (2, 1), ()),
        ]
    direct = [(-1, (half + n,) * 2, (n + 1,) * 2, ()) for n in range(0, half, 2)]
    return direct + [(n, (1, 1), (1, 1), ()) for n in reversed(range(half // 2))]


def origins(shards):
    found = []
    for what, other, own, _ in plan(shards):
        before = found[what] if what >= 0 else ((0, 0), (0, 0))
        found.append([[a ^ b for a, b in zip(*pair)] for pair in zip(before, (other, own))])
    return found


def gram_sum(half, message_ref, grads_ref, ins_ref, parts):
    rank = message_ref.shape[0] - EXTRA
    onehot = members(message_ref[rank : rank + 1, :], DOCS_DEV).astype(jnp.bfloat16)
    doubled = jnp.concatenate([onehot, onehot], axis=1)
    total = None
    for first in range(0, len(parts), 4):
        codes, ids, scales = [], [], []
        for block, place in parts[first : first + 4]:
            codes.append(block[:rank, :])
            ids.append(block[rank : rank + 1, :] + place * DOCS_DEV)
            grades = block[rank + 1 : rank + 2, :] + block[rank + 2 : rank + 3, :]
            scales.append(grades.astype(jnp.float32))
        codes, ids, scales = (jnp.concatenate(part, axis=1) for part in (codes, ids, scales))
        product = None
        for units, left in (
            (lax.shift_right_arithmetic(codes, 16), grads_ref),
            (lax.shift_right_arithmetic(lax.shift_left(codes, 16), 16), ins_ref),
        ):
            high, low = halves(units.astype(jnp.float32))
            part = dot(left[...], jnp.concatenate([high, low, high, low], axis=0), NN)
            product = part if product is None else product * part
        high, low = halves(product)
        by_doc = dot(doubled, jnp.concatenate([high, low], axis=0), NN)
        by_doc = by_doc * (jnp.exp2(scales * (1.0 / STEPS)) * (1.0 / (TOP * TOP * rank * rank)))
        high, low = halves(by_doc)
        theirs = members(ids, half * DOCS_DEV).astype(jnp.bfloat16)
        part = dot(jnp.concatenate([high, low], axis=0), theirs, NT)
        total = part if total is None else total + part
    return total[:DOCS_DEV, :] + total[DOCS_DEV:, :]


def place_of(shard, half, own_half, origin):
    far, near = origin
    return lax.rem(lax.bitwise_xor(shard, jnp.where(own_half, near, far)), half)


def blocks_at(shard, half, own_half, numbers, refs):
    parts = []
    for ref, n in zip(refs, numbers):
        far, near = (jnp.where(shard < half, *bits) for bits in origins(2 * half)[n])
        place = lax.rem(lax.bitwise_xor(shard, jnp.where(own_half, near, far)), half)
        parts.append((ref[...], place))
    return parts


def position(half):
    shard, core = lax.axis_index("dp"), lax.axis_index("tensor")
    return shard, lax.div(shard, half) == core


def early_kernel(half, numbers, message_ref, grads_ref, ins_ref, *refs):
    blocks, sum_ref = refs[:-1], refs[-1]
    shard, own_half = position(half)
    parts = blocks_at(shard, half, own_half, numbers, blocks)
    parts.append((message_ref[...], jnp.where(own_half, lax.rem(shard, half), -half)))
    sum_ref[...] = gram_sum(half, message_ref, grads_ref, ins_ref, parts)


def write_out(total_ref, scores_ref, out_ref, scores_out_ref, sems):
    copies = (
        pltpu.make_async_copy(scores_ref, scores_out_ref, sems.at[0]),
        pltpu.make_async_copy(total_ref, out_ref, sems.at[1]),
    )
    for copy in copies:
        copy.start()
    for copy in copies:
        copy.wait()


def middle_kernel(half, numbers, message_ref, grads_ref, ins_ref, scores_ref, sum_ref, *refs):
    blocks, (out_ref, scores_out_ref, total_ref, sems) = refs[:-4], refs[-4:]
    shard, own_half = position(half)
    parts = blocks_at(shard, half, own_half, numbers, blocks)
    total_ref[...] = sum_ref[...] + gram_sum(half, message_ref, grads_ref, ins_ref, parts)

    @pl.when(own_half)
    def _():
        write_out(total_ref, scores_ref, out_ref, scores_out_ref, sems)


def last_kernel(half, feats_ref, scores_ref, sum_ref, block_ref, *refs):
    out_ref, scores_out_ref, total_ref, sems = refs[-4:]
    shard, own_half = position(half)
    rank = feats_ref.shape[1] // 4

    @pl.when(jnp.logical_not(own_half))
    def _():
        ((block, place),) = blocks_at(shard, half, own_half, [half - 1], [block_ref])
        codes = block[:rank, :]
        grads = lax.shift_right_arithmetic(codes, 16).astype(jnp.float32)
        ins = lax.shift_right_arithmetic(lax.shift_left(codes, 16), 16).astype(jnp.float32)
        high, low = halves(ins)
        right = jnp.concatenate([high, low, high, low], axis=0)
        count = rank // 4
        terms = []
        for first in range(0, rank, count):
            shares = dot(feats_ref[first * DOCS_DEV : (first + count) * DOCS_DEV, :], right, NN)
            terms.append(
                sum_of(
                    [
                        shares[n * DOCS_DEV : (n + 1) * DOCS_DEV, :] * grads[first + n : first + n + 1, :]
                        for n in range(count)
                    ]
                )
            )
        grades = block[rank + 1 : rank + 2, :] + block[rank + 2 : rank + 3, :]
        scales = jnp.exp2(grades.astype(jnp.float32) * (1.0 / STEPS)) * (1.0 / (TOP * TOP * rank * rank))
        high, low = halves(sum_of(terms) * scales)
        theirs = members(block[rank : rank + 1, :] + place * DOCS_DEV, half * DOCS_DEV).astype(jnp.bfloat16)
        part = dot(jnp.concatenate([high, low], axis=0), theirs, NT)
        total_ref[...] = sum_ref[...] + (part[:DOCS_DEV, :] + part[DOCS_DEV:, :])
        write_out(total_ref, scores_ref, out_ref, scores_out_ref, sems)


def gram_of(message, grads, ins, feats, scores, blocks):
    half = len(blocks)
    rows = jax.ShapeDtypeStruct((DOCS_DEV, half * DOCS_DEV), jnp.float32)
    results = (rows, jax.ShapeDtypeStruct(scores.shape, scores.dtype))
    operands = (message, grads, ins)
    early, middle = range(half - 3), range(half - 3, half - 1)
    so_far = pl.pallas_call(
        functools.partial(early_kernel, half, early),
        out_shape=rows,
        in_specs=[VMEM] * (3 + len(early)),
        out_specs=VMEM,
        compiler_params=SMALL,
        name="gram_early",
    )(*operands, *(blocks[n] for n in early))
    *results_own, so_far = pl.pallas_call(
        functools.partial(middle_kernel, half, middle),
        out_shape=(*results, rows),
        in_specs=[VMEM] * (5 + len(middle)),
        out_specs=(HBM, HBM, VMEM),
        scratch_shapes=[pltpu.SemaphoreType.DMA((2,))],
        compiler_params=SMALL,
        name="gram_middle",
    )(*operands, scores, so_far, *(blocks[n] for n in middle))
    return pl.pallas_call(
        functools.partial(last_kernel, half),
        out_shape=results,
        in_specs=[VMEM] * 4 + [HBM] * 2,
        out_specs=(HBM, HBM),
        scratch_shapes=[pltpu.VMEM(rows.shape, rows.dtype), pltpu.SemaphoreType.DMA((2,))],
        input_output_aliases={4: 0, 5: 1},
        compiler_params=SMALL,
        name="gram_last",
    )(feats, scores, so_far, blocks[-1], *results_own)


def local(inputs, out_grads, proj_in, proj_out, doc_ids, queries):
    shards = lax.axis_size("dp")
    half = shards // 2
    mine = partial_codes(inputs, out_grads, proj_in.T, proj_out.T)
    other = lax.ppermute(mine, "tensor", [(0, 1), (1, 0)])
    own, message = pack(mine, other, doc_ids)
    blocks = []
    for what, far, near, crossed in plan(shards):
        moves = []
        for s in range(shards):
            side = s // half
            for core in range(2):
                to = s ^ (near if core == side else far)[side]
                to_core = core if to // half == side else 1 - core
                by = 1 - core if side in crossed else core
                moves.append((2 * s + by, 2 * to + to_core))
        blocks.append(lax.ppermute(blocks[what] if what >= 0 else message, ("dp", "tensor"), moves))
    scores, grads, ins, feats = score_docs(own, message, queries)
    return gram_of(message, grads, ins, feats, scores, blocks)


def solution(mesh):
    return jax.shard_map(
        local,
        mesh=mesh,
        in_specs=(
            P(("groups", "dp"), "tensor"),
            P(("groups", "dp"), "tensor"),
            P(),
            P(),
            P(("groups", "dp"), None),
            P(),
        ),
        out_specs=(P(("groups", "dp"), "tensor"), P(("groups", "dp"), None)),
        check_vma=False,
    )
```

```python
import functools

import jax
import jax.numpy as jnp
from jax import lax
from jax.experimental import pallas as pl
from jax.experimental.pallas import tpu as pltpu
from jax.sharding import PartitionSpec as P

DOCS_DEV = 8
EXTRA = 8
STEPS = 8.0
TOP = 32767.0
NT = (((1,), (1,)), ((), ()))
NN = (((1,), (0,)), ((), ()))
VMEM = pl.BlockSpec(memory_space=pltpu.VMEM)
HBM = pl.BlockSpec(memory_space=pltpu.HBM)
SMALL = pltpu.CompilerParams(vmem_limit_bytes=16 << 20)

dot = functools.partial(lax.dot_general, preferred_element_type=jnp.float32)


def pieces_of(depth):
    count = -(-depth // 2432)
    size = -(-depth // (count * 128)) * 128
    return [(at, min(size, depth - at)) for at in range(0, depth, size)]


def sum_of(parts):
    while len(parts) > 1:
        parts = [sum(parts[n : n + 2]) for n in range(0, len(parts), 2)]
    return parts[0]


def halves(values):
    high = values.astype(jnp.bfloat16)
    return high, (values - high.astype(jnp.float32)).astype(jnp.bfloat16)


def members(ids, docs):
    rows = lax.broadcasted_iota(jnp.int32, (docs, ids.shape[1]), 0)
    return (rows == ids).astype(jnp.float32)


def codes_kernel(x_hbm, y_hbm, wx_hbm, wy_hbm, out_ref, x, y, wx, wy, sems):
    at_core = lax.axis_index("tensor")
    rank = wx.shape[0]
    jobs = []
    for src, w_src, dst, w_dst, row in ((y_hbm, wy_hbm, y, wy, 0), (x_hbm, wx_hbm, x, wx, rank)):
        depth = dst.shape[1]
        for at, size in pieces_of(depth):
            there = pl.multiple_of(at_core * depth + at, 128)
            here = pl.ds(at, size)
            sem = 2 * len(jobs)
            copies = (
                pltpu.make_async_copy(w_src.at[:, pl.ds(there, size)], w_dst.at[:, here], sems.at[sem]),
                pltpu.make_async_copy(src.at[:, here], dst.at[:, here], sems.at[sem + 1]),
            )
            for priority, copy in zip((1, 0), copies):
                copy.start(priority=priority)
            jobs.append((copies, dst, w_dst, row, at, size))
    totals = {}
    for copies, dst, w_dst, row, at, size in jobs:
        for copy in copies:
            copy.wait()
        here = slice(at, at + size)
        totals.setdefault(row, []).append(dot(w_dst[:, here], dst[:, here], NT))
    for row, parts in totals.items():
        out_ref[row : row + rank, :] = sum_of(parts)


def partial_codes(inputs, out_grads, proj_in_t, proj_out_t):
    tokens, depth_in = inputs.shape
    depth_out = out_grads.shape[1]
    rank = proj_in_t.shape[0]
    copies = 2 * (len(pieces_of(depth_in)) + len(pieces_of(depth_out)))
    return pl.pallas_call(
        codes_kernel,
        out_shape=jax.ShapeDtypeStruct((2 * rank, tokens), jnp.float32),
        in_specs=[HBM] * 4,
        out_specs=VMEM,
        scratch_shapes=[
            pltpu.VMEM((tokens, depth_in), inputs.dtype),
            pltpu.VMEM((tokens, depth_out), out_grads.dtype),
            pltpu.VMEM((rank, depth_in), proj_in_t.dtype),
            pltpu.VMEM((rank, depth_out), proj_out_t.dtype),
            pltpu.SemaphoreType.DMA((copies,)),
        ],
        compiler_params=pltpu.CompilerParams(vmem_limit_bytes=56_000_000),
        name="partial_codes",
    )(inputs, out_grads, proj_in_t, proj_out_t)


def fixed_point(values):
    largest = jnp.max(jnp.abs(values), axis=0, keepdims=True)
    grade = jnp.ceil(jnp.log(jnp.maximum(largest, 1e-30)) * (STEPS / 0.6931471805599453) + 0.01)
    units = values * (TOP * jnp.exp2(grade * (-1.0 / STEPS)))
    units = jnp.clip(jnp.floor(units + 0.5), -TOP, TOP)
    return units.astype(jnp.int32), grade.astype(jnp.int32)


def pack_kernel(mine_ref, other_ref, ids_ref, own_ref, message_ref):
    rows, tokens = mine_ref.shape
    rank = rows // 2
    ids = ids_ref[...]
    onehot = members(ids, DOCS_DEV)
    count = jnp.maximum(jnp.sum(onehot, axis=1, keepdims=True), 1.0)
    weight = jnp.sum(onehot / jnp.sqrt(count), axis=0, keepdims=True)
    grads = mine_ref[:rank, :] + other_ref[:rank, :]
    ins = (mine_ref[rank:, :] + other_ref[rank:, :]) * weight
    own_ref[:rank, :] = grads
    own_ref[rank:, :] = ins
    grad_units, grad_grade = fixed_point(grads)
    in_units, in_grade = fixed_point(ins)
    message_ref[:rank, :] = lax.shift_left(grad_units, 16) | (in_units & 0xFFFF)
    line = lax.broadcasted_iota(jnp.int32, (EXTRA, tokens), 0)
    message_ref[rank:, :] = jnp.where(
        line == 0, ids, jnp.where(line == 1, grad_grade, in_grade)
    )


def pack(mine, other, doc_ids):
    rows, tokens = mine.shape
    rank = rows // 2
    return pl.pallas_call(
        pack_kernel,
        out_shape=(
            jax.ShapeDtypeStruct((rows, tokens), jnp.float32),
            jax.ShapeDtypeStruct((rank + EXTRA, tokens), jnp.int32),
        ),
        in_specs=[VMEM] * 3,
        out_specs=(VMEM, VMEM),
        compiler_params=SMALL,
        name="pack_codes",
    )(mine, other, doc_ids)


def scores_kernel(own_ref, message_ref, queries, scores_ref, grads_ref, ins_ref, feats_ref):
    rows, tokens = own_ref.shape
    rank = rows // 2
    grads = own_ref[:rank, :]
    ins = own_ref[rank:, :]
    onehot = members(message_ref[rank : rank + 1, :], DOCS_DEV)
    for values, ref in ((grads, grads_ref), (ins, ins_ref)):
        high, low = halves(values)
        stacked = jnp.concatenate([high, high, low, low], axis=0)
        ref[...] = stacked.T
    weighted = (grads[:, None, :] * onehot[None, :, :]).reshape(rank * DOCS_DEV, tokens)
    w_high, w_low = halves(weighted)
    i_high, i_low = halves(jnp.concatenate([ins, ins], axis=0))
    feats = dot(
        jnp.concatenate([w_high, w_high, w_low], axis=1),
        jnp.concatenate([i_high, i_low, i_high], axis=1),
        NT,
    )
    feats_ref[...] = jnp.concatenate(halves(feats), axis=1)
    left = lax.broadcasted_iota(jnp.int32, (DOCS_DEV, 2 * rank), 1) < rank
    pairs = [
        jnp.where(
            left,
            feats[i * DOCS_DEV : (i + 1) * DOCS_DEV],
            feats[(i + 1) * DOCS_DEV : (i + 2) * DOCS_DEV],
        )
        for i in range(0, rank, 2)
    ]
    count = queries.shape[0]
    sums = [None] * count
    for n, pair in enumerate(pairs):
        block = queries[:, n * 2 * rank : (n + 1) * 2 * rank]
        for q in range(count):
            term = pair * block[q : q + 1, :]
            sums[q] = term if n == 0 else sums[q] + term
    columns = [jnp.sum(total, axis=1, keepdims=True) for total in sums]
    scores_ref[...] = jnp.concatenate(columns, axis=1) * (1.0 / rank)


def score_docs(own, message, queries):
    rows, tokens = own.shape
    rank = rows // 2
    operand = jax.ShapeDtypeStruct((tokens, 4 * rank), jnp.bfloat16)
    return pl.pallas_call(
        scores_kernel,
        out_shape=(
            jax.ShapeDtypeStruct((DOCS_DEV, queries.shape[0]), jnp.float32),
            operand,
            operand,
            jax.ShapeDtypeStruct((rank * DOCS_DEV, 4 * rank), jnp.bfloat16),
        ),
        in_specs=[VMEM] * 3,
        out_specs=(VMEM,) * 4,
        compiler_params=SMALL,
        cost_estimate=pl.CostEstimate(flops=1 << 26, bytes_accessed=1 << 19, transcendentals=0),
        name="score_docs",
    )(own, message, queries)


def plan(shards):
    half = shards // 2
    if half == 4:
        return [
            (-1, (4, 4), (1, 1), (1,)),
            (-1, (7, 7), (2, 2), (1,)),
            (0, (2, 1), (2, 2), ()),
            (0, (1, 2), (2, 1), ()),
        ]
    direct = [(-1, (half + n,) * 2, (n + 1,) * 2, ()) for n in range(0, half, 2)]
    return direct + [(n, (1, 1), (1, 1), ()) for n in reversed(range(half // 2))]


def origins(shards):
    found = []
    for what, other, own, _ in plan(shards):
        before = found[what] if what >= 0 else ((0, 0), (0, 0))
        found.append([[a ^ b for a, b in zip(*pair)] for pair in zip(before, (other, own))])
    return found


def gram_sum(half, message_ref, grads_ref, ins_ref, parts):
    rank = message_ref.shape[0] - EXTRA
    onehot = members(message_ref[rank : rank + 1, :], DOCS_DEV).astype(jnp.bfloat16)
    doubled = jnp.concatenate([onehot, onehot], axis=1)
    total = None
    for first in range(0, len(parts), 4):
        codes, ids, scales = [], [], []
        for block, place in parts[first : first + 4]:
            codes.append(block[:rank, :])
            ids.append(block[rank : rank + 1, :] + place * DOCS_DEV)
            grades = block[rank + 1 : rank + 2, :] + block[rank + 2 : rank + 3, :]
            scales.append(grades.astype(jnp.float32))
        codes, ids, scales = (jnp.concatenate(part, axis=1) for part in (codes, ids, scales))
        product = None
        for units, left in (
            (lax.shift_right_arithmetic(codes, 16), grads_ref),
            (lax.shift_right_arithmetic(lax.shift_left(codes, 16), 16), ins_ref),
        ):
            high, low = halves(units.astype(jnp.float32))
            part = dot(left[...], jnp.concatenate([high, low, high, low], axis=0), NN)
            product = part if product is None else product * part
        high, low = halves(product)
        by_doc = dot(doubled, jnp.concatenate([high, low], axis=0), NN)
        by_doc = by_doc * (jnp.exp2(scales * (1.0 / STEPS)) * (1.0 / (TOP * TOP * rank * rank)))
        high, low = halves(by_doc)
        theirs = members(ids, half * DOCS_DEV).astype(jnp.bfloat16)
        part = dot(jnp.concatenate([high, low], axis=0), theirs, NT)
        total = part if total is None else total + part
    return total[:DOCS_DEV, :] + total[DOCS_DEV:, :]


def place_of(shard, half, own_half, origin):
    far, near = origin
    return lax.rem(lax.bitwise_xor(shard, jnp.where(own_half, near, far)), half)


def blocks_at(shard, half, own_half, numbers, refs):
    parts = []
    for ref, n in zip(refs, numbers):
        far, near = (jnp.where(shard < half, *bits) for bits in origins(2 * half)[n])
        place = lax.rem(lax.bitwise_xor(shard, jnp.where(own_half, near, far)), half)
        parts.append((ref[...], place))
    return parts


def position(half):
    shard, core = lax.axis_index("dp"), lax.axis_index("tensor")
    return shard, lax.div(shard, half) == core


def early_kernel(half, numbers, message_ref, grads_ref, ins_ref, *refs):
    blocks, sum_ref = refs[:-1], refs[-1]
    shard, own_half = position(half)
    parts = blocks_at(shard, half, own_half, numbers, blocks)
    parts.append((message_ref[...], jnp.where(own_half, lax.rem(shard, half), -half)))
    sum_ref[...] = gram_sum(half, message_ref, grads_ref, ins_ref, parts)


def write_out(total_ref, scores_ref, out_ref, scores_out_ref, sems):
    copies = (
        pltpu.make_async_copy(scores_ref, scores_out_ref, sems.at[0]),
        pltpu.make_async_copy(total_ref, out_ref, sems.at[1]),
    )
    for copy in copies:
        copy.start()
    for copy in copies:
        copy.wait()


def middle_kernel(half, numbers, message_ref, grads_ref, ins_ref, scores_ref, sum_ref, *refs):
    blocks, (out_ref, scores_out_ref, total_ref, sems) = refs[:-4], refs[-4:]
    shard, own_half = position(half)
    parts = blocks_at(shard, half, own_half, numbers, blocks)
    total_ref[...] = sum_ref[...] + gram_sum(half, message_ref, grads_ref, ins_ref, parts)

    @pl.when(own_half)
    def _():
        write_out(total_ref, scores_ref, out_ref, scores_out_ref, sems)


def last_kernel(half, feats_ref, scores_ref, sum_ref, block_ref, *refs):
    out_ref, scores_out_ref, total_ref, sems = refs[-4:]
    shard, own_half = position(half)
    rank = feats_ref.shape[1] // 4

    @pl.when(jnp.logical_not(own_half))
    def _():
        ((block, place),) = blocks_at(shard, half, own_half, [half - 1], [block_ref])
        codes = block[:rank, :]
        grads = lax.shift_right_arithmetic(codes, 16).astype(jnp.float32)
        ins = lax.shift_right_arithmetic(lax.shift_left(codes, 16), 16).astype(jnp.float32)
        high, low = halves(ins)
        shares = dot(feats_ref[...], jnp.concatenate([high, low, high, low], axis=0), NN)
        terms = [shares[i * DOCS_DEV : (i + 1) * DOCS_DEV, :] * grads[i : i + 1, :] for i in range(rank)]
        grades = block[rank + 1 : rank + 2, :] + block[rank + 2 : rank + 3, :]
        scales = jnp.exp2(grades.astype(jnp.float32) * (1.0 / STEPS)) * (1.0 / (TOP * TOP * rank * rank))
        high, low = halves(sum_of(terms) * scales)
        theirs = members(block[rank : rank + 1, :] + place * DOCS_DEV, half * DOCS_DEV).astype(jnp.bfloat16)
        part = dot(jnp.concatenate([high, low], axis=0), theirs, NT)
        total_ref[...] = sum_ref[...] + (part[:DOCS_DEV, :] + part[DOCS_DEV:, :])
        write_out(total_ref, scores_ref, out_ref, scores_out_ref, sems)


def gram_of(message, grads, ins, feats, scores, blocks):
    half = len(blocks)
    rows = jax.ShapeDtypeStruct((DOCS_DEV, half * DOCS_DEV), jnp.float32)
    results = (rows, jax.ShapeDtypeStruct(scores.shape, scores.dtype))
    operands = (message, grads, ins)
    early, middle = range(half - 3), range(half - 3, half - 1)
    so_far = pl.pallas_call(
        functools.partial(early_kernel, half, early),
        out_shape=rows,
        in_specs=[VMEM] * (3 + len(early)),
        out_specs=VMEM,
        compiler_params=SMALL,
        name="gram_early",
    )(*operands, *(blocks[n] for n in early))
    *results_own, so_far = pl.pallas_call(
        functools.partial(middle_kernel, half, middle),
        out_shape=(*results, rows),
        in_specs=[VMEM] * (5 + len(middle)),
        out_specs=(HBM, HBM, VMEM),
        scratch_shapes=[pltpu.SemaphoreType.DMA((2,))],
        compiler_params=SMALL,
        name="gram_middle",
    )(*operands, scores, so_far, *(blocks[n] for n in middle))
    return pl.pallas_call(
        functools.partial(last_kernel, half),
        out_shape=results,
        in_specs=[VMEM] * 4 + [HBM] * 2,
        out_specs=(HBM, HBM),
        scratch_shapes=[pltpu.VMEM(rows.shape, rows.dtype), pltpu.SemaphoreType.DMA((2,))],
        input_output_aliases={4: 0, 5: 1},
        compiler_params=SMALL,
        name="gram_last",
    )(feats, scores, so_far, blocks[-1], *results_own)


def local(inputs, out_grads, proj_in, proj_out, doc_ids, queries):
    shards = lax.axis_size("dp")
    half = shards // 2
    mine = partial_codes(inputs, out_grads, proj_in.T, proj_out.T)
    other = lax.ppermute(mine, "tensor", [(0, 1), (1, 0)])
    own, message = pack(mine, other, doc_ids)
    blocks = []
    for what, far, near, crossed in plan(shards):
        moves = []
        for s in range(shards):
            side = s // half
            for core in range(2):
                to = s ^ (near if core == side else far)[side]
                to_core = core if to // half == side else 1 - core
                by = 1 - core if side in crossed else core
                moves.append((2 * s + by, 2 * to + to_core))
        blocks.append(lax.ppermute(blocks[what] if what >= 0 else message, ("dp", "tensor"), moves))
    scores, grads, ins, feats = score_docs(own, message, queries)
    return gram_of(message, grads, ins, feats, scores, blocks)


def solution(mesh):
    return jax.shard_map(
        local,
        mesh=mesh,
        in_specs=(
            P(("groups", "dp"), "tensor"),
            P(("groups", "dp"), "tensor"),
            P(),
            P(),
            P(("groups", "dp"), None),
            P(),
        ),
        out_specs=(P(("groups", "dp"), "tensor"), P(("groups", "dp"), None)),
        check_vma=False,
    )
```

```python
import functools

import jax
import jax.numpy as jnp
from jax import lax
from jax.experimental import pallas as pl
from jax.experimental.pallas import tpu as pltpu
from jax.sharding import PartitionSpec as P

DOCS_DEV = 8
EXTRA = 8
STEPS = 8.0
TOP = 32767.0
NT = (((1,), (1,)), ((), ()))
NN = (((1,), (0,)), ((), ()))
VMEM = pl.BlockSpec(memory_space=pltpu.VMEM)
HBM = pl.BlockSpec(memory_space=pltpu.HBM)
SMALL = pltpu.CompilerParams(vmem_limit_bytes=16 << 20)

dot = functools.partial(lax.dot_general, preferred_element_type=jnp.float32)


def pieces_of(depth):
    count = -(-depth // 2432)
    pieces, at = [], 0
    for n in range(count):
        share = 1.0 + 0.19 * ((count - 1) / 2 - n)
        size = max(round(depth * share / (count * 128)), 1) * 128
        size = depth - at if n == count - 1 else min(size, depth - at)
        if size > 0:
            pieces.append((at, size))
        at += size
    return pieces


def sum_of(parts):
    while len(parts) > 1:
        parts = [sum(parts[n : n + 2]) for n in range(0, len(parts), 2)]
    return parts[0]


def halves(values):
    high = values.astype(jnp.bfloat16)
    return high, (values - high.astype(jnp.float32)).astype(jnp.bfloat16)


def members(ids, docs):
    rows = lax.broadcasted_iota(jnp.int32, (docs, ids.shape[1]), 0)
    return (rows == ids).astype(jnp.float32)


def codes_kernel(x_hbm, y_hbm, wx_hbm, wy_hbm, out_ref, x, y, wx, wy, sems):
    at_core = lax.axis_index("tensor")
    rank = wx.shape[0]
    jobs = []
    for src, w_src, dst, w_dst, row in ((y_hbm, wy_hbm, y, wy, 0), (x_hbm, wx_hbm, x, wx, rank)):
        depth = dst.shape[1]
        for at, size in pieces_of(depth):
            there = pl.multiple_of(at_core * depth + at, 128)
            here = pl.ds(at, size)
            sem = 2 * len(jobs)
            copies = (
                pltpu.make_async_copy(w_src.at[:, pl.ds(there, size)], w_dst.at[:, here], sems.at[sem]),
                pltpu.make_async_copy(src.at[:, here], dst.at[:, here], sems.at[sem + 1]),
            )
            for copy in copies:
                copy.start()
            jobs.append((copies, dst, w_dst, row, at, size))
    totals = {}
    for copies, dst, w_dst, row, at, size in jobs:
        for copy in copies:
            copy.wait()
        here = slice(at, at + size)
        totals.setdefault(row, []).append(dot(w_dst[:, here], dst[:, here], NT))
    for row, parts in totals.items():
        out_ref[row : row + rank, :] = sum_of(parts)


def partial_codes(inputs, out_grads, proj_in_t, proj_out_t):
    tokens, depth_in = inputs.shape
    depth_out = out_grads.shape[1]
    rank = proj_in_t.shape[0]
    copies = 2 * (len(pieces_of(depth_in)) + len(pieces_of(depth_out)))
    return pl.pallas_call(
        codes_kernel,
        out_shape=jax.ShapeDtypeStruct((2 * rank, tokens), jnp.float32),
        in_specs=[HBM] * 4,
        out_specs=VMEM,
        scratch_shapes=[
            pltpu.VMEM((tokens, depth_in), inputs.dtype),
            pltpu.VMEM((tokens, depth_out), out_grads.dtype),
            pltpu.VMEM((rank, depth_in), proj_in_t.dtype),
            pltpu.VMEM((rank, depth_out), proj_out_t.dtype),
            pltpu.SemaphoreType.DMA((copies,)),
        ],
        compiler_params=pltpu.CompilerParams(vmem_limit_bytes=56_000_000),
        name="partial_codes",
    )(inputs, out_grads, proj_in_t, proj_out_t)


def fixed_point(values):
    largest = jnp.max(jnp.abs(values), axis=0, keepdims=True)
    grade = jnp.ceil(jnp.log(jnp.maximum(largest, 1e-30)) * (STEPS / 0.6931471805599453) + 0.01)
    units = values * (TOP * jnp.exp2(grade * (-1.0 / STEPS)))
    units = jnp.clip(jnp.floor(units + 0.5), -TOP, TOP)
    return units.astype(jnp.int32), grade.astype(jnp.int32)


def pack_kernel(mine_ref, other_ref, ids_ref, own_ref, message_ref):
    rows, tokens = mine_ref.shape
    rank = rows // 2
    ids = ids_ref[...]
    onehot = members(ids, DOCS_DEV)
    count = jnp.maximum(jnp.sum(onehot, axis=1, keepdims=True), 1.0)
    weight = jnp.sum(onehot / jnp.sqrt(count), axis=0, keepdims=True)
    grads = mine_ref[:rank, :] + other_ref[:rank, :]
    ins = (mine_ref[rank:, :] + other_ref[rank:, :]) * weight
    own_ref[:rank, :] = grads
    own_ref[rank:, :] = ins
    grad_units, grad_grade = fixed_point(grads)
    in_units, in_grade = fixed_point(ins)
    message_ref[:rank, :] = lax.shift_left(grad_units, 16) | (in_units & 0xFFFF)
    line = lax.broadcasted_iota(jnp.int32, (EXTRA, tokens), 0)
    message_ref[rank:, :] = jnp.where(
        line == 0, ids, jnp.where(line == 1, grad_grade, in_grade)
    )


def pack(mine, other, doc_ids):
    rows, tokens = mine.shape
    rank = rows // 2
    return pl.pallas_call(
        pack_kernel,
        out_shape=(
            jax.ShapeDtypeStruct((rows, tokens), jnp.float32),
            jax.ShapeDtypeStruct((rank + EXTRA, tokens), jnp.int32),
        ),
        in_specs=[VMEM] * 3,
        out_specs=(VMEM, VMEM),
        compiler_params=SMALL,
        name="pack_codes",
    )(mine, other, doc_ids)


def scores_kernel(own_ref, message_ref, queries, scores_ref, grads_ref, ins_ref, feats_ref):
    rows, tokens = own_ref.shape
    rank = rows // 2
    grads = own_ref[:rank, :]
    ins = own_ref[rank:, :]
    onehot = members(message_ref[rank : rank + 1, :], DOCS_DEV)
    for values, ref in ((grads, grads_ref), (ins, ins_ref)):
        high, low = halves(values)
        stacked = jnp.concatenate([high, high, low, low], axis=0)
        ref[...] = stacked.T
    weighted = (grads[:, None, :] * onehot[None, :, :]).reshape(rank * DOCS_DEV, tokens)
    w_high, w_low = halves(weighted)
    i_high, i_low = halves(jnp.concatenate([ins, ins], axis=0))
    feats = dot(
        jnp.concatenate([w_high, w_high, w_low], axis=1),
        jnp.concatenate([i_high, i_low, i_high], axis=1),
        NT,
    )
    feats_ref[...] = jnp.concatenate(halves(feats), axis=1)
    left = lax.broadcasted_iota(jnp.int32, (DOCS_DEV, 2 * rank), 1) < rank
    pairs = [
        jnp.where(
            left,
            feats[i * DOCS_DEV : (i + 1) * DOCS_DEV],
            feats[(i + 1) * DOCS_DEV : (i + 2) * DOCS_DEV],
        )
        for i in range(0, rank, 2)
    ]
    count = queries.shape[0]
    sums = [None] * count
    for n, pair in enumerate(pairs):
        block = queries[:, n * 2 * rank : (n + 1) * 2 * rank]
        for q in range(count):
            term = pair * block[q : q + 1, :]
            sums[q] = term if n == 0 else sums[q] + term
    columns = [jnp.sum(total, axis=1, keepdims=True) for total in sums]
    scores_ref[...] = jnp.concatenate(columns, axis=1) * (1.0 / rank)


def score_docs(own, message, queries):
    rows, tokens = own.shape
    rank = rows // 2
    operand = jax.ShapeDtypeStruct((tokens, 4 * rank), jnp.bfloat16)
    return pl.pallas_call(
        scores_kernel,
        out_shape=(
            jax.ShapeDtypeStruct((DOCS_DEV, queries.shape[0]), jnp.float32),
            operand,
            operand,
            jax.ShapeDtypeStruct((rank * DOCS_DEV, 4 * rank), jnp.bfloat16),
        ),
        in_specs=[VMEM] * 3,
        out_specs=(VMEM,) * 4,
        compiler_params=SMALL,
        cost_estimate=pl.CostEstimate(flops=1 << 26, bytes_accessed=1 << 19, transcendentals=0),
        name="score_docs",
    )(own, message, queries)


def plan(shards):
    half = shards // 2
    if half == 4:
        return [
            (-1, (4, 4), (1, 1), (1,)),
            (-1, (7, 7), (2, 2), (1,)),
            (0, (2, 1), (2, 2), ()),
            (0, (1, 2), (2, 1), ()),
        ]
    direct = [(-1, (half + n,) * 2, (n + 1,) * 2, ()) for n in range(0, half, 2)]
    return direct + [(n, (1, 1), (1, 1), ()) for n in reversed(range(half // 2))]


def origins(shards):
    found = []
    for what, other, own, _ in plan(shards):
        before = found[what] if what >= 0 else ((0, 0), (0, 0))
        found.append([[a ^ b for a, b in zip(*pair)] for pair in zip(before, (other, own))])
    return found


def gram_sum(half, message_ref, grads_ref, ins_ref, parts):
    rank = message_ref.shape[0] - EXTRA
    onehot = members(message_ref[rank : rank + 1, :], DOCS_DEV).astype(jnp.bfloat16)
    doubled = jnp.concatenate([onehot, onehot], axis=1)
    total = None
    for first in range(0, len(parts), 4):
        codes, ids, scales = [], [], []
        for block, place in parts[first : first + 4]:
            codes.append(block[:rank, :])
            ids.append(block[rank : rank + 1, :] + place * DOCS_DEV)
            grades = block[rank + 1 : rank + 2, :] + block[rank + 2 : rank + 3, :]
            scales.append(grades.astype(jnp.float32))
        codes, ids, scales = (jnp.concatenate(part, axis=1) for part in (codes, ids, scales))
        product = None
        for units, left in (
            (lax.shift_right_arithmetic(codes, 16), grads_ref),
            (lax.shift_right_arithmetic(lax.shift_left(codes, 16), 16), ins_ref),
        ):
            high, low = halves(units.astype(jnp.float32))
            part = dot(left[...], jnp.concatenate([high, low, high, low], axis=0), NN)
            product = part if product is None else product * part
        high, low = halves(product)
        by_doc = dot(doubled, jnp.concatenate([high, low], axis=0), NN)
        by_doc = by_doc * (jnp.exp2(scales * (1.0 / STEPS)) * (1.0 / (TOP * TOP * rank * rank)))
        high, low = halves(by_doc)
        theirs = members(ids, half * DOCS_DEV).astype(jnp.bfloat16)
        part = dot(jnp.concatenate([high, low], axis=0), theirs, NT)
        total = part if total is None else total + part
    return total[:DOCS_DEV, :] + total[DOCS_DEV:, :]


def place_of(shard, half, own_half, origin):
    far, near = origin
    return lax.rem(lax.bitwise_xor(shard, jnp.where(own_half, near, far)), half)


def blocks_at(shard, half, own_half, numbers, refs):
    parts = []
    for ref, n in zip(refs, numbers):
        far, near = (jnp.where(shard < half, *bits) for bits in origins(2 * half)[n])
        place = lax.rem(lax.bitwise_xor(shard, jnp.where(own_half, near, far)), half)
        parts.append((ref[...], place))
    return parts


def position(half):
    shard, core = lax.axis_index("dp"), lax.axis_index("tensor")
    return shard, lax.div(shard, half) == core


def early_kernel(half, numbers, message_ref, grads_ref, ins_ref, *refs):
    blocks, sum_ref = refs[:-1], refs[-1]
    shard, own_half = position(half)
    parts = blocks_at(shard, half, own_half, numbers, blocks)
    parts.append((message_ref[...], jnp.where(own_half, lax.rem(shard, half), -half)))
    sum_ref[...] = gram_sum(half, message_ref, grads_ref, ins_ref, parts)


def write_out(total_ref, scores_ref, out_ref, scores_out_ref, sems):
    copies = (
        pltpu.make_async_copy(scores_ref, scores_out_ref, sems.at[0]),
        pltpu.make_async_copy(total_ref, out_ref, sems.at[1]),
    )
    for copy in copies:
        copy.start()
    for copy in copies:
        copy.wait()


def middle_kernel(half, numbers, message_ref, grads_ref, ins_ref, scores_ref, sum_ref, *refs):
    blocks, (out_ref, scores_out_ref, total_ref, sems) = refs[:-4], refs[-4:]
    shard, own_half = position(half)
    parts = blocks_at(shard, half, own_half, numbers, blocks)
    total_ref[...] = sum_ref[...] + gram_sum(half, message_ref, grads_ref, ins_ref, parts)

    @pl.when(own_half)
    def _():
        write_out(total_ref, scores_ref, out_ref, scores_out_ref, sems)


def last_kernel(half, feats_ref, scores_ref, sum_ref, block_ref, *refs):
    out_ref, scores_out_ref, total_ref, sems = refs[-4:]
    shard, own_half = position(half)
    rank = feats_ref.shape[1] // 4

    @pl.when(jnp.logical_not(own_half))
    def _():
        ((block, place),) = blocks_at(shard, half, own_half, [half - 1], [block_ref])
        codes = block[:rank, :]
        grads = lax.shift_right_arithmetic(codes, 16).astype(jnp.float32)
        ins = lax.shift_right_arithmetic(lax.shift_left(codes, 16), 16).astype(jnp.float32)
        high, low = halves(ins)
        shares = dot(feats_ref[...], jnp.concatenate([high, low, high, low], axis=0), NN)
        terms = [shares[i * DOCS_DEV : (i + 1) * DOCS_DEV, :] * grads[i : i + 1, :] for i in range(rank)]
        grades = block[rank + 1 : rank + 2, :] + block[rank + 2 : rank + 3, :]
        scales = jnp.exp2(grades.astype(jnp.float32) * (1.0 / STEPS)) * (1.0 / (TOP * TOP * rank * rank))
        high, low = halves(sum_of(terms) * scales)
        theirs = members(block[rank : rank + 1, :] + place * DOCS_DEV, half * DOCS_DEV).astype(jnp.bfloat16)
        part = dot(jnp.concatenate([high, low], axis=0), theirs, NT)
        total_ref[...] = sum_ref[...] + (part[:DOCS_DEV, :] + part[DOCS_DEV:, :])
        write_out(total_ref, scores_ref, out_ref, scores_out_ref, sems)


def gram_of(message, grads, ins, feats, scores, blocks):
    half = len(blocks)
    rows = jax.ShapeDtypeStruct((DOCS_DEV, half * DOCS_DEV), jnp.float32)
    results = (rows, jax.ShapeDtypeStruct(scores.shape, scores.dtype))
    operands = (message, grads, ins)
    early, middle = range(half - 3), range(half - 3, half - 1)
    so_far = pl.pallas_call(
        functools.partial(early_kernel, half, early),
        out_shape=rows,
        in_specs=[VMEM] * (3 + len(early)),
        out_specs=VMEM,
        compiler_params=SMALL,
        name="gram_early",
    )(*operands, *(blocks[n] for n in early))
    *results_own, so_far = pl.pallas_call(
        functools.partial(middle_kernel, half, middle),
        out_shape=(*results, rows),
        in_specs=[VMEM] * (5 + len(middle)),
        out_specs=(HBM, HBM, VMEM),
        scratch_shapes=[pltpu.SemaphoreType.DMA((2,))],
        compiler_params=SMALL,
        name="gram_middle",
    )(*operands, scores, so_far, *(blocks[n] for n in middle))
    return pl.pallas_call(
        functools.partial(last_kernel, half),
        out_shape=results,
        in_specs=[VMEM] * 4 + [HBM] * 2,
        out_specs=(HBM, HBM),
        scratch_shapes=[pltpu.VMEM(rows.shape, rows.dtype), pltpu.SemaphoreType.DMA((2,))],
        input_output_aliases={4: 0, 5: 1},
        compiler_params=SMALL,
        name="gram_last",
    )(feats, scores, so_far, blocks[-1], *results_own)


def local(inputs, out_grads, proj_in, proj_out, doc_ids, queries):
    shards = lax.axis_size("dp")
    half = shards // 2
    mine = partial_codes(inputs, out_grads, proj_in.T, proj_out.T)
    other = lax.ppermute(mine, "tensor", [(0, 1), (1, 0)])
    own, message = pack(mine, other, doc_ids)
    blocks = []
    for what, far, near, crossed in plan(shards):
        moves = []
        for s in range(shards):
            side = s // half
            for core in range(2):
                to = s ^ (near if core == side else far)[side]
                to_core = core if to // half == side else 1 - core
                by = 1 - core if side in crossed else core
                moves.append((2 * s + by, 2 * to + to_core))
        blocks.append(lax.ppermute(blocks[what] if what >= 0 else message, ("dp", "tensor"), moves))
    scores, grads, ins, feats = score_docs(own, message, queries)
    return gram_of(message, grads, ins, feats, scores, blocks)


def solution(mesh):
    return jax.shard_map(
        local,
        mesh=mesh,
        in_specs=(
            P(("groups", "dp"), "tensor"),
            P(("groups", "dp"), "tensor"),
            P(),
            P(),
            P(("groups", "dp"), None),
            P(),
        ),
        out_specs=(P(("groups", "dp"), "tensor"), P(("groups", "dp"), None)),
        check_vma=False,
    )
```

```python
import functools

import jax
import jax.numpy as jnp
from jax import lax
from jax.experimental import pallas as pl
from jax.experimental.pallas import tpu as pltpu
from jax.sharding import PartitionSpec as P

DOCS_DEV = 8
EXTRA = 8
STEPS = 8.0
TOP = 32767.0
NT = (((1,), (1,)), ((), ()))
NN = (((1,), (0,)), ((), ()))
VMEM = pl.BlockSpec(memory_space=pltpu.VMEM)
HBM = pl.BlockSpec(memory_space=pltpu.HBM)
SMALL = pltpu.CompilerParams(vmem_limit_bytes=16 << 20)

dot = functools.partial(lax.dot_general, preferred_element_type=jnp.float32)


def pieces_of(depth):
    count = -(-depth // 2432)
    size = -(-depth // (count * 128)) * 128
    return [(at, min(size, depth - at)) for at in range(0, depth, size)]


def sum_of(parts):
    while len(parts) > 1:
        parts = [sum(parts[n : n + 2]) for n in range(0, len(parts), 2)]
    return parts[0]


def halves(values):
    high = values.astype(jnp.bfloat16)
    return high, (values - high.astype(jnp.float32)).astype(jnp.bfloat16)


def members(ids, docs):
    rows = lax.broadcasted_iota(jnp.int32, (docs, ids.shape[1]), 0)
    return (rows == ids).astype(jnp.float32)


def codes_kernel(x_hbm, y_hbm, wx_hbm, wy_hbm, out_ref, x, y, wx, wy, sems):
    at_core = lax.axis_index("tensor")
    rank = wx.shape[0]
    jobs = []
    for src, w_src, dst, w_dst, row in ((y_hbm, wy_hbm, y, wy, 0), (x_hbm, wx_hbm, x, wx, rank)):
        depth = dst.shape[1]
        for at, size in pieces_of(depth):
            there = pl.multiple_of(at_core * depth + at, 128)
            here = pl.ds(at, size)
            sem = 2 * len(jobs)
            copies = (
                pltpu.make_async_copy(w_src.at[:, pl.ds(there, size)], w_dst.at[:, here], sems.at[sem]),
                pltpu.make_async_copy(src.at[:, here], dst.at[:, here], sems.at[sem + 1]),
            )
            for copy in copies:
                copy.start()
            jobs.append((copies, dst, w_dst, row, at, size))
    totals = {}
    for copies, dst, w_dst, row, at, size in jobs:
        for copy in copies:
            copy.wait()
        here = slice(at, at + size)
        totals.setdefault(row, []).append(dot(w_dst[:, here], dst[:, here], NT))
    for row, parts in totals.items():
        out_ref[row : row + rank, :] = sum_of(parts)


def partial_codes(inputs, out_grads, proj_in_t, proj_out_t):
    tokens, depth_in = inputs.shape
    depth_out = out_grads.shape[1]
    rank = proj_in_t.shape[0]
    copies = 2 * (len(pieces_of(depth_in)) + len(pieces_of(depth_out)))
    return pl.pallas_call(
        codes_kernel,
        out_shape=jax.ShapeDtypeStruct((2 * rank, tokens), jnp.float32),
        in_specs=[HBM] * 4,
        out_specs=VMEM,
        scratch_shapes=[
            pltpu.VMEM((tokens, depth_in), inputs.dtype),
            pltpu.VMEM((tokens, depth_out), out_grads.dtype),
            pltpu.VMEM((rank, depth_in), proj_in_t.dtype),
            pltpu.VMEM((rank, depth_out), proj_out_t.dtype),
            pltpu.SemaphoreType.DMA((copies,)),
        ],
        compiler_params=pltpu.CompilerParams(vmem_limit_bytes=56_000_000),
        name="partial_codes",
    )(inputs, out_grads, proj_in_t, proj_out_t)


def fixed_point(values):
    largest = jnp.max(jnp.abs(values), axis=0, keepdims=True)
    grade = jnp.ceil(jnp.log(jnp.maximum(largest, 1e-30)) * (STEPS / 0.6931471805599453) + 0.01)
    units = values * (TOP * jnp.exp2(grade * (-1.0 / STEPS)))
    units = jnp.clip(jnp.floor(units + 0.5), -TOP, TOP)
    return units.astype(jnp.int32), grade.astype(jnp.int32)


def pack_kernel(mine_ref, other_ref, ids_ref, own_ref, message_ref):
    rows, tokens = mine_ref.shape
    rank = rows // 2
    ids = ids_ref[...]
    onehot = members(ids, DOCS_DEV)
    count = jnp.maximum(jnp.sum(onehot, axis=1, keepdims=True), 1.0)
    weight = jnp.sum(onehot / jnp.sqrt(count), axis=0, keepdims=True)
    grads = mine_ref[:rank, :] + other_ref[:rank, :]
    ins = (mine_ref[rank:, :] + other_ref[rank:, :]) * weight
    own_ref[:rank, :] = grads
    own_ref[rank:, :] = ins
    grad_units, grad_grade = fixed_point(grads)
    in_units, in_grade = fixed_point(ins)
    message_ref[:rank, :] = lax.shift_left(grad_units, 16) | (in_units & 0xFFFF)
    line = lax.broadcasted_iota(jnp.int32, (EXTRA, tokens), 0)
    message_ref[rank:, :] = jnp.where(
        line == 0, ids, jnp.where(line == 1, grad_grade, in_grade)
    )


def pack(mine, other, doc_ids):
    rows, tokens = mine.shape
    rank = rows // 2
    return pl.pallas_call(
        pack_kernel,
        out_shape=(
            jax.ShapeDtypeStruct((rows, tokens), jnp.float32),
            jax.ShapeDtypeStruct((rank + EXTRA, tokens), jnp.int32),
        ),
        in_specs=[VMEM] * 3,
        out_specs=(VMEM, VMEM),
        compiler_params=SMALL,
        name="pack_codes",
    )(mine, other, doc_ids)


def scores_kernel(own_ref, message_ref, queries, scores_ref, grads_ref, ins_ref, feats_ref):
    rows, tokens = own_ref.shape
    rank = rows // 2
    grads = own_ref[:rank, :]
    ins = own_ref[rank:, :]
    onehot = members(message_ref[rank : rank + 1, :], DOCS_DEV)
    for values, ref in ((grads, grads_ref), (ins, ins_ref)):
        high, low = halves(values)
        stacked = jnp.concatenate([high, high, low, low], axis=0)
        ref[...] = stacked.T
    weighted = (grads[:, None, :] * onehot[None, :, :]).reshape(rank * DOCS_DEV, tokens)
    w_high, w_low = halves(weighted)
    i_high, i_low = halves(jnp.concatenate([ins, ins], axis=0))
    feats = dot(
        jnp.concatenate([w_high, w_high, w_low], axis=1),
        jnp.concatenate([i_high, i_low, i_high], axis=1),
        NT,
    )
    feats_ref[...] = jnp.concatenate(halves(feats), axis=1)
    left = lax.broadcasted_iota(jnp.int32, (DOCS_DEV, 2 * rank), 1) < rank
    pairs = [
        jnp.where(
            left,
            feats[i * DOCS_DEV : (i + 1) * DOCS_DEV],
            feats[(i + 1) * DOCS_DEV : (i + 2) * DOCS_DEV],
        )
        for i in range(0, rank, 2)
    ]
    count = queries.shape[0]
    sums = [None] * count
    for n, pair in enumerate(pairs):
        block = queries[:, n * 2 * rank : (n + 1) * 2 * rank]
        for q in range(count):
            term = pair * block[q : q + 1, :]
            sums[q] = term if n == 0 else sums[q] + term
    columns = [jnp.sum(total, axis=1, keepdims=True) for total in sums]
    scores_ref[...] = jnp.concatenate(columns, axis=1) * (1.0 / rank)


def score_docs(own, message, queries):
    rows, tokens = own.shape
    rank = rows // 2
    operand = jax.ShapeDtypeStruct((tokens, 4 * rank), jnp.bfloat16)
    return pl.pallas_call(
        scores_kernel,
        out_shape=(
            jax.ShapeDtypeStruct((DOCS_DEV, queries.shape[0]), jnp.float32),
            operand,
            operand,
            jax.ShapeDtypeStruct((rank * DOCS_DEV, 4 * rank), jnp.bfloat16),
        ),
        in_specs=[VMEM] * 3,
        out_specs=(VMEM,) * 4,
        compiler_params=SMALL,
        cost_estimate=pl.CostEstimate(flops=1 << 26, bytes_accessed=1 << 19, transcendentals=0),
        name="score_docs",
    )(own, message, queries)


def plan(shards):
    half = shards // 2
    if half == 4:
        return [
            (-1, (4, 4), (1, 1), (1,)),
            (-1, (7, 7), (2, 2), ()),
            (0, (2, 1), (2, 2), ()),
            (0, (1, 2), (2, 1), ()),
        ]
    direct = [(-1, (half + n,) * 2, (n + 1,) * 2, ()) for n in range(0, half, 2)]
    return direct + [(n, (1, 1), (1, 1), ()) for n in reversed(range(half // 2))]


def origins(shards):
    found = []
    for what, other, own, _ in plan(shards):
        before = found[what] if what >= 0 else ((0, 0), (0, 0))
        found.append([[a ^ b for a, b in zip(*pair)] for pair in zip(before, (other, own))])
    return found


def gram_sum(half, message_ref, grads_ref, ins_ref, parts):
    rank = message_ref.shape[0] - EXTRA
    onehot = members(message_ref[rank : rank + 1, :], DOCS_DEV).astype(jnp.bfloat16)
    doubled = jnp.concatenate([onehot, onehot], axis=1)
    total = None
    for first in range(0, len(parts), 4):
        codes, ids, scales = [], [], []
        for block, place in parts[first : first + 4]:
            codes.append(block[:rank, :])
            ids.append(block[rank : rank + 1, :] + place * DOCS_DEV)
            grades = block[rank + 1 : rank + 2, :] + block[rank + 2 : rank + 3, :]
            scales.append(grades.astype(jnp.float32))
        codes, ids, scales = (jnp.concatenate(part, axis=1) for part in (codes, ids, scales))
        product = None
        for units, left in (
            (lax.shift_right_arithmetic(codes, 16), grads_ref),
            (lax.shift_right_arithmetic(lax.shift_left(codes, 16), 16), ins_ref),
        ):
            high, low = halves(units.astype(jnp.float32))
            part = dot(left[...], jnp.concatenate([high, low, high, low], axis=0), NN)
            product = part if product is None else product * part
        high, low = halves(product)
        by_doc = dot(doubled, jnp.concatenate([high, low], axis=0), NN)
        by_doc = by_doc * (jnp.exp2(scales * (1.0 / STEPS)) * (1.0 / (TOP * TOP * rank * rank)))
        high, low = halves(by_doc)
        theirs = members(ids, half * DOCS_DEV).astype(jnp.bfloat16)
        part = dot(jnp.concatenate([high, low], axis=0), theirs, NT)
        total = part if total is None else total + part
    return total[:DOCS_DEV, :] + total[DOCS_DEV:, :]


def place_of(shard, half, own_half, origin):
    far, near = origin
    return lax.rem(lax.bitwise_xor(shard, jnp.where(own_half, near, far)), half)


def blocks_at(shard, half, own_half, numbers, refs):
    parts = []
    for ref, n in zip(refs, numbers):
        far, near = (jnp.where(shard < half, *bits) for bits in origins(2 * half)[n])
        place = lax.rem(lax.bitwise_xor(shard, jnp.where(own_half, near, far)), half)
        parts.append((ref[...], place))
    return parts


def position(half):
    shard, core = lax.axis_index("dp"), lax.axis_index("tensor")
    return shard, lax.div(shard, half) == core


def early_kernel(half, numbers, message_ref, grads_ref, ins_ref, *refs):
    blocks, sum_ref = refs[:-1], refs[-1]
    shard, own_half = position(half)
    parts = blocks_at(shard, half, own_half, numbers, blocks)
    parts.append((message_ref[...], jnp.where(own_half, lax.rem(shard, half), -half)))
    sum_ref[...] = gram_sum(half, message_ref, grads_ref, ins_ref, parts)


def write_out(total_ref, scores_ref, out_ref, scores_out_ref, sems):
    copies = (
        pltpu.make_async_copy(scores_ref, scores_out_ref, sems.at[0]),
        pltpu.make_async_copy(total_ref, out_ref, sems.at[1]),
    )
    for copy in copies:
        copy.start()
    for copy in copies:
        copy.wait()


def middle_kernel(half, numbers, message_ref, grads_ref, ins_ref, scores_ref, sum_ref, *refs):
    blocks, (out_ref, scores_out_ref, total_ref, sems) = refs[:-4], refs[-4:]
    shard, own_half = position(half)
    parts = blocks_at(shard, half, own_half, numbers, blocks)
    total_ref[...] = sum_ref[...] + gram_sum(half, message_ref, grads_ref, ins_ref, parts)

    @pl.when(own_half)
    def _():
        write_out(total_ref, scores_ref, out_ref, scores_out_ref, sems)


def last_kernel(half, feats_ref, scores_ref, sum_ref, block_ref, *refs):
    out_ref, scores_out_ref, total_ref, sems = refs[-4:]
    shard, own_half = position(half)
    rank = feats_ref.shape[1] // 4

    @pl.when(jnp.logical_not(own_half))
    def _():
        ((block, place),) = blocks_at(shard, half, own_half, [half - 1], [block_ref])
        codes = block[:rank, :]
        grads = lax.shift_right_arithmetic(codes, 16).astype(jnp.float32)
        ins = lax.shift_right_arithmetic(lax.shift_left(codes, 16), 16).astype(jnp.float32)
        high, low = halves(ins)
        shares = dot(feats_ref[...], jnp.concatenate([high, low, high, low], axis=0), NN)
        terms = [shares[i * DOCS_DEV : (i + 1) * DOCS_DEV, :] * grads[i : i + 1, :] for i in range(rank)]
        grades = block[rank + 1 : rank + 2, :] + block[rank + 2 : rank + 3, :]
        scales = jnp.exp2(grades.astype(jnp.float32) * (1.0 / STEPS)) * (1.0 / (TOP * TOP * rank * rank))
        high, low = halves(sum_of(terms) * scales)
        theirs = members(block[rank : rank + 1, :] + place * DOCS_DEV, half * DOCS_DEV).astype(jnp.bfloat16)
        part = dot(jnp.concatenate([high, low], axis=0), theirs, NT)
        total_ref[...] = sum_ref[...] + (part[:DOCS_DEV, :] + part[DOCS_DEV:, :])
        write_out(total_ref, scores_ref, out_ref, scores_out_ref, sems)


def gram_of(message, grads, ins, feats, scores, blocks):
    half = len(blocks)
    rows = jax.ShapeDtypeStruct((DOCS_DEV, half * DOCS_DEV), jnp.float32)
    results = (rows, jax.ShapeDtypeStruct(scores.shape, scores.dtype))
    operands = (message, grads, ins)
    early, middle = range(half - 3), range(half - 3, half - 1)
    so_far = pl.pallas_call(
        functools.partial(early_kernel, half, early),
        out_shape=rows,
        in_specs=[VMEM] * (3 + len(early)),
        out_specs=VMEM,
        compiler_params=SMALL,
        name="gram_early",
    )(*operands, *(blocks[n] for n in early))
    *results_own, so_far = pl.pallas_call(
        functools.partial(middle_kernel, half, middle),
        out_shape=(*results, rows),
        in_specs=[VMEM] * (5 + len(middle)),
        out_specs=(HBM, HBM, VMEM),
        scratch_shapes=[pltpu.SemaphoreType.DMA((2,))],
        compiler_params=SMALL,
        name="gram_middle",
    )(*operands, scores, so_far, *(blocks[n] for n in middle))
    return pl.pallas_call(
        functools.partial(last_kernel, half),
        out_shape=results,
        in_specs=[VMEM] * 4 + [HBM] * 2,
        out_specs=(HBM, HBM),
        scratch_shapes=[pltpu.VMEM(rows.shape, rows.dtype), pltpu.SemaphoreType.DMA((2,))],
        input_output_aliases={4: 0, 5: 1},
        compiler_params=SMALL,
        name="gram_last",
    )(feats, scores, so_far, blocks[-1], *results_own)


def local(inputs, out_grads, proj_in, proj_out, doc_ids, queries):
    shards = lax.axis_size("dp")
    half = shards // 2
    mine = partial_codes(inputs, out_grads, proj_in.T, proj_out.T)
    other = lax.ppermute(mine, "tensor", [(0, 1), (1, 0)])
    own, message = pack(mine, other, doc_ids)
    blocks = []
    for what, far, near, crossed in plan(shards):
        moves = []
        for s in range(shards):
            side = s // half
            for core in range(2):
                to = s ^ (near if core == side else far)[side]
                to_core = core if to // half == side else 1 - core
                by = 1 - core if side in crossed else core
                moves.append((2 * s + by, 2 * to + to_core))
        blocks.append(lax.ppermute(blocks[what] if what >= 0 else message, ("dp", "tensor"), moves))
    scores, grads, ins, feats = score_docs(own, message, queries)
    return gram_of(message, grads, ins, feats, scores, blocks)


def solution(mesh):
    return jax.shard_map(
        local,
        mesh=mesh,
        in_specs=(
            P(("groups", "dp"), "tensor"),
            P(("groups", "dp"), "tensor"),
            P(),
            P(),
            P(("groups", "dp"), None),
            P(),
        ),
        out_specs=(P(("groups", "dp"), "tensor"), P(("groups", "dp"), None)),
        check_vma=False,
    )
```
